32 devices in a mesh: lon: 8 (over z, core), lev: 4 (over y, x).
Axes of the slice: x: 2, y: 2, z: 4, core: 2. Of those that a mesh axis runs over, the one named last changes fastest.
Arguments:
- inputs: bfloat16 [2, 8, 48, 96, 192], P(None, 'lev', None, 'lon'), may hold values from -6 to 6
- cotangent: bfloat16 [2, 8, 48, 96, 192], P(None, 'lev', None, 'lon'), may hold values from -6 to 6
- grid_sizes: int32 [2, 2], replicated, may hold values from 43 to 96, as said below
- offsets: int32 [2], replicated, may hold values from 1 to 6, as said below
- gain_one: float32 [192], replicated, may hold values from 0.25 to 1.75
- shift_one: float32 [192], replicated, may hold values from -1 to 1
- qkv_window: bfloat16 [192, 576], replicated, may hold values from -0.4375 to 0.4375
- out_window: bfloat16 [192, 192], replicated, may hold values from -1.25 to 1.25
- bias_table: float32 [8, 6, 6, 6, 23], replicated, may hold values from -3 to 3
- gain_two: float32 [192], replicated, may hold values from 0.25 to 1.75
- shift_two: float32 [192], replicated, may hold values from -1 to 1
- qkv_column: bfloat16 [192, 576], replicated, may hold values from -0.4375 to 0.4375
- out_column: bfloat16 [192, 192], replicated, may hold values from -0.75 to 0.75
- gain_three: float32 [192], replicated, may hold values from 0.25 to 1.75
- shift_three: float32 [192], replicated, may hold values from -1 to 1
- w_up: bfloat16 [192, 768], replicated, may hold values from -0.4375 to 0.4375
- w_down: bfloat16 [768, 192], replicated, may hold values from -0.21875 to 0.21875
Outputs:
- result: bfloat16 [2, 8, 48, 96, 192], P(None, 'lev', None, 'lon')
- input_grad: bfloat16 [2, 8, 48, 96, 192], P(None, 'lev', None, 'lon')
- grad_gain_one: float32 [192], replicated
- grad_shift_one: float32 [192], replicated
- grad_qkv_window: float32 [192, 576], replicated
- grad_out_window: float32 [192, 192], replicated
- grad_bias_table: float32 [8, 6, 6, 6, 23], replicated
- grad_gain_two: float32 [192], replicated
- grad_shift_two: float32 [192], replicated
- grad_qkv_column: float32 [192, 576], replicated
- grad_out_column: float32 [192, 192], replicated
- grad_gain_three: float32 [192], replicated
- grad_shift_three: float32 [192], replicated
- grad_w_up: float32 [192, 768], replicated
- grad_w_down: float32 [768, 192], replicated
The draws below stay inside these ranges and needn't reach their ends.
Inputs may be any that keep to these rules, and one draw needn't show every extreme that they name: grid_sizes[b, 0] is from 43 to 48 and grid_sizes[b, 1] from 90 to 96; one sample holds the largest value of the array and another one the smallest. `offsets`: every offset is 1 to 6; sample 0's is 6.
All inputs are finite; a program needn't handle non-finite values.
Results may differ from the reference program's by a relative error of at most 0.018.
Values may be sent and summed in bfloat16 or wider, within the bound.
No kernel may reach another device: no remote copies, remote signals or barrier semaphores. Data moves between devices by JAX's collectives and lax.ppermute only.
A program may use at most 256 MiB of HBM per device.

```python
import jax
import jax.numpy as jnp
from jax import lax

D = 192
HEADS = 6
FF = 768
LEV = 8
WLAT = 6
WLON = 12
SAMPLES = 2
LAT = 48
LON = 96
BANDS = 8


def draw_grid_sizes(key, part):
    lat_key = jax.random.fold_in(key, 11)
    lon_key = jax.random.fold_in(key, 23)
    pick_key = jax.random.fold_in(key, 41)
    step_key = jax.random.fold_in(key, 53)
    full_lat_key = jax.random.fold_in(key, 67)
    full_lon_key = jax.random.fold_in(key, 71)
    pad_lat_key = jax.random.fold_in(key, 79)
    pad_lon_key = jax.random.fold_in(key, 83)
    lat_valid = jax.random.randint(lat_key, (SAMPLES,), LAT - 5, LAT + 1)
    lon_valid = jax.random.randint(lon_key, (SAMPLES,), LON - 6, LON + 1)
    padded_index = jax.random.randint(pick_key, (), 0, SAMPLES)
    full_index = (padded_index + jax.random.randint(step_key, (), 1, SAMPLES)) % SAMPLES
    if LAT >= LON:
        full_lat = jnp.int32(LAT)
        full_lon = jax.random.randint(full_lon_key, (), LON - 6, LON + 1)
    else:
        full_lat = jax.random.randint(full_lat_key, (), LAT - 5, LAT + 1)
        full_lon = jnp.int32(LON)
    if LAT - 5 <= LON - 6:
        pad_lat = jnp.int32(LAT - 5)
        pad_lon = jax.random.randint(pad_lon_key, (), LON - 6, LON + 1)
    else:
        pad_lat = jax.random.randint(pad_lat_key, (), LAT - 5, LAT + 1)
        pad_lon = jnp.int32(LON - 6)
    sample_index = jnp.arange(SAMPLES)
    lat_valid = jnp.where(sample_index == full_index, full_lat, jnp.where(sample_index == padded_index, pad_lat, lat_valid))
    lon_valid = jnp.where(sample_index == full_index, full_lon, jnp.where(sample_index == padded_index, pad_lon, lon_valid))
    return jnp.stack([lat_valid, lon_valid], axis=1).astype(jnp.int32)


def draw_offsets(key, part):
    shift_key = jax.random.fold_in(key, 37)
    drawn = jax.random.randint(shift_key, (SAMPLES,), 1, WLON // 2 + 1)
    sample_index = jnp.arange(SAMPLES)
    return jnp.where(sample_index == 0, WLON // 2, drawn).astype(jnp.int32)


def shard_levels(own_key, dims, split, low, largest):
    level = 1.0
    for dim, blocks in split:
        draws = jax.random.uniform(jax.random.fold_in(jax.random.fold_in(own_key, 6), dim), (blocks,), jnp.float32, low / len(split), largest / len(split))
        level = level * jnp.repeat(jnp.exp(draws), dims[dim] // blocks).reshape((-1,) + (1,) * (len(dims) - 1 - dim))
    return level


def bell_draw(key, shape, scale, bound, split=(), kind=jnp.bfloat16):
    array = jax.random.normal(key, shape, jnp.float32) * scale
    if len(split) > 0:
        array = shard_levels(key, shape, split, -0.22, 0.18) * array
    return jnp.clip(array, min=-bound, max=bound).astype(kind)


def setup_inputs(seed: int = 0) -> dict:
    arg_keys = jax.random.split(jax.random.key(seed), 18)
    inputs = bell_draw(arg_keys[0], (SAMPLES, LEV, LAT, LON, D), 1.0, 6.0, ((1, 4), (3, 8)))
    cotangent = bell_draw(arg_keys[1], (SAMPLES, LEV, LAT, LON, D), 1.0, 6.0, ((1, 4), (3, 8)))
    grid_sizes = draw_grid_sizes(jax.random.fold_in(arg_keys[17], 71), 0)
    offsets = draw_offsets(jax.random.fold_in(arg_keys[17], 71), 0)
    gain_one = jnp.clip(1.0 + 0.15 * jax.random.normal(arg_keys[4], (D,), jnp.float32), 0.25, 1.75)
    shift_one = bell_draw(arg_keys[5], (D,), 0.2, 1.0, (), jnp.float32)
    qkv_window = bell_draw(arg_keys[6], (D, 3 * D), D ** -0.5, 0.4375)
    out_window = bell_draw(arg_keys[7], (D, D), (D // 8) ** -0.5, 1.25)
    bias_table = bell_draw(arg_keys[8], (BANDS, HEADS, WLAT, WLAT, 2 * WLON - 1), 0.5, 3.0, (), jnp.float32)
    gain_two = jnp.clip(1.0 + 0.15 * jax.random.normal(arg_keys[9], (D,), jnp.float32), 0.25, 1.75)
    shift_two = bell_draw(arg_keys[10], (D,), 0.2, 1.0, (), jnp.float32)
    qkv_column = bell_draw(arg_keys[11], (D, 3 * D), D ** -0.5, 0.4375)
    out_column = bell_draw(arg_keys[12], (D, D), (D // 3) ** -0.5, 0.75)
    gain_three = jnp.clip(1.0 + 0.15 * jax.random.normal(arg_keys[13], (D,), jnp.float32), 0.25, 1.75)
    shift_three = bell_draw(arg_keys[14], (D,), 0.2, 1.0, (), jnp.float32)
    w_up = bell_draw(arg_keys[15], (D, FF), D ** -0.5, 0.4375)
    w_down = bell_draw(arg_keys[16], (FF, D), FF ** -0.5, 0.21875)
    return {"inputs": inputs, "cotangent": cotangent, "grid_sizes": grid_sizes, "offsets": offsets, "gain_one": gain_one, "shift_one": shift_one, "qkv_window": qkv_window, "out_window": out_window, "bias_table": bias_table, "gain_two": gain_two, "shift_two": shift_two, "qkv_column": qkv_column, "out_column": out_column, "gain_three": gain_three, "shift_three": shift_three, "w_up": w_up, "w_down": w_down}


@jax.custom_vjp
def low(v):
    return lax.optimization_barrier(v.astype(jnp.bfloat16)).astype(jnp.float32)

@jax.custom_vjp
def low_back(v):
    return v

def low_keep(v):
    return (low(v), None)

def low_pass(kept, grad):
    return (grad,)

def back_keep(v):
    return (v, None)

def back_low(kept, grad):
    return (low(grad),)
low.defvjp(low_keep, low_pass)
low_back.defvjp(back_keep, back_low)
EPSILON = 1e-05
NEGATIVE = -1000000000.0

def layer_norm(values, gain, shift):
    center = values - lax.optimization_barrier(jnp.mean(values, axis=-1, keepdims=True))
    spread = lax.optimization_barrier(jnp.mean(center * center, axis=-1, keepdims=True))
    return center * lax.rsqrt(spread + EPSILON) * gain + shift

def gelu_exact(values):
    return jax.nn.gelu(values, approximate=False)

def product(left, right):
    return jnp.einsum('...i,ij->...j', left, right, precision=lax.Precision.HIGHEST)

def lon_table():
    relative = jnp.arange(2 * WLON - 1, dtype=jnp.int32)[:, None, None]
    query_col = jnp.arange(WLON, dtype=jnp.int32)[None, :, None]
    key_col = jnp.arange(WLON, dtype=jnp.int32)[None, None, :]
    return (query_col - key_col + WLON - 1 == relative).astype(jnp.float32)

def soft_weights(scores):
    row_peak = lax.optimization_barrier(jnp.max(scores, axis=-1, keepdims=True))
    exps = jnp.exp(scores - row_peak)
    return exps / lax.optimization_barrier(jnp.sum(exps, axis=-1, keepdims=True))

def band_forward(params, band_input, band_index, offset, lat_limit, lon_limit):
    gain_one, shift_one, qkv_window, out_window, bias_table, gain_two, shift_two, qkv_column, out_column, gain_three, shift_three, w_up, w_down = params
    levels, lat_rows, lon_cols, feature_count = band_input.shape
    head_count = bias_table.shape[1]
    head_size = feature_count // head_count
    scale = head_size ** (-0.5)
    window_count = lon_cols // WLON
    tokens_win = lat_rows * WLON
    normed_one = low(layer_norm(band_input, gain_one, shift_one))
    rolled = jnp.roll(normed_one, -offset, axis=2)
    windows = rolled.reshape(levels, lat_rows, window_count, WLON, feature_count)
    windows = windows.transpose(0, 2, 1, 3, 4).reshape(levels, window_count, tokens_win, feature_count)
    qkv_one = low_back(low(product(windows, qkv_window)))
    shaped = (levels, window_count, tokens_win, head_count, head_size)
    queries = qkv_one[..., :feature_count].reshape(shaped)
    keyset = qkv_one[..., feature_count:2 * feature_count].reshape(shaped)
    values = qkv_one[..., 2 * feature_count:].reshape(shaped)
    table = lax.dynamic_index_in_dim(bias_table, band_index, 0, keepdims=False)
    earth_bias = jnp.einsum('hijr,rab->hiajb', table, lon_table(), precision=lax.Precision.HIGHEST)
    earth_bias = earth_bias.reshape(head_count, tokens_win, tokens_win)
    scores = jnp.einsum('lwqhe,lwkhe->lwhqk', queries, keyset, precision=lax.Precision.HIGHEST) * scale + earth_bias
    scores = low_back(scores)
    row_ok = band_index * WLAT + jnp.arange(lat_rows, dtype=jnp.int32) < lat_limit
    col_ok = (jnp.arange(lon_cols, dtype=jnp.int32) + offset) % lon_cols < lon_limit
    valid = (row_ok[None, :, None] & col_ok.reshape(window_count, 1, WLON)).reshape(window_count, tokens_win)
    masked = jnp.where(valid[None, :, None, None, :], scores, NEGATIVE)
    window_probs = soft_weights(masked)
    attended = jnp.einsum('lwhqk,lwkhe->lwqhe', low(window_probs), values, precision=lax.Precision.HIGHEST)
    attended = low_back(low(attended.reshape(levels, window_count, lat_rows, WLON, feature_count)))
    attended = attended.transpose(0, 2, 1, 3, 4).reshape(levels, lat_rows, lon_cols, feature_count)
    unrolled = jnp.roll(attended, offset, axis=2)
    after_window = band_input + low_back(product(unrolled, out_window))
    normed_two = low(layer_norm(after_window, gain_two, shift_two))
    qkv_two = low_back(low(product(normed_two, qkv_column)))
    col_shape = (levels, lat_rows, lon_cols, head_count, head_size)
    col_queries = qkv_two[..., :feature_count].reshape(col_shape)
    col_keys = qkv_two[..., feature_count:2 * feature_count].reshape(col_shape)
    col_values = qkv_two[..., 2 * feature_count:].reshape(col_shape)
    col_scores = low_back(jnp.einsum('qabhe,kabhe->abhqk', col_queries, col_keys, precision=lax.Precision.HIGHEST) * scale)
    column_probs = soft_weights(col_scores)
    column_out = jnp.einsum('abhqk,kabhe->qabhe', low(column_probs), col_values, precision=lax.Precision.HIGHEST)
    column_out = low_back(low(column_out.reshape(levels, lat_rows, lon_cols, feature_count)))
    after_column = after_window + low_back(product(column_out, out_column))
    normed_three = low(layer_norm(after_column, gain_three, shift_three))
    hidden = low_back(product(normed_three, w_up))
    activated = low(gelu_exact(hidden))
    return after_column + low_back(product(activated, w_down))

def reference(inputs, cotangent, grid_sizes, offsets, gain_one, shift_one, qkv_window, out_window, bias_table, gain_two, shift_two, qkv_column, out_column, gain_three, shift_three, w_up, w_down):
    params = tuple((member.astype(jnp.float32) for member in (gain_one, shift_one, qkv_window, out_window, bias_table, gain_two, shift_two, qkv_column, out_column, gain_three, shift_three, w_up, w_down)))
    samples, levels, lat_rows, lon_cols, feature_count = inputs.shape
    band_count = lat_rows // WLAT
    shaped_in = inputs.reshape(samples, levels, band_count, WLAT, lon_cols, feature_count)
    shaped_cot = cotangent.reshape(samples, levels, band_count, WLAT, lon_cols, feature_count)

    def one_band(totals, position):
        sample = position // band_count
        band_index = position % band_count
        band_input = shaped_in[sample, :, band_index].astype(jnp.float32)
        band_cot = shaped_cot[sample, :, band_index].astype(jnp.float32)

        def forward(weights_all, band_values):
            return band_forward(weights_all, band_values, band_index, offsets[sample], grid_sizes[sample, 0], grid_sizes[sample, 1])
        band_out, pullback = jax.vjp(forward, params, band_input)
        grad_params, grad_band = pullback(band_cot)
        totals = jax.tree.map(lambda left, right: left + right, totals, grad_params)
        return (totals, (band_out.astype(jnp.bfloat16), grad_band.astype(jnp.bfloat16)))
    zero_grads = tuple((jnp.zeros_like(member) for member in params))
    totals, (outputs, grads) = lax.scan(one_band, zero_grads, jnp.arange(samples * band_count, dtype=jnp.int32))

    def regrid(stacked):
        stacked = stacked.reshape(samples, band_count, levels, WLAT, lon_cols, feature_count)
        return stacked.transpose(0, 2, 1, 3, 4, 5).reshape(samples, levels, lat_rows, lon_cols, feature_count)
    return (regrid(outputs), regrid(grads), totals[0], totals[1], totals[2], totals[3], totals[4], totals[5], totals[6], totals[7], totals[8], totals[9], totals[10], totals[11], totals[12])
```

```python
import functools

import jax
import jax.numpy as jnp
import numpy as np
from jax import lax
from jax.experimental import pallas as pl
from jax.experimental.pallas import tpu as pltpu
from jax.sharding import PartitionSpec as P

WLAT = 6
WLON = 12
TOK = WLAT * WLON
HALF = TOK // 2
HALO0 = 32
HALO = TOK - HALO0
GROUP = 8
EPSILON = 1e-05
NEGATIVE = -1000000000.0
F32 = jnp.float32
BF16 = jnp.bfloat16
LANES = 128
UNIT = 16


def up16(n):
    return (n + 15) // 16 * 16


def nn(a, b, **kw):
    return lax.dot_general(a, b, (((1,), (0,)), ((), ())), preferred_element_type=F32, **kw)


def nt(a, b):
    return lax.dot_general(a, b, (((1,), (1,)), ((), ())), preferred_element_type=F32)


def tn(a, b):
    return lax.dot_general(a, b, (((0,), (0,)), ((), ())), preferred_element_type=F32)


class Sizes:
    def __init__(self, lev, lon, shape, heads, hidden):
        self.lev, self.lon = lev, lon
        self.s, self.l, self.rows, self.cells, self.d = shape
        self.heads, self.ff = heads, hidden
        self.bands = self.rows // WLAT
        self.nb = self.bands // lev
        self.lt = self.l * lev
        self.n = self.lt * TOK
        self.ro = up16(self.nb * TOK)
        self.rh = up16(self.nb * HALO)
        self.nblk = self.l + (self.l + 1) // 2
        self.tokens = self.cells * self.rows
        self.np = 2 * lev
        self.blocks = 2 * (2 * hidden // 2 + 3 * self.d + self.d) // LANES * (self.d // 96)
        self.hb = self.blocks // self.np
        self.units = self.bands * 4 + 2
        self.upp = -(-self.units // self.np)
        self.pr = self.hb * 96 + self.upp * UNIT


def slot_rows(z):
    own = np.full((z.ro,), -(10**6), np.int32)
    halo = np.full((z.rh,), -(10**6), np.int32)
    for b in range(z.nb):
        for t in range(TOK):
            own[b * TOK + t] = (t // WLAT) * z.rows + b * WLAT + t % WLAT
            if t >= HALF:
                halo[b * HALO + t - HALO0] = own[b * TOK + t] - z.tokens
    return own, halo


def pack_kernel(z, scal, own_base, halo_base, x_ref, *rest):
    own_refs, halo_refs, onehot = rest[: z.lev], rest[z.lev : 2 * z.lev], rest[2 * z.lev]
    p = scal[0]
    off = scal[1 + pl.program_id(0)]
    span = z.ro + z.rh
    for k in range(z.lev):
        add = off * z.rows + (p ^ k) * (z.nb * WLAT)
        for base, at, size in ((own_base, 0, z.ro), (halo_base, z.ro, z.rh)):
            hit = lax.broadcasted_iota(jnp.int32, (size, z.tokens), 1) == base[...] + add
            onehot[k * span + at : k * span + at + size] = jnp.where(hit, 1.0, 0.0).astype(BF16)
    parts, high = [], []
    for l in range(z.l):
        x = x_ref[0, l].reshape(z.tokens, z.d)
        parts.append(x[:, :LANES])
        high.append(x[:, LANES:])
    if z.l % 2:
        high.append(jnp.zeros_like(high[0]))
    for l in range(0, len(high), 2):
        parts.append(jnp.concatenate([high[l], high[l + 1]], axis=1))
    moved = nn(onehot[...], jnp.concatenate(parts, axis=1)).astype(BF16)
    for k in range(z.lev):
        for j in range(z.nblk):
            piece = moved[k * span : (k + 1) * span, j * LANES : (j + 1) * LANES]
            own_refs[k][0, j] = piece[: z.ro]
            halo_refs[k][0, j] = piece[z.ro :]


def pack(z, x, scal, interpret=False):
    own, halo = slot_rows(z)
    shapes = [jax.ShapeDtypeStruct((z.s, z.nblk, z.ro, LANES), BF16)] * z.lev
    shapes += [jax.ShapeDtypeStruct((z.s, z.nblk, z.rh, LANES), BF16)] * z.lev
    spec = lambda r: pl.BlockSpec((1, z.nblk, r, LANES), lambda s, _: (s, 0, 0, 0))
    whole = lambda r: pl.BlockSpec((r, 1), lambda s, _: (0, 0))
    out = pl.pallas_call(
        functools.partial(pack_kernel, z),
        grid_spec=pltpu.PrefetchScalarGridSpec(
            num_scalar_prefetch=1,
            grid=(z.s,),
            in_specs=[
                whole(z.ro),
                whole(z.rh),
                pl.BlockSpec((1, z.l, z.cells, z.rows, z.d), lambda s, _: (s, 0, 0, 0, 0)),
            ],
            out_specs=[spec(z.ro)] * z.lev + [spec(z.rh)] * z.lev,
            scratch_shapes=[pltpu.VMEM((z.lev * (z.ro + z.rh), z.tokens), BF16)],
        ),
        out_shape=shapes,
        compiler_params=pltpu.CompilerParams(vmem_limit_bytes=60 * 2**20),
        name="pack",
    )(scal, jnp.asarray(own)[:, None], jnp.asarray(halo)[:, None], x)
    return out[: z.lev], out[z.lev :]


def unpack_kernel(z, scal, base, *rest):
    pieces, out_ref, onehot = rest[: 2 * z.lev], rest[2 * z.lev], rest[2 * z.lev + 1]
    p = scal[0]
    off = scal[1 + pl.program_id(0)]
    span = z.ro + z.rh
    for k in range(z.lev):
        add = off * z.rows + (p ^ k) * (z.nb * WLAT)
        row = lax.broadcasted_iota(jnp.int32, (z.tokens, span), 0)
        hit = row == base[...] + add
        onehot[:, k * span : (k + 1) * span] = jnp.where(hit, 1.0, 0.0).astype(BF16)
    columns = []
    for j in range(z.nblk):
        rows = []
        for k in range(z.lev):
            rows += [pieces[k][0, j], pieces[z.lev + k][0, j]]
        columns.append(jnp.concatenate(rows, axis=0))
    moved = nn(onehot[...], jnp.concatenate(columns, axis=1))
    half = z.d - LANES
    for l in range(z.l):
        low = moved[:, l * LANES : (l + 1) * LANES]
        at = (z.l + l // 2) * LANES + (l % 2) * half
        tokens = jnp.concatenate([low, moved[:, at : at + half]], axis=1)
        out_ref[0, l] = tokens.reshape(z.cells, z.rows, z.d).astype(BF16)


def unpack(z, own, halo, scal):
    own_rows, halo_rows = slot_rows(z)
    base = jnp.asarray(np.concatenate([own_rows, halo_rows]))[None]
    spec = lambda r: pl.BlockSpec((1, z.nblk, r, LANES), lambda s, _: (s, 0, 0, 0))
    span = z.ro + z.rh
    return pl.pallas_call(
        functools.partial(unpack_kernel, z),
        grid_spec=pltpu.PrefetchScalarGridSpec(
            num_scalar_prefetch=1,
            grid=(z.s,),
            in_specs=[pl.BlockSpec((1, span), lambda s, _: (0, 0))]
            + [spec(z.ro)] * z.lev
            + [spec(z.rh)] * z.lev,
            out_specs=pl.BlockSpec((1, z.l, z.cells, z.rows, z.d), lambda s, _: (s, 0, 0, 0, 0)),
            scratch_shapes=[pltpu.VMEM((z.tokens, z.lev * span), BF16)],
        ),
        out_shape=jax.ShapeDtypeStruct((z.s, z.l, z.cells, z.rows, z.d), BF16),
        compiler_params=pltpu.CompilerParams(vmem_limit_bytes=60 * 2**20),
        name="unpack",
    )(scal, base, *own, *halo)


def loop(n, body):
    lax.fori_loop(0, n, lambda i, c: (body(i), c)[1], 0)


def head_masks(z):
    lane = lax.broadcasted_iota(jnp.int32, (1, z.d), 1)
    size = z.d // z.heads
    return [(lane >= h * size) & (lane < (h + 1) * size) for h in range(z.heads)]


def spread(values, masks):
    return jnp.concatenate([jnp.where(m, values, 0.0) for m in masks], axis=0).astype(BF16)


def gather_heads(stacked, masks):
    n = stacked.shape[0] // len(masks)
    total = jnp.where(masks[0], stacked[:n], 0.0)
    for h in range(1, len(masks)):
        total = jnp.where(masks[h], stacked[h * n : (h + 1) * n], total)
    return total


def attend(q, k, v, bias, masks, scale):
    scores = nt(k.astype(BF16), spread(q, masks)) * scale + bias
    exps = jnp.exp(scores - jnp.max(scores, axis=0, keepdims=True))
    probs = (exps * (1.0 / jnp.sum(exps, axis=0, keepdims=True))).astype(BF16)
    return probs, gather_heads(tn(probs, v.astype(BF16)), masks)


def attend_back(q, k, v, probs, grad_out, masks, scale):
    q_rows, g_rows = spread(q, masks), spread(grad_out, masks)
    wide = probs.astype(F32)
    grad_probs = nt(v.astype(BF16), g_rows)
    inner = jnp.sum(grad_probs * wide, axis=0, keepdims=True)
    grad_scores = (wide * (grad_probs - inner)).astype(BF16)
    grad_v = nn(probs, g_rows)
    grad_k = nn(grad_scores, q_rows) * scale
    grad_q = gather_heads(tn(grad_scores, k.astype(BF16)), masks) * scale
    return grad_q, grad_k, grad_v, grad_scores


def normalized(values):
    center = values - jnp.mean(values, axis=-1, keepdims=True)
    rstd = lax.rsqrt(jnp.mean(center * center, axis=-1, keepdims=True) + EPSILON)
    return center * rstd, rstd


def norm_back(normed, rstd, grad, gain):
    gained = grad * gain
    return rstd * (
        gained
        - jnp.mean(gained, axis=-1, keepdims=True)
        - normed * jnp.mean(gained * normed, axis=-1, keepdims=True)
    )


def fold_rows(values):
    return jnp.sum(values.reshape(values.shape[0] // 8, 8, values.shape[1]), axis=0)


def load_wire(z, own_refs, halo_refs, own_s, halo_s):
    for k in range(z.lev):
        own_s[k] = own_refs[k][0].astype(F32)
        halo_s[k] = halo_refs[k][0].astype(F32)


def wire_level(z, own_s, halo_s, k, l, b):
    half = z.d - LANES
    at = (l % 2) * half

    def rows(ref, size):
        start = pl.multiple_of(b * size, 8)
        low = ref[k, l, pl.ds(start, size), :]
        high = ref[k, z.l + l // 2, pl.ds(start, size), :]
        return jnp.concatenate([low, high[:, at : at + half]], axis=1)

    own, halo = rows(own_s, TOK), rows(halo_s, HALO)
    return jnp.concatenate([own[:HALO0], own[HALO0:] + halo], axis=0)


def store_wire_level(z, own_s, halo_s, k, b, tokens):
    parts = [t[:, :LANES] for t in tokens]
    high = [t[:, LANES:] for t in tokens]
    if z.l % 2:
        high.append(jnp.zeros_like(high[0]))
    for l in range(0, len(high), 2):
        parts.append(jnp.concatenate([high[l], high[l + 1]], axis=1))
    for j, part in enumerate(parts):
        own_s[k, j, pl.ds(pl.multiple_of(b * TOK, 8), TOK), :] = part
        halo_s[k, j, pl.ds(pl.multiple_of(b * HALO, 8), HALO), :] = part[HALO0:]


def clear_pad(z, own_s, halo_s):
    if z.ro > z.nb * TOK:
        own_s[:, :, z.nb * TOK :, :] = jnp.zeros_like(own_s[:, :, z.nb * TOK :, :])
    if z.rh > z.nb * HALO:
        halo_s[:, :, z.nb * HALO :, :] = jnp.zeros_like(halo_s[:, :, z.nb * HALO :, :])


def flush_wire(z, own_s, halo_s, own_refs, halo_refs):
    for k in range(z.lev):
        own_refs[k][0] = own_s[k].astype(BF16)
        halo_refs[k][0] = halo_s[k].astype(BF16)


def bf16_rows(z, ref):
    return ref[...].reshape(z.n, z.d).astype(BF16)


def put_rows(z, ref, values):
    ref[...] = values.reshape(z.lt, TOK, z.d)


def forward_kernel(z, *refs):
    it = iter(refs)
    take = lambda n: [next(it) for _ in range(n)]
    own_in, halo_in = take(z.lev), take(z.lev)
    bias_ref, mask_ref, column_mask = take(3)
    gain1, shift1, gain2, shift2, gain3, shift3 = take(6)
    wq1, wk1, wv1, wo1, wq2, wk2, wv2, wo2, w_up, w_down_t = take(10)
    own_out, halo_out = take(z.lev), take(z.lev)
    aw_ref, ac_ref, att_ref, co_ref, act_ref, slope_ref, probs_ref, probs2_ref = take(8)
    own_s, halo_s, x_s, n_s, q_s, k_s, v_s, o_s, bias_s, h_s = take(10)
    scale = (z.d // z.heads) ** (-0.5)
    masks = head_masks(z)
    b = pl.program_id(1)

    @pl.when(b == 0)
    def _():
        load_wire(z, own_in, halo_in, own_s, halo_s)

    bias_s[...] = bias_ref[0] + mask_ref[0, 0]

    def first(k):
        for l in range(z.l):
            x = wire_level(z, own_s, halo_s, k, l, b)
            x_s[k * z.l + l] = x
            n_s[k * z.l + l] = normalized(x)[0] * gain1[...] + shift1[...]

    loop(z.lev, first)
    tokens = bf16_rows(z, n_s)
    for w, out in ((wq1, q_s), (wk1, k_s), (wv1, v_s)):
        put_rows(z, out, nn(tokens, w[...]))

    def window(lv):
        probs, out = attend(
            q_s[lv], k_s[lv], v_s[lv], bias_s[...], masks, scale
        )
        probs_ref[0, 0, lv] = probs
        o_s[lv] = out

    loop(z.lt, window)
    att = bf16_rows(z, o_s)
    att_ref[0, 0] = att
    put_rows(z, o_s, nn(att, wo1[...]))

    def second(lv):
        after = x_s[lv] + o_s[lv]
        aw_ref[0, 0, lv] = after
        n_s[lv] = normalized(after)[0] * gain2[...] + shift2[...]

    loop(z.lt, second)
    tokens = bf16_rows(z, n_s)
    for w, out in ((wq2, q_s), (wk2, k_s), (wv2, v_s)):
        put_rows(z, out, nn(tokens, w[...]))

    def column(g):
        at = pl.ds(pl.multiple_of(g * GROUP, GROUP), GROUP)
        flat = lambda ref: ref[:, at, :].reshape(z.lt * GROUP, z.d)
        probs, out = attend(
            flat(q_s), flat(k_s), flat(v_s), column_mask[...], masks, scale
        )
        probs2_ref[0, 0, g] = probs
        o_s[:, at, :] = out.reshape(z.lt, GROUP, z.d)

    loop(TOK // GROUP, column)
    co = bf16_rows(z, o_s)
    co_ref[0, 0] = co
    put_rows(z, o_s, nn(co, wo2[...]))

    def third(lv):
        after = aw_ref[0, 0, lv] + o_s[lv]
        ac_ref[0, 0, lv] = after
        n_s[lv] = normalized(after)[0] * gain3[...] + shift3[...]

    loop(z.lt, third)
    h_s[...] = nn(bf16_rows(z, n_s), w_up[...])

    def gelu(i):
        at = pl.ds(pl.multiple_of(i * 16, 16), 16)
        hidden = h_s[at, :]
        share = 0.5 + 0.5 * lax.erf(hidden * (0.5**0.5))
        density = jnp.exp(hidden * hidden * -0.5) * ((2.0 * np.pi) ** -0.5)
        act_ref[0, 0, at, :] = (hidden * share).astype(BF16)
        slope_ref[0, 0, at, :] = (share + hidden * density).astype(BF16)

    loop(z.n // 16, gelu)
    put_rows(z, o_s, nt(act_ref[0, 0], w_down_t[...]))

    def last(k):
        store_wire_level(
            z, own_s, halo_s, k, b,
            [ac_ref[0, 0, k * z.l + l] + o_s[k * z.l + l] for l in range(z.l)],
        )

    loop(z.lev, last)

    @pl.when(b == z.nb - 1)
    def _():
        clear_pad(z, own_s, halo_s)
        flush_wire(z, own_s, halo_s, own_out, halo_out)


def wire_specs(z):
    spec = lambda r: pl.BlockSpec((1, z.nblk, r, LANES), lambda s, b: (s, 0, 0, 0))
    return [spec(z.ro)] * z.lev + [spec(z.rh)] * z.lev


def wire_shapes(z):
    return [jax.ShapeDtypeStruct((z.s, z.nblk, r, LANES), BF16) for r in [z.ro] * z.lev + [z.rh] * z.lev]


def unit_spec(shape):
    return pl.BlockSpec((1, 1) + shape, lambda s, b: (s, b) + (0,) * len(shape))


def whole_spec(array):
    return pl.BlockSpec(array.shape, lambda s, b: (0,) * array.ndim)


def residual_shapes(z):
    return [
        ((z.lt, TOK, z.d), F32),
        ((z.lt, TOK, z.d), F32),
        ((z.n, z.d), BF16),
        ((z.n, z.d), BF16),
        ((z.n, z.ff), BF16),
        ((z.n, z.ff), BF16),
        ((z.lt, TOK, z.heads * TOK), BF16),
        ((TOK // GROUP, z.lt * GROUP, z.heads * z.lt * GROUP), BF16),
    ]


def forward(z, own, halo, bias, mask, column_mask, norms, weights):
    res = residual_shapes(z)
    rows3 = (z.lt, TOK, z.d)
    out = pl.pallas_call(
        functools.partial(forward_kernel, z),
        grid=(z.s, z.nb),
        in_specs=wire_specs(z)
        + [
            pl.BlockSpec((1, TOK, z.heads * TOK), lambda s, b: (b, 0, 0)),
            pl.BlockSpec((1, 1, TOK, 1), lambda s, b: (s, b, 0, 0)),
            whole_spec(column_mask),
        ]
        + [whole_spec(a) for a in norms]
        + [whole_spec(a) for a in weights],
        out_specs=wire_specs(z) + [unit_spec(shape) for shape, _ in res],
        out_shape=wire_shapes(z) + [jax.ShapeDtypeStruct((z.s, z.nb) + shape, t) for shape, t in res],
        scratch_shapes=[
            pltpu.VMEM((z.lev, z.nblk, z.ro, LANES), F32),
            pltpu.VMEM((z.lev, z.nblk, z.rh, LANES), F32),
        ]
        + [pltpu.VMEM(rows3, F32)] * 6
        + [pltpu.VMEM((TOK, z.heads * TOK), F32), pltpu.VMEM((z.n, z.ff), F32)],
        compiler_params=pltpu.CompilerParams(vmem_limit_bytes=60 * 2**20),
        name="forward",
    )(*own, *halo, bias, mask, column_mask, *norms, *weights)
    return out[: z.lev], out[z.lev : 2 * z.lev], out[2 * z.lev :]


def grad_list(z):
    return [
        ("up", z.ff), ("down_t", z.ff),
        ("q1", z.d), ("k1", z.d), ("v1", z.d),
        ("q2", z.d), ("k2", z.d), ("v2", z.d),
        ("o1", z.d), ("o2", z.d),
    ]


def half_blocks(z):
    full, rest = [], []
    for name, columns in grad_list(z):
        for row in range(0, z.d, 96):
            for col in range(0, columns, LANES):
                width = min(LANES, columns - col)
                (full if width == LANES else rest).append((name, row, col, width))
    out = [[piece + (0,)] for piece in full]
    for i in range(0, len(rest), 2):
        out.append([rest[i] + (0,), rest[i + 1] + (rest[i][3],)])
    return out


def bias_rows(z):
    pick = np.zeros((WLON * 8, TOK), np.float32)
    for a in range(WLON):
        for i in range(WLAT):
            pick[a * 8 + i, a * WLAT + i] = 1.0
    return pick


def backward_kernel(z, scal, *refs):
    it = iter(refs)
    take = lambda n: [next(it) for _ in range(n)]
    own_x, halo_x = take(z.lev), take(z.lev)
    own_c, halo_c = take(z.lev), take(z.lev)
    aw_ref, ac_ref, att_ref, co_ref, act_ref, slope_ref, probs_ref, probs2_ref = take(8)
    (pick_ref,) = take(1)
    gain1, shift1, gain2, shift2, gain3, shift3 = take(6)
    wq1, wk1, wv1, wo1, wq2, wk2, wv2, wo2, w_up, w_down_t = take(10)
    own_out, halo_out = take(z.lev), take(z.lev)
    (wire_ref,) = take(1)
    own_s, halo_s, owc_s, hac_s = take(4)
    x_s, g_s, n_s, q_s, k_s, v_s, dq_s, dk_s, dv_s, o_s, rstd_s = take(11)
    ga_s, gh_s, db_s, vec_s = take(4)
    grads = {name: ref for (name, _), ref in zip(grad_list(z), take(len(grad_list(z))))}
    scale = (z.d // z.heads) ** (-0.5)
    masks = head_masks(z)
    s, b = pl.program_id(0), pl.program_id(1)

    @pl.when((s == 0) & (b == 0))
    def _():
        for ref in list(grads.values()) + [db_s, vec_s]:
            ref[...] = jnp.zeros_like(ref)

    @pl.when(b == 0)
    def _():
        load_wire(z, own_x, halo_x, own_s, halo_s)
        load_wire(z, own_c, halo_c, owc_s, hac_s)

    def first(k):
        for l in range(z.l):
            g_s[k * z.l + l] = wire_level(z, owc_s, hac_s, k, l, b)
            x_s[k * z.l + l] = wire_level(z, own_s, halo_s, k, l, b)

    loop(z.lev, first)

    cot = bf16_rows(z, g_s)
    ga_s[...] = nn(cot, w_down_t[...])
    grads["down_t"][...] += tn(cot, act_ref[0, 0])

    def slope(i):
        at = pl.ds(pl.multiple_of(i * 16, 16), 16)
        gh_s[at, :] = (ga_s[at, :] * slope_ref[0, 0, at, :].astype(F32)).astype(BF16)

    loop(z.n // 16, slope)

    def renorm(source):
        def body(lv):
            normed, rstd = normalized(source(lv))
            n_s[lv] = normed
            rstd_s[lv] = rstd

        loop(z.lt, body)

    def normed_tokens(gain, shift):
        return (n_s[...] * gain[...] + shift[...]).reshape(z.n, z.d).astype(BF16)

    def norm_step(gain, at, target):
        def body(lv):
            grad, normed = o_s[lv], n_s[lv]
            vec_s[at] += fold_rows(grad * normed)
            vec_s[at + 1] += fold_rows(grad)
            target[lv] = target[lv] + norm_back(normed, rstd_s[lv], grad, gain[...])

        loop(z.lt, body)

    renorm(lambda lv: ac_ref[0, 0, lv])
    grads["up"][...] += tn(normed_tokens(gain3, shift3), gh_s[...])
    put_rows(z, o_s, nt(gh_s[...], w_up[...]))
    norm_step(gain3, 4, g_s)

    branch = bf16_rows(z, g_s)
    grads["o2"][...] += tn(co_ref[0, 0], branch)
    put_rows(z, o_s, nt(branch, wo2[...]))
    renorm(lambda lv: aw_ref[0, 0, lv])
    tokens = normed_tokens(gain2, shift2)
    for w, out in ((wq2, q_s), (wk2, k_s), (wv2, v_s)):
        put_rows(z, out, nn(tokens, w[...]))

    def column(g):
        at = pl.ds(pl.multiple_of(g * GROUP, GROUP), GROUP)
        flat = lambda ref: ref[:, at, :].reshape(z.lt * GROUP, z.d)
        dq, dk, dv, _ = attend_back(
            flat(q_s), flat(k_s), flat(v_s), probs2_ref[0, 0, g], flat(o_s), masks, scale
        )
        for ref, value in ((dq_s, dq), (dk_s, dk), (dv_s, dv)):
            ref[:, at, :] = value.reshape(z.lt, GROUP, z.d)

    loop(TOK // GROUP, column)

    def project_back(tokens, names, ws):
        total = None
        for name, w, ref in zip(names, ws, (dq_s, dk_s, dv_s)):
            grad = bf16_rows(z, ref)
            grads[name][...] += tn(tokens, grad)
            part = nt(grad, w[...])
            total = part if total is None else total + part
        put_rows(z, o_s, total)

    project_back(tokens, ("q2", "k2", "v2"), (wq2, wk2, wv2))
    norm_step(gain2, 2, g_s)

    branch = bf16_rows(z, g_s)
    grads["o1"][...] += tn(att_ref[0, 0], branch)
    put_rows(z, o_s, nt(branch, wo1[...]))
    renorm(lambda lv: x_s[lv])
    tokens = normed_tokens(gain1, shift1)
    for w, out in ((wq1, q_s), (wk1, k_s), (wv1, v_s)):
        put_rows(z, out, nn(tokens, w[...]))

    def window(lv):
        dq, dk, dv, ds = attend_back(
            q_s[lv], k_s[lv], v_s[lv], probs_ref[0, 0, lv], o_s[lv], masks, scale
        )
        dq_s[lv], dk_s[lv], dv_s[lv] = dq, dk, dv
        db_s[b] += ds.astype(F32)

    loop(z.lt, window)
    project_back(tokens, ("q1", "k1", "v1"), (wq1, wk1, wv1))
    norm_step(gain1, 0, g_s)

    def last(k):
        store_wire_level(z, owc_s, hac_s, k, b, [g_s[k * z.l + l] for l in range(z.l)])

    loop(z.lev, last)

    @pl.when(b == z.nb - 1)
    def _():
        clear_pad(z, owc_s, hac_s)
        flush_wire(z, owc_s, hac_s, own_out, halo_out)

    @pl.when((s == z.s - 1) & (b == z.nb - 1))
    def _():
        for at, pieces in enumerate(half_blocks(z)):
            values = [grads[n][r : r + 96, c : c + width] for n, r, c, width, _ in pieces]
            block = values[0] if len(values) == 1 else jnp.concatenate(values, axis=1)
            start = (at % z.hb) * 96
            wire_ref[at // z.hb, start : start + 96, :] = block.astype(BF16)
        extra = z.hb * 96
        wire_ref[:, extra:, :] = jnp.zeros_like(wire_ref[:, extra:, :])
        vectors = [jnp.sum(vec_s[i], axis=0, keepdims=True) for i in range(6)]
        vectors = jnp.concatenate(vectors + [jnp.zeros((UNIT - 6, z.d), F32)], axis=0)
        vectors = jnp.concatenate([vectors, jnp.zeros((UNIT, 2 * LANES - z.d), F32)], axis=1)

        def put_unit(u, value):
            start = extra + (u % z.upp) * UNIT
            if not isinstance(u, int):
                start = pl.multiple_of(start, UNIT)
            wire_ref[u // z.upp, pl.ds(start, UNIT), :] = value.astype(BF16)

        for j in range(2):
            put_unit(z.bands * 4 + j, vectors[:, j * LANES : (j + 1) * LANES])
        lane = lax.broadcasted_iota(jnp.int32, (1, z.heads * TOK), 1)
        odd = jnp.zeros(lane.shape, jnp.bool_)
        for h in range(1, z.heads, 2):
            odd = odd | ((lane >= h * TOK) & (lane < (h + 1) * TOK))
        width = -(-(z.heads * TOK) // LANES) * LANES
        for band in range(z.nb):
            rows = nn(pick_ref[...], db_s[band], precision=lax.Precision.HIGHEST)
            halves = []
            for parity in range(2):
                kept = jnp.where(odd if parity else ~odd, rows, 0.0)
                kept = jnp.concatenate(
                    [kept, jnp.zeros((rows.shape[0], width - z.heads * TOK), F32)], axis=1
                )
                total = None
                for a in range(WLON):
                    part = kept[a * 8 : (a + 1) * 8]
                    shift = (WLON - 1 - a) * WLAT
                    if shift:
                        part = pltpu.roll(part, shift, 1)
                    total = part if total is None else total + part
                halves.append(total)
            both = jnp.concatenate(halves, axis=0)
            for j in range(4):
                put_unit((scal[0] * z.nb + band) * 4 + j, both[:, j * LANES : (j + 1) * LANES])


def backward(z, scal, own_x, halo_x, own_c, halo_c, residuals, norms, weights):
    res = residual_shapes(z)
    rows3 = (z.lt, TOK, z.d)
    pick = jnp.asarray(bias_rows(z))
    drop = lambda spec: pl.BlockSpec(spec.block_shape, lambda s, b, _, m=spec.index_map: m(s, b))
    out = pl.pallas_call(
        functools.partial(backward_kernel, z),
        grid_spec=pltpu.PrefetchScalarGridSpec(
            num_scalar_prefetch=1,
            grid=(z.s, z.nb),
            in_specs=[
                drop(spec)
                for spec in wire_specs(z) * 2
                + [unit_spec(shape) for shape, _ in res]
                + [whole_spec(pick)]
                + [whole_spec(a) for a in norms]
                + [whole_spec(a) for a in weights]
            ],
            out_specs=[drop(spec) for spec in wire_specs(z)]
            + [pl.BlockSpec((z.np, z.pr, LANES), lambda s, b, _: (0, 0, 0))],
            scratch_shapes=[
                pltpu.VMEM((z.lev, z.nblk, z.ro, LANES), F32),
                pltpu.VMEM((z.lev, z.nblk, z.rh, LANES), F32),
            ]
            * 2
            + [pltpu.VMEM(rows3, F32)] * 10
            + [
                pltpu.VMEM((z.lt, TOK, 1), F32),
                pltpu.VMEM((z.n, z.ff), F32),
                pltpu.VMEM((z.n, z.ff), BF16),
                pltpu.VMEM((z.nb, TOK, z.heads * TOK), F32),
                pltpu.VMEM((6, 8, z.d), F32),
            ]
            + [pltpu.VMEM((z.d, columns), F32) for _, columns in grad_list(z)],
        ),
        out_shape=wire_shapes(z) + [jax.ShapeDtypeStruct((z.np, z.pr, LANES), BF16)],
        compiler_params=pltpu.CompilerParams(vmem_limit_bytes=62 * 2**20),
        name="backward",
    )(scal, *own_x, *halo_x, *own_c, *halo_c, *residuals, pick, *norms, *weights)
    return out[: z.lev], out[z.lev : 2 * z.lev], out[2 * z.lev]


def tree(parts):
    while len(parts) > 1:
        parts = [parts[i] + parts[i + 1] for i in range(0, len(parts), 2)]
    return parts[0]


def lev_swap(z, array, k):
    return lax.ppermute(array, "lev", [(i, i ^ k) for i in range(z.lev)])


def lon_swap(z, array, k):
    return lax.ppermute(array, "lon", [(i, i ^ k) for i in range(z.lon)])


def sum_wire(z, wire, p, w):
    core = w % 2
    mine = lax.dynamic_slice_in_dim(wire, core * z.lev, z.lev, axis=0)
    other = lax.dynamic_slice_in_dim(wire, (1 - core) * z.lev, z.lev, axis=0)
    half = (mine.astype(F32) + lon_swap(z, other, 1).astype(F32)).astype(BF16)
    piece = lambda k: lax.dynamic_index_in_dim(half, p ^ k, axis=0, keepdims=False)
    parts = [piece(0)] + [lev_swap(z, piece(k), k) for k in range(1, z.lev)]
    quarter = tree([v.astype(F32) for v in parts]).astype(BF16)
    parts = [quarter] + [lon_swap(z, quarter, 2 * k) for k in range(1, z.lon // 2)]
    done = tree([v.astype(F32) for v in parts]).astype(BF16)
    own = jnp.stack([done] + [lev_swap(z, done, k) for k in range(1, z.lev)])
    return own, lon_swap(z, own, 1)


def finish_kernel(z, scal, own, other, *outs):
    p, core = scal[0], scal[1]
    named = {name: ref for (name, _), ref in zip(grad_list(z), outs)}
    vec_ref, bias_ref = outs[len(named) :]

    def read(piece, start, size):
        half, j = piece // z.lev, piece % z.lev
        rows = slice(start, start + size)
        a = own[p ^ j, rows, :].astype(F32)
        c = other[p ^ j, rows, :].astype(F32)
        return jnp.where(core == half, a, c)

    for at, pieces in enumerate(half_blocks(z)):
        block = read(at // z.hb, (at % z.hb) * 96, 96)
        for n, r, c, width, lane in pieces:
            named[n][r : r + 96, c : c + width] = block[:, lane : lane + width]
    extra = z.hb * 96
    for u in range(z.units):
        value = read(u // z.upp, extra + (u % z.upp) * UNIT, UNIT)
        if u < z.bands * 4:
            bias_ref[u // 4, :, (u % 4) * LANES : (u % 4 + 1) * LANES] = value
        else:
            j = u - z.bands * 4
            vec_ref[:, j * LANES : (j + 1) * LANES] = value


def finish(z, scal, own, other):
    shapes = [jax.ShapeDtypeStruct((z.d, columns), F32) for _, columns in grad_list(z)]
    shapes += [
        jax.ShapeDtypeStruct((UNIT, 2 * LANES), F32),
        jax.ShapeDtypeStruct((z.bands, UNIT, 4 * LANES), F32),
    ]
    full = lambda a: pl.BlockSpec(a.shape, lambda _, n=len(a.shape): (0,) * n)
    full0 = lambda a: pl.BlockSpec(a.shape, lambda i, _, n=len(a.shape): (0,) * n)
    out = pl.pallas_call(
        functools.partial(finish_kernel, z),
        grid_spec=pltpu.PrefetchScalarGridSpec(
            num_scalar_prefetch=1,
            grid=(1,),
            in_specs=[full0(own), full0(other)],
            out_specs=[full0(a) for a in shapes],
        ),
        out_shape=shapes,
        compiler_params=pltpu.CompilerParams(vmem_limit_bytes=60 * 2**20),
        name="finish",
    )(scal, own, other)
    named = {name: value for (name, _), value in zip(grad_list(z), out)}
    return named, out[-2], out[-1]


def table_of(z, rows):
    rows = rows.reshape(z.bands, 2, 8, 4 * LANES)[:, :, :WLAT]
    distances = 2 * WLON - 1
    halves = []
    for parity in range(2):
        lanes = rows[:, parity, :, parity * TOK :]
        lanes = jnp.pad(lanes, ((0, 0), (0, 0), (0, TOK)))[..., : z.heads * TOK]
        lanes = lanes.reshape(z.bands, WLAT, z.heads // 2, 2 * TOK)[..., : distances * WLAT]
        halves.append(lanes.reshape(z.bands, WLAT, z.heads // 2, distances, WLAT))
    both = jnp.stack(halves, axis=3)
    return both.transpose(0, 2, 3, 5, 1, 4).reshape(z.bands, z.heads, WLAT, WLAT, distances)


def lon_table():
    relative = jnp.arange(2 * WLON - 1, dtype=jnp.int32)[:, None, None]
    query_col = jnp.arange(WLON, dtype=jnp.int32)[None, :, None]
    key_col = jnp.arange(WLON, dtype=jnp.int32)[None, None, :]
    return (query_col - key_col + WLON - 1 == relative).astype(F32)


def exchange(z, own, halo):
    own = [own[0]] + [lev_swap(z, own[k], k) for k in range(1, z.lev)]
    both = lambda a, k, d: lax.ppermute(
        a,
        ("lon", "lev"),
        [
            (w * z.lev + i, (w + d) % z.lon * z.lev + (i ^ k))
            for w in range(z.lon)
            for i in range(z.lev)
        ],
    )
    return own, both, halo


def send_west(z, own, halo):
    own, both, halo = exchange(z, own, halo)
    return own, [both(halo[k], k, -1) for k in range(z.lev)]


def send_east(z, own, halo):
    own, both, halo = exchange(z, own, halo)
    return own, [both(halo[k], k, 1) for k in range(z.lev)]


def on_device(
    inputs, cotangent, grid_sizes, offsets, gain_one, shift_one, qkv_window, out_window, bias_table,
    gain_two, shift_two, qkv_column, out_column, gain_three, shift_three, w_up, w_down,
):
    d = inputs.shape[-1]
    z = Sizes(lax.axis_size("lev"), lax.axis_size("lon"), inputs.shape, bias_table.shape[1], w_up.shape[1])
    p, w = lax.axis_index("lev"), lax.axis_index("lon")
    scal = jnp.concatenate([p[None].astype(jnp.int32), offsets.astype(jnp.int32)])
    swap = lambda a: a.transpose(0, 1, 3, 2, 4)

    own_x, halo_x = send_west(z, *pack(z, swap(inputs), scal))
    own_c, halo_c = send_west(z, *pack(z, swap(cotangent), scal))

    table = lax.dynamic_slice_in_dim(bias_table, p * z.nb, z.nb, axis=0)
    bias = jnp.einsum("khijr,rab->kbjhai", table, lon_table(), precision=lax.Precision.HIGHEST)
    bias = bias.reshape(z.nb, TOK, z.heads * TOK)
    cell = (w * z.cells + offsets[:, None] + jnp.arange(WLON)[None, :]) % (z.cells * z.lon)
    row = (p * z.nb + jnp.arange(z.nb))[:, None] * WLAT + jnp.arange(WLAT)[None, :]
    cell_ok = cell < grid_sizes[:, 1:2]
    row_ok = row[None] < grid_sizes[:, 0][:, None, None]
    valid = cell_ok[:, None, :, None] & row_ok[:, :, None, :]
    mask = jnp.where(valid, 0.0, NEGATIVE).astype(F32).reshape(z.s, z.nb, TOK, 1)
    of_key = np.arange(z.lt * GROUP) % GROUP
    of_query = np.tile(of_key, z.heads)
    column_mask = jnp.asarray(
        np.where(of_key[:, None] == of_query[None, :], 0.0, NEGATIVE).astype(np.float32)
    )

    norms = [v[None] for v in (gain_one, shift_one, gain_two, shift_two, gain_three, shift_three)]
    three = lambda a: [a[:, :d], a[:, d : 2 * d], a[:, 2 * d :]]
    weights = three(qkv_window) + [out_window] + three(qkv_column) + [out_column, w_up, w_down.T]

    own_r, halo_r, residuals = forward(z, own_x, halo_x, bias, mask, column_mask, norms, weights)
    own_r, halo_r = send_east(z, own_r, halo_r)
    own_g, halo_g, wire = backward(
        z, scal, own_x, halo_x, own_c, halo_c, residuals, norms, weights
    )
    own_g, halo_g = send_east(z, own_g, halo_g)
    result = unpack(z, own_r, halo_r, scal)
    input_grad = unpack(z, own_g, halo_g, scal)
    own, other = sum_wire(z, wire, p, w)
    named, vectors, rows = finish(z, jnp.stack([p, w % 2]).astype(jnp.int32), own, other)
    vec = [vectors[i, :d] for i in range(6)]
    qkv = lambda i: jnp.concatenate([named["q" + i], named["k" + i], named["v" + i]], axis=1)
    return (
        swap(result), swap(input_grad),
        vec[0], vec[1], qkv("1"), named["o1"], table_of(z, rows),
        vec[2], vec[3], qkv("2"), named["o2"],
        vec[4], vec[5], named["up"], named["down_t"].T,
    )


def solution(mesh):
    tokens = P(None, "lev", None, "lon", None)
    return jax.shard_map(
        on_device,
        mesh=mesh,
        in_specs=(tokens, tokens) + (P(),) * 15,
        out_specs=(tokens, tokens) + (P(),) * 13,
        check_vma=False,
    )
```

```python
import functools

import jax
import jax.numpy as jnp
import numpy as np
from jax import lax
from jax.experimental import pallas as pl
from jax.experimental.pallas import tpu as pltpu
from jax.sharding import PartitionSpec as P

WLAT = 6
WLON = 12
TOK = WLAT * WLON
HALF = TOK // 2
HALO0 = 32
HALO = TOK - HALO0
GROUP = 8
CHUNK = 2
EPSILON = 1e-05
NEGATIVE = -1000000000.0
F32 = jnp.float32
BF16 = jnp.bfloat16
LANES = 128
UNIT = 16


def up16(n):
    return (n + 15) // 16 * 16


def nn(a, b, **kw):
    return lax.dot_general(a, b, (((1,), (0,)), ((), ())), preferred_element_type=F32, **kw)


def nt(a, b):
    return lax.dot_general(a, b, (((1,), (1,)), ((), ())), preferred_element_type=F32)


def tn(a, b):
    return lax.dot_general(a, b, (((0,), (0,)), ((), ())), preferred_element_type=F32)


class Sizes:
    def __init__(self, lev, lon, shape, heads, hidden):
        self.lev, self.lon = lev, lon
        self.s, self.l, self.rows, self.cells, self.d = shape
        self.heads, self.ff = heads, hidden
        self.bands = self.rows // WLAT
        self.nb = self.bands // lev
        self.lt = self.l * lev
        self.n = self.lt * TOK
        self.ro = up16(self.nb * TOK)
        self.rh = self.nb * HALO
        self.nblk = self.l + (self.l + 1) // 2
        self.tokens = self.cells * self.rows
        self.np = 2 * lev
        self.blocks = 2 * (2 * hidden // 2 + 3 * self.d + self.d) // LANES * (self.d // 96)
        self.hb = self.blocks // self.np
        self.units = self.bands * 4 + 2
        self.upp = -(-self.units // self.np)
        self.pr = self.hb * 96 + self.upp * UNIT


def slot_rows(z):
    own = np.full((z.ro,), -(10**6), np.int32)
    halo = np.full((z.rh,), -(10**6), np.int32)
    for b in range(z.nb):
        for t in range(TOK):
            own[b * TOK + t] = (t // WLAT) * z.rows + b * WLAT + t % WLAT
            if t >= HALF:
                halo[b * HALO + t - HALO0] = own[b * TOK + t] - z.tokens
    return own, halo


def lane_parts(z, levels):
    parts = [v[:, :LANES] for v in levels]
    high = [v[:, LANES:] for v in levels]
    if z.l % 2:
        high.append(jnp.zeros_like(high[0]))
    for l in range(0, len(high), 2):
        parts.append(jnp.concatenate([high[l], high[l + 1]], axis=1))
    return parts


def pack_kernel(z, scal, base, x_ref, halo_ref, *rest):
    outs, onehot = rest[: z.lev], rest[z.lev]
    p = scal[0]
    off = scal[1 + pl.program_id(0)]
    rows = z.tokens + halo_ref.shape[2] * z.rows
    column = lax.broadcasted_iota(jnp.int32, (z.ro, rows), 1)
    for k in range(z.lev):
        hit = column == base[...] + (off * z.rows + (p ^ k) * (z.nb * WLAT))
        onehot[k * z.ro : (k + 1) * z.ro] = jnp.where(hit, 1.0, 0.0).astype(BF16)
    levels = []
    for l in range(z.l):
        cells = [r[0, l].reshape(r.shape[2] * z.rows, z.d) for r in (x_ref, halo_ref)]
        levels.append(jnp.concatenate(cells, axis=0))
    moved = nn(onehot[...], jnp.concatenate(lane_parts(z, levels), axis=1)).astype(BF16)
    for k in range(z.lev):
        for j in range(z.nblk):
            outs[k][0, j] = moved[k * z.ro : (k + 1) * z.ro, j * LANES : (j + 1) * LANES]


def pack(z, x, halo, scal):
    own, _ = slot_rows(z)
    tokens = lambda a: pl.BlockSpec((1,) + a.shape[1:], lambda s, _: (s, 0, 0, 0, 0))
    spec = pl.BlockSpec((1, z.nblk, z.ro, LANES), lambda s, _: (s, 0, 0, 0))
    return pl.pallas_call(
        functools.partial(pack_kernel, z),
        grid_spec=pltpu.PrefetchScalarGridSpec(
            num_scalar_prefetch=1,
            grid=(x.shape[0],),
            in_specs=[pl.BlockSpec((z.ro, 1), lambda s, _: (0, 0)), tokens(x), tokens(halo)],
            out_specs=[spec] * z.lev,
            scratch_shapes=[
                pltpu.VMEM((z.lev * z.ro, z.tokens + halo.shape[2] * z.rows), BF16)
            ],
        ),
        out_shape=[jax.ShapeDtypeStruct((x.shape[0], z.nblk, z.ro, LANES), BF16)] * z.lev,
        compiler_params=pltpu.CompilerParams(vmem_limit_bytes=60 * 2**20),
        cost_estimate=cost(4),
        name="pack",
    )(scal, jnp.asarray(own)[:, None], x, halo)


def unpack_kernel(z, scal, own_base, halo_base, *rest):
    pieces, halo_ref, out_ref, onehot = rest[: z.lev], rest[z.lev], rest[z.lev + 1], rest[z.lev + 2]
    p = scal[0]
    off = scal[1 + pl.program_id(0)]
    at = 0
    for base, size in ((own_base, z.ro), (halo_base, z.rh)):
        row = lax.broadcasted_iota(jnp.int32, (z.tokens, size), 0)
        for k in range(z.lev):
            hit = row == base[...] + (off * z.rows + (p ^ k) * (z.nb * WLAT))
            onehot[:, at : at + size] = jnp.where(hit, 1.0, 0.0).astype(BF16)
            at += size
    columns = []
    for j in range(z.nblk):
        rows = [r[0, j] for r in pieces] + [halo_ref[k, 0, j] for k in range(z.lev)]
        columns.append(jnp.concatenate(rows, axis=0))
    moved = nn(onehot[...], jnp.concatenate(columns, axis=1))
    half = z.d - LANES
    for l in range(z.l):
        low = moved[:, l * LANES : (l + 1) * LANES]
        at = (z.l + l // 2) * LANES + (l % 2) * half
        tokens = jnp.concatenate([low, moved[:, at : at + half]], axis=1)
        out_ref[0, l] = tokens.reshape(z.cells, z.rows, z.d).astype(BF16)


def unpack(z, own, halo, scal):
    bases = [jnp.asarray(v)[None] for v in slot_rows(z)]
    spec = pl.BlockSpec((1, z.nblk, z.ro, LANES), lambda s, _: (s, 0, 0, 0))
    return pl.pallas_call(
        functools.partial(unpack_kernel, z),
        grid_spec=pltpu.PrefetchScalarGridSpec(
            num_scalar_prefetch=1,
            grid=(z.s,),
            in_specs=[pl.BlockSpec((1, v.shape[1]), lambda s, _: (0, 0)) for v in bases]
            + [spec] * z.lev
            + [pl.BlockSpec((z.lev, 1, z.nblk, z.rh, LANES), lambda s, _: (0, s, 0, 0, 0))],
            out_specs=pl.BlockSpec((1, z.l, z.cells, z.rows, z.d), lambda s, _: (s, 0, 0, 0, 0)),
            scratch_shapes=[pltpu.VMEM((z.tokens, z.lev * (z.ro + z.rh)), BF16)],
        ),
        out_shape=jax.ShapeDtypeStruct((z.s, z.l, z.cells, z.rows, z.d), BF16),
        compiler_params=pltpu.CompilerParams(vmem_limit_bytes=60 * 2**20),
        cost_estimate=cost(4),
        name="unpack",
    )(scal, *bases, *own, halo)


def cost(microseconds):
    return pl.CostEstimate(
        flops=int(microseconds * 5e8), transcendentals=0, bytes_accessed=int(microseconds * 3e6)
    )


def loop(n, body, unroll=None):
    unroll = n if unroll is None else unroll

    def some(i, c):
        for j in range(unroll):
            body(i * unroll + j)
        return c

    if n == unroll:
        some(0, 0)
    else:
        lax.fori_loop(0, n // unroll, some, 0)


def head_masks(z, weight=1.0):
    lane = lax.broadcasted_iota(jnp.int32, (1, LANES), 1)
    size = z.d // z.heads
    inside = [(lane >= h * size) & (lane < (h + 1) * size) for h in range(z.heads // 2)]
    return [jnp.where(m, weight, 0.0) for m in inside]


def spread(values, factors):
    return jnp.concatenate([values * f for f in factors], axis=0).astype(BF16)


def gather_heads(stacked, factors):
    n = stacked.shape[0] // len(factors)
    total = stacked[:n] * factors[0]
    for h in range(1, len(factors)):
        total = total + stacked[h * n : (h + 1) * n] * factors[h]
    return total


def pipelined(n, first, second, third):
    one, two = {}, {}
    for i in range(n + 2):
        if i < n:
            one[i] = first(i)
        if 0 <= i - 1 < n:
            two[i - 1] = second(i - 1, one.pop(i - 1))
        if i >= 2:
            third(i - 2, two.pop(i - 2))


def score(q, k, ones):
    return nt(k.astype(BF16), spread(q, ones))


def soften(scores):
    exps = jnp.exp2(scores - jnp.max(scores, axis=0, keepdims=True))
    return (exps * (1.0 / jnp.sum(exps, axis=0, keepdims=True))).astype(BF16)


def mix(probs, v, ones):
    return gather_heads(tn(probs, v.astype(BF16)), ones)


def grad_scores_of(probs, grad_probs):
    wide = probs.astype(F32)
    inner = jnp.sum(grad_probs * wide, axis=0, keepdims=True)
    return (wide * (grad_probs - inner)).astype(BF16)


def centered(values):
    return values - jnp.mean(values, axis=-1, keepdims=True)


def rstd_of(center):
    return lax.rsqrt(jnp.mean(center * center, axis=-1, keepdims=True) + EPSILON)


def norm_levels(n, load, store):
    def first(i):
        values = load(i)
        return values, centered(values)

    def second(i, got):
        return got + (rstd_of(got[1]),)

    def third(i, got):
        values, center, rstd = got
        store(i, values, center * rstd, rstd)

    pipelined(n, first, second, third)


def fold_rows(values):
    return jnp.sum(values.reshape(values.shape[0] // 8, 8, values.shape[1]), axis=0)


def load_wire(z, refs, wire_s):
    for k in range(z.lev):
        wire_s[k] = refs[k][0].astype(F32)


def wire_level(z, wire_s, k, l, b):
    half = z.d - LANES
    at = (l % 2) * half
    rows = pl.ds(pl.multiple_of(b * TOK, 8), TOK)
    low, high = wire_s[k, l, rows, :], wire_s[k, z.l + l // 2, rows, :]
    return jnp.concatenate([low, high[:, at : at + half]], axis=1)


def store_wire_levels(z, wire_s, b, level):
    for k in range(z.lev):
        parts = lane_parts(z, [level(k * z.l + l) for l in range(z.l)])
        for j, part in enumerate(parts):
            wire_s[k, j, pl.ds(pl.multiple_of(b * TOK, 8), TOK), :] = part


def flush_wire(z, wire_s, refs):
    if z.ro > z.nb * TOK:
        wire_s[:, :, z.nb * TOK :, :] = jnp.zeros_like(wire_s[:, :, z.nb * TOK :, :])
    for k in range(z.lev):
        refs[k][0] = wire_s[k].astype(BF16)


def bf16_rows(z, ref):
    return ref[...].reshape(z.n, ref.shape[-1]).astype(BF16)


def put_rows(z, ref, values):
    ref[...] = values.reshape(z.lt, TOK, values.shape[-1])


def some_rows(z, ref, i):
    rows = ref[i * CHUNK : (i + 1) * CHUNK]
    return rows.reshape(CHUNK * TOK, ref.shape[-1]).astype(BF16)


def tile(j, t):
    return slice((2 * j + t) * LANES, (2 * j + t + 1) * LANES)


def put(ref, at, value):
    ref[at] = value


def group(g):
    return slice(g * GROUP, (g + 1) * GROUP)


def attention(n, qkv, bias, probs_at, store, ones, factor):
    def first(i):
        return [
            (score(qkv(i, 0, t), qkv(i, 1, t), ones) * factor + bias(t), qkv(i, 2, t)) for t in range(2)
        ]

    def second(i, got):
        return [(soften(scores), v) for scores, v in got]

    def third(i, got):
        outs = [mix(probs, v, ones) for probs, v in got]
        for t in range(2):
            probs_at(i, t)[...] = got[t][0]
            store(i, t, outs[t])

    pipelined(n, first, second, third)


def attention_back(n, qkv, grad, probs_at, store, ones, scales, scale):
    def first(i):
        out = []
        for t in range(2):
            q, k, v = (qkv(i, j, t) for j in range(3))
            g_rows = spread(grad(i, t), ones)
            out.append(
                (probs_at(i, t)[...], nt(v.astype(BF16), g_rows), g_rows, spread(q, ones), k.astype(BF16))
            )
        return out

    def second(i, got):
        return [(item[0], grad_scores_of(item[0], item[1])) + item[2:] for item in got]

    def third(i, got):
        outs = []
        for probs, grad_scores, g_rows, q_rows, k in got:
            outs.append(
                (
                    gather_heads(tn(grad_scores, k), scales),
                    nn(grad_scores, q_rows) * scale,
                    nn(probs, g_rows),
                    grad_scores,
                )
            )
        for t in range(2):
            store(i, t, outs[t])

    pipelined(n, first, second, third)


def score_factor(z):
    return np.float32((z.d // z.heads) ** (-0.5) * np.log2(np.e))


def forward_kernel(z, *refs):
    it = iter(refs)
    take = lambda n: [next(it) for _ in range(n)]
    wire_in = take(z.lev)
    bias_ref, mask_ref, column_mask = take(3)
    gain1, shift1, gain2, shift2, gain3, shift3 = take(6)
    w_qkv1, wo1, w_qkv2, wo2, w_up, w_down_t = take(6)
    wire_out = take(z.lev)
    norm1_ref, norm2_ref, norm3_ref, att_ref, co_ref, act_ref, slope_ref, probs_ref, probs2_ref = take(9)
    wire_s, x_s, n_s, o_s, a_s, qkv_s, bias_s = take(7)
    ones = head_masks(z)
    b = pl.program_id(1)

    @pl.when(b == 0)
    def _():
        load_wire(z, wire_in, wire_s)

    bias_s[...] = bias_ref[0] + mask_ref[0, 0]

    def keep(ref, gain, shift):
        def store(lv, values, normed, rstd):
            x_s[lv] = values
            n_s[lv] = normed * gain[...] + shift[...]
            room = jnp.broadcast_to(rstd, (TOK, 2 * LANES - z.d))
            ref[0, 0, lv] = jnp.concatenate([normed, room], axis=1)

        return store

    norm_levels(
        z.lt, lambda lv: wire_level(z, wire_s, lv // z.l, lv % z.l, b), keep(norm1_ref, gain1, shift1)
    )
    put_rows(z, qkv_s, nn(bf16_rows(z, n_s), w_qkv1[...]))

    attention(
        z.lt,
        lambda lv, j, t: qkv_s[lv, :, tile(j, t)],
        lambda t: bias_s[t],
        lambda lv, t: probs_ref.at[0, 0, lv, t],
        lambda lv, t, out: put(a_s, (lv, slice(None), tile(0, t)), out),
        ones,
        score_factor(z),
    )
    att = bf16_rows(z, a_s)
    att_ref[0, 0] = att
    put_rows(z, o_s, nn(att, wo1[...]))

    norm_levels(z.lt, lambda lv: x_s[lv] + o_s[lv], keep(norm2_ref, gain2, shift2))
    put_rows(z, qkv_s, nn(bf16_rows(z, n_s), w_qkv2[...]))

    attention(
        TOK // GROUP,
        lambda g, j, t: qkv_s[:, group(g), tile(j, t)].reshape(z.lt * GROUP, LANES),
        lambda t: column_mask[...],
        lambda g, t: probs2_ref.at[0, 0, g, t],
        lambda g, t, out: put(a_s, (slice(None), group(g), tile(0, t)), out.reshape(z.lt, GROUP, LANES)),
        ones,
        score_factor(z),
    )
    co = bf16_rows(z, a_s)
    co_ref[0, 0] = co
    put_rows(z, o_s, nn(co, wo2[...]))

    norm_levels(z.lt, lambda lv: x_s[lv] + o_s[lv], keep(norm3_ref, gain3, shift3))

    def up(i):
        return nn(some_rows(z, n_s, i), w_up[...])

    def gelu(i, hidden):
        share = 0.5 + 0.5 * lax.erf(hidden * (0.5**0.5))
        density = jnp.exp(hidden * hidden * -0.5) * ((2.0 * np.pi) ** -0.5)
        return (hidden * share).astype(BF16), (share + hidden * density).astype(BF16)

    def down(i, got):
        act, slope = got
        out = nt(act, w_down_t[...])
        rows = slice(i * CHUNK * TOK, (i + 1) * CHUNK * TOK)
        act_ref[0, 0, rows], slope_ref[0, 0, rows] = act, slope
        o_s[i * CHUNK : (i + 1) * CHUNK] = out.reshape(CHUNK, TOK, z.d)

    pipelined(z.lt // CHUNK, up, gelu, down)

    store_wire_levels(z, wire_s, b, lambda lv: x_s[lv] + o_s[lv])

    @pl.when(b == z.nb - 1)
    def _():
        flush_wire(z, wire_s, wire_out)


def wire_specs(z):
    return [pl.BlockSpec((1, z.nblk, z.ro, LANES), lambda s, b: (s, 0, 0, 0))] * z.lev


def wire_shapes(z):
    return [jax.ShapeDtypeStruct((z.s, z.nblk, z.ro, LANES), BF16)] * z.lev


def unit_spec(shape):
    return pl.BlockSpec((1, 1) + shape, lambda s, b: (s, b) + (0,) * len(shape))


def whole_spec(array):
    return pl.BlockSpec(array.shape, lambda s, b: (0,) * array.ndim)


def residual_shapes(z):
    return [
        ((z.lt, TOK, 2 * LANES), F32),
        ((z.lt, TOK, 2 * LANES), F32),
        ((z.lt, TOK, 2 * LANES), F32),
        ((z.n, 2 * LANES), BF16),
        ((z.n, 2 * LANES), BF16),
        ((z.n, z.ff), BF16),
        ((z.n, z.ff), BF16),
        ((z.lt, 2, TOK, z.heads // 2 * TOK), BF16),
        ((TOK // GROUP, 2, z.lt * GROUP, z.heads // 2 * z.lt * GROUP), BF16),
    ]


def forward(z, wire, bias, mask, column_mask, norms, weights):
    res = residual_shapes(z)
    rows3 = (z.lt, TOK, z.d)
    out = pl.pallas_call(
        functools.partial(forward_kernel, z),
        grid=(z.s, z.nb),
        in_specs=wire_specs(z)
        + [
            pl.BlockSpec((1, 2, TOK, z.heads // 2 * TOK), lambda s, b: (b, 0, 0, 0)),
            pl.BlockSpec((1, 1, TOK, 1), lambda s, b: (s, b, 0, 0)),
            whole_spec(column_mask),
        ]
        + [whole_spec(a) for a in norms]
        + [whole_spec(a) for a in weights],
        out_specs=wire_specs(z) + [unit_spec(shape) for shape, _ in res],
        out_shape=wire_shapes(z) + [jax.ShapeDtypeStruct((z.s, z.nb) + shape, t) for shape, t in res],
        scratch_shapes=[pltpu.VMEM((z.lev, z.nblk, z.ro, LANES), F32)]
        + [pltpu.VMEM(rows3, F32)] * 3
        + [
            pltpu.VMEM((z.lt, TOK, 2 * LANES), F32),
            pltpu.VMEM((z.lt, TOK, 6 * LANES), F32),
            pltpu.VMEM((2, TOK, z.heads // 2 * TOK), F32),
        ],
        compiler_params=pltpu.CompilerParams(vmem_limit_bytes=60 * 2**20),
        cost_estimate=cost(30),
        name="forward",
    )(*wire, bias, mask, column_mask, *norms, *weights)
    return out[: z.lev], out[z.lev :]


def grad_list(z):
    return [
        ("up", z.ff), ("down_t", z.ff),
        ("qkv1", 3 * z.d), ("qkv2", 3 * z.d),
        ("o1", z.d), ("o2", z.d),
    ]


def half_blocks(z):
    full, rest = [], []
    for name, columns in grad_list(z):
        for row in range(0, z.d, 96):
            for col in range(0, columns, LANES):
                width = min(LANES, columns - col)
                (full if width == LANES else rest).append((name, row, col, width))
    out = [[piece + (0,)] for piece in full]
    for i in range(0, len(rest), 2):
        out.append([rest[i] + (0,), rest[i + 1] + (rest[i][3],)])
    return out


def grad_buffer(z, name, columns):
    if name[:3] == "qkv":
        return (z.d, 6 * LANES)
    if name[0] == "o":
        return (2 * LANES, columns)
    return (z.d, columns)


def grad_block(z, name, ref, row, col, width):
    half = z.d // 2
    if name[0] == "o":
        start = row // half * LANES
        return ref[start : start + 96, col : col + width]
    if name[:3] != "qkv":
        return ref[row : row + 96, col : col + width]
    pieces = []
    while width:
        t, lane = col // half, col % half
        count = min(width, half - lane)
        pieces.append(ref[row : row + 96, t * LANES + lane : t * LANES + lane + count])
        col, width = col + count, width - count
    return pieces[0] if len(pieces) == 1 else jnp.concatenate(pieces, axis=1)


def bias_rows(z):
    pick = np.zeros((WLON * 8, TOK), np.float32)
    for a in range(WLON):
        for i in range(WLAT):
            pick[a * 8 + i, a * WLAT + i] = 1.0
    return pick


def backward_kernel(z, scal, *refs):
    it = iter(refs)
    take = lambda n: [next(it) for _ in range(n)]
    wire_in = take(z.lev)
    norm1_ref, norm2_ref, norm3_ref, att_ref, co_ref, act_ref, slope_ref, probs_ref, probs2_ref = take(9)
    (pick_ref,) = take(1)
    gain1, shift1, gain2, shift2, gain3, shift3 = take(6)
    w_qkv1, wo1, w_qkv2, wo2, w_up, w_down_t = take(6)
    wire_out = take(z.lev)
    mine_ref, other_ref = take(2)
    wire_s, g_s, o_s, a_s, qkv_s, grad_s, gh_s, db_s, vec_s, sums_s = take(10)
    grads = {name: ref for (name, _), ref in zip(grad_list(z), take(len(grad_list(z))))}
    scale = np.float32((z.d // z.heads) ** (-0.5))
    ones, scales = head_masks(z), head_masks(z, scale)
    s, b = pl.program_id(0), pl.program_id(1)

    @pl.when((s == 0) & (b == 0))
    def _():
        for ref in list(grads.values()) + [db_s, vec_s]:
            ref[...] = jnp.zeros_like(ref)

    @pl.when(b == 0)
    def _():
        load_wire(z, wire_in, wire_s)

    for k in range(z.lev):
        got = [wire_level(z, wire_s, k, l, b) for l in range(z.l)]
        for l in range(z.l):
            g_s[k * z.l + l] = got[l]

    def normed_tokens(ref, gain, shift):
        normed = ref[0, 0][:, :, : z.d] * gain[...] + shift[...]
        return normed.reshape(z.n, z.d).astype(BF16)

    def back_down(i):
        rows = slice(i * CHUNK * TOK, (i + 1) * CHUNK * TOK)
        return nn(some_rows(z, g_s, i), w_down_t[...]), slope_ref[0, 0, rows, :].astype(F32)

    def back_gelu(i, got):
        return (got[0] * got[1]).astype(BF16)

    def back_up(i, grad):
        out = nt(grad, w_up[...])
        gh_s[i * CHUNK * TOK : (i + 1) * CHUNK * TOK] = grad
        o_s[i * CHUNK : (i + 1) * CHUNK] = out.reshape(CHUNK, TOK, z.d)

    pipelined(z.lt // CHUNK, back_down, back_gelu, back_up)
    grads["down_t"][...] += tn(bf16_rows(z, g_s), act_ref[0, 0])
    grads["up"][...] += tn(normed_tokens(norm3_ref, gain3, shift3), gh_s[...])

    def norm_step(ref, gain, at, target):
        sums = [vec_s[at], vec_s[at + 1]]

        def first(lv):
            grad, normed, rstd = o_s[lv], ref[0, 0, lv, :, : z.d], ref[0, 0, lv, :, z.d : z.d + 1]
            sums[0] += fold_rows(grad * normed)
            sums[1] += fold_rows(grad)
            return target[lv], normed, rstd, grad * gain[...]

        def second(lv, got):
            old, normed, rstd, gained = got
            one = jnp.mean(gained, axis=-1, keepdims=True)
            two = jnp.mean(gained * normed, axis=-1, keepdims=True)
            return old, normed, rstd, gained, one, two

        def third(lv, got):
            old, normed, rstd, gained, one, two = got
            target[lv] = old + rstd * (gained - one - normed * two)

        pipelined(z.lt, first, second, third)
        vec_s[at], vec_s[at + 1] = sums

    norm_step(norm3_ref, gain3, 4, g_s)

    branch = bf16_rows(z, g_s)
    grads["o2"][...] += tn(co_ref[0, 0], branch)
    put_rows(z, a_s, nt(branch, wo2[...]))
    tokens = normed_tokens(norm2_ref, gain2, shift2)
    put_rows(z, qkv_s, nn(tokens, w_qkv2[...]))

    def keep_column(g, t, got):
        for j in range(3):
            grad_s[:, group(g), tile(j, t)] = got[j].reshape(z.lt, GROUP, LANES)

    attention_back(
        TOK // GROUP,
        lambda g, j, t: qkv_s[:, group(g), tile(j, t)].reshape(z.lt * GROUP, LANES),
        lambda g, t: a_s[:, group(g), tile(0, t)].reshape(z.lt * GROUP, LANES),
        lambda g, t: probs2_ref.at[0, 0, g, t],
        keep_column,
        ones,
        scales,
        scale,
    )

    def project_back(tokens, name, w):
        grad = bf16_rows(z, grad_s)
        grads[name][...] += tn(tokens, grad)
        put_rows(z, o_s, nt(grad, w[...]))

    project_back(tokens, "qkv2", w_qkv2)
    norm_step(norm2_ref, gain2, 2, g_s)

    branch = bf16_rows(z, g_s)
    grads["o1"][...] += tn(att_ref[0, 0], branch)
    put_rows(z, a_s, nt(branch, wo1[...]))
    tokens = normed_tokens(norm1_ref, gain1, shift1)
    put_rows(z, qkv_s, nn(tokens, w_qkv1[...]))

    def keep_window(lv, t, got):
        for j in range(3):
            grad_s[lv, :, tile(j, t)] = got[j]
        db_s[b, t] += got[3].astype(F32)

    attention_back(
        z.lt,
        lambda lv, j, t: qkv_s[lv, :, tile(j, t)],
        lambda lv, t: a_s[lv, :, tile(0, t)],
        lambda lv, t: probs_ref.at[0, 0, lv, t],
        keep_window,
        ones,
        scales,
        scale,
    )
    project_back(tokens, "qkv1", w_qkv1)
    norm_step(norm1_ref, gain1, 0, g_s)

    store_wire_levels(z, wire_s, b, lambda lv: g_s[lv])

    @pl.when(b == z.nb - 1)
    def _():
        flush_wire(z, wire_s, wire_out)

    @pl.when((s == z.s - 1) & (b == z.nb - 1))
    def _():
        p, core = scal[0], scal[1]

        def place(i):
            return ((i // z.lev) ^ core) * z.lev + ((i % z.lev) ^ p)

        for at, pieces in enumerate(half_blocks(z)):
            values = [grad_block(z, n, grads[n], r, c, width) for n, r, c, width, _ in pieces]
            block = values[0] if len(values) == 1 else jnp.concatenate(values, axis=1)
            start = (at % z.hb) * 96
            sums_s[place(at // z.hb), start : start + 96, :] = block.astype(BF16)
        extra = z.hb * 96
        sums_s[:, extra:, :] = jnp.zeros_like(sums_s[:, extra:, :])
        vectors = [jnp.sum(vec_s[i], axis=0, keepdims=True) for i in range(6)]
        vectors = jnp.concatenate(vectors + [jnp.zeros((UNIT - 6, z.d), F32)], axis=0)
        vectors = jnp.concatenate([vectors, jnp.zeros((UNIT, 2 * LANES - z.d), F32)], axis=1)

        def put_unit(u, value):
            start = extra + (u % z.upp) * UNIT
            if not isinstance(u, int):
                start = pl.multiple_of(start, UNIT)
            sums_s[place(u // z.upp), pl.ds(start, UNIT), :] = value.astype(BF16)

        for j in range(2):
            put_unit(z.bands * 4 + j, vectors[:, j * LANES : (j + 1) * LANES])
        lane = lax.broadcasted_iota(jnp.int32, (1, z.heads * TOK), 1)
        odd = jnp.zeros(lane.shape, jnp.bool_)
        for h in range(1, z.heads, 2):
            odd = odd | ((lane >= h * TOK) & (lane < (h + 1) * TOK))
        width = -(-(z.heads * TOK) // LANES) * LANES
        for band in range(z.nb):
            rows = [nn(pick_ref[...], db_s[band, t], precision=lax.Precision.HIGHEST) for t in range(2)]
            rows = jnp.concatenate(rows, axis=1)
            halves = []
            for parity in range(2):
                kept = jnp.where(odd if parity else ~odd, rows, 0.0)
                kept = jnp.concatenate(
                    [kept, jnp.zeros((rows.shape[0], width - z.heads * TOK), F32)], axis=1
                )
                total = None
                for a in range(WLON):
                    part = kept[a * 8 : (a + 1) * 8]
                    shift = (WLON - 1 - a) * WLAT
                    if shift:
                        part = pltpu.roll(part, shift, 1)
                    total = part if total is None else total + part
                halves.append(total)
            both = jnp.concatenate(halves, axis=0)
            for j in range(4):
                put_unit((scal[0] * z.nb + band) * 4 + j, both[:, j * LANES : (j + 1) * LANES])
        mine_ref[...] = sums_s[: z.lev]
        other_ref[...] = sums_s[z.lev :]


def backward(z, scal, wire, residuals, norms, weights):
    res = residual_shapes(z)
    rows3 = (z.lt, TOK, z.d)
    pick = jnp.asarray(bias_rows(z))
    drop = lambda spec: pl.BlockSpec(spec.block_shape, lambda s, b, _, m=spec.index_map: m(s, b))
    half = (z.lev, z.pr, LANES)
    out = pl.pallas_call(
        functools.partial(backward_kernel, z),
        grid_spec=pltpu.PrefetchScalarGridSpec(
            num_scalar_prefetch=1,
            grid=(z.s, z.nb),
            in_specs=[
                drop(spec)
                for spec in wire_specs(z)
                + [unit_spec(shape) for shape, _ in res]
                + [whole_spec(pick)]
                + [whole_spec(a) for a in norms]
                + [whole_spec(a) for a in weights]
            ],
            out_specs=[drop(spec) for spec in wire_specs(z)]
            + [pl.BlockSpec(half, lambda s, b, _: (0, 0, 0))] * 2,
            scratch_shapes=[pltpu.VMEM((z.lev, z.nblk, z.ro, LANES), F32)]
            + [pltpu.VMEM(rows3, F32)] * 2
            + [
                pltpu.VMEM((z.lt, TOK, 2 * LANES), F32),
                pltpu.VMEM((z.lt, TOK, 6 * LANES), F32),
                pltpu.VMEM((z.lt, TOK, 6 * LANES), F32),
                pltpu.VMEM((z.n, z.ff), BF16),
                pltpu.VMEM((z.nb, 2, TOK, z.heads // 2 * TOK), F32),
                pltpu.VMEM((6, 8, z.d), F32),
                pltpu.VMEM((z.np, z.pr, LANES), BF16),
            ]
            + [pltpu.VMEM(grad_buffer(z, *item), F32) for item in grad_list(z)],
        ),
        out_shape=wire_shapes(z) + [jax.ShapeDtypeStruct(half, BF16)] * 2,
        compiler_params=pltpu.CompilerParams(vmem_limit_bytes=62 * 2**20),
        cost_estimate=cost(40),
        name="backward",
    )(scal, *wire, *residuals, pick, *norms, *weights)
    return out[: z.lev], out[z.lev], out[z.lev + 1]


def tree(parts):
    while len(parts) > 1:
        parts = [parts[i] + parts[i + 1] for i in range(0, len(parts), 2)]
    return parts[0]


def lev_swap(z, array, k):
    return lax.ppermute(array, "lev", [(i, i ^ k) for i in range(z.lev)])


def lon_swap(z, array, k):
    return lax.ppermute(array, "lon", [(i, i ^ k) for i in range(z.lon)])


def sum_wire(z, mine, other):
    got = lon_swap(z, other, 1)
    half = [(mine[k].astype(F32) + got[k].astype(F32)).astype(BF16) for k in range(z.lev)]
    parts = [half[0]] + [lev_swap(z, half[k], k) for k in range(1, z.lev)]
    quarter = tree([v.astype(F32) for v in parts]).astype(BF16)
    parts = [quarter] + [lon_swap(z, quarter, 2 * k) for k in range(1, z.lon // 2)]
    done = tree([v.astype(F32) for v in parts]).astype(BF16)
    own = jnp.stack([done] + [lev_swap(z, done, k) for k in range(1, z.lev)])
    return own, lon_swap(z, own, 1)


def table_lanes(z, h):
    lanes = np.full((WLAT, 32), -1, np.int32)
    for i in range(WLAT):
        lanes[i, : 2 * WLON - 1] = h * TOK + np.arange(2 * WLON - 1) * WLAT + i
    return lanes.reshape(1, WLAT * 32)


def finish_kernel(z, scal, lanes, order, own, other, *outs):
    p, core = scal[0], scal[1]
    named = {name: ref for (name, _), ref in zip(grad_list(z), outs)}
    vec_refs, bias_ref = outs[len(named) : len(named) + 6], outs[len(named) + 6]

    def read(piece, start, size):
        half, j = piece // z.lev, piece % z.lev
        rows = slice(start, start + size)
        return jnp.where(core == half, own[p ^ j, rows, :], other[p ^ j, rows, :])

    for at, pieces in enumerate(half_blocks(z)):
        block = read(at // z.hb, (at % z.hb) * 96, 96).astype(F32)
        for n, r, c, width, lane in pieces:
            named[n][r : r + 96, c : c + width] = block[:, lane : lane + width]
    extra = z.hb * 96
    units = [read(u // z.upp, extra + (u % z.upp) * UNIT, UNIT) for u in range(z.units)]
    vectors = jnp.concatenate(units[z.bands * 4 :], axis=1).astype(F32)
    for i in range(6):
        vec_refs[i][...] = vectors[i : i + 1, : z.d]
    table = [jnp.concatenate(units[4 * k : 4 * k + 4], axis=1) for k in range(z.bands)]
    table = nn(order[...], jnp.concatenate(table, axis=0)).astype(BF16)
    half = table.shape[0] // 2
    for h in range(z.heads):
        at = lax.broadcasted_iota(jnp.int32, (4 * LANES, WLAT * 32), 0)
        pick = jnp.where(at == lanes[h : h + 1, :], 1.0, 0.0).astype(BF16)
        rows = table[(h % 2) * half : (h % 2) * half + half]
        got = nn(rows, pick)
        for i in range(WLAT):
            values = got[: WLAT * z.bands, i * 32 : i * 32 + 2 * WLON - 1]
            bias_ref[h, i] = values.reshape(WLAT, z.bands, 2 * WLON - 1)


def finish(z, scal, own, other):
    shapes = [jax.ShapeDtypeStruct((z.d, columns), F32) for _, columns in grad_list(z)]
    shapes += [jax.ShapeDtypeStruct((1, z.d), F32)] * 6
    shapes += [jax.ShapeDtypeStruct((z.heads, WLAT, WLAT, z.bands, 2 * WLON - 1), F32)]
    lanes = jnp.asarray(np.concatenate([table_lanes(z, h) for h in range(z.heads)]))
    order = np.zeros((2 * 8 * z.bands, z.bands * UNIT), np.float32)
    for parity in range(2):
        for i in range(8):
            for k in range(z.bands):
                order[parity * 8 * z.bands + i * z.bands + k, k * UNIT + parity * 8 + i] = 1.0
    order = jnp.asarray(order, BF16)
    full = lambda a: pl.BlockSpec(a.shape, lambda i, _, n=len(a.shape): (0,) * n)
    out = pl.pallas_call(
        functools.partial(finish_kernel, z),
        grid_spec=pltpu.PrefetchScalarGridSpec(
            num_scalar_prefetch=1,
            grid=(1,),
            in_specs=[full(a) for a in (lanes, order, own, other)],
            out_specs=[full(a) for a in shapes],
        ),
        out_shape=shapes,
        compiler_params=pltpu.CompilerParams(vmem_limit_bytes=60 * 2**20),
        cost_estimate=cost(4),
        name="finish",
    )(scal, lanes, order, own, other)
    named = {name: value for (name, _), value in zip(grad_list(z), out)}
    vectors = [v.reshape(z.d) for v in out[len(named) : len(named) + 6]]
    return named, vectors, out[-1].transpose(3, 0, 1, 2, 4)


def bias_kernel(z, table_ref, pick_ref, out_ref, even_s, odd_s):
    width = 4 * LANES
    lane = lax.broadcasted_iota(jnp.int32, (2 * WLON - 1, width), 1)
    step = lax.broadcasted_iota(jnp.int32, (2 * WLON - 1, width), 0) * WLAT
    for parity, ref in ((0, even_s), (1, odd_s)):
        total = None
        for h in range(parity, z.heads, 2):
            for i in range(WLAT):
                place = jnp.where(lane == step + (h * TOK + i), 1.0, 0.0).astype(BF16)
                values = table_ref[h, i]
                high = values.astype(BF16)
                low = (values - high.astype(F32)).astype(BF16)
                part = nn(jnp.concatenate([high, low], axis=0), place)
                total = part if total is None else total + part
        rows = z.nb * 8
        ref[...] = total[:rows] + total[rows:]
    head = lax.broadcasted_iota(jnp.int32, (1, width), 1)
    odd = jnp.zeros(head.shape, jnp.bool_)
    for h in range(1, z.heads, 2):
        odd = odd | ((head >= h * TOK) & (head < (h + 1) * TOK))
    side = z.heads // 2 * TOK
    for b in range(z.nb):
        even, uneven = even_s[b * 8 : (b + 1) * 8], odd_s[b * 8 : (b + 1) * 8]
        rows = []
        for a in range(WLON):
            shift = (width - (WLON - 1 - a) * WLAT) % width
            turned = [pltpu.roll(v, shift, 1) if shift else v for v in (even, uneven)]
            rows.append(jnp.where(odd, turned[1], turned[0]))
        rows = jnp.concatenate(rows, axis=0)
        full = lax.dot_general(
            pick_ref[...], rows, (((0,), (0,)), ((), ())),
            precision=lax.Precision.HIGHEST, preferred_element_type=F32,
        ) * np.float32(np.log2(np.e))
        out_ref[b, 0] = full[:, :side]
        out_ref[b, 1] = full[:, side : 2 * side]


def bias_of(z, bias_table, p):
    table = lax.dynamic_slice_in_dim(bias_table, p * z.nb, z.nb, axis=0)
    table = jnp.pad(table.transpose(1, 2, 0, 3, 4), ((0, 0),) * 3 + ((0, 2), (0, 0)))
    table = table.reshape(z.heads, WLAT, z.nb * 8, 2 * WLON - 1)
    return pl.pallas_call(
        functools.partial(bias_kernel, z),
        out_shape=jax.ShapeDtypeStruct((z.nb, 2, TOK, z.heads // 2 * TOK), F32),
        scratch_shapes=[pltpu.VMEM((z.nb * 8, 4 * LANES), F32)] * 2,
        compiler_params=pltpu.CompilerParams(vmem_limit_bytes=60 * 2**20),
        cost_estimate=cost(4),
        name="bias",
    )(table, jnp.asarray(bias_rows(z)))


def lev_exchange(z, wire):
    return [wire[0]] + [lev_swap(z, wire[k], k) for k in range(1, z.lev)]


def lon_shift(z, array, distance):
    return lax.ppermute(array, "lon", [(w, (w + distance) % z.lon) for w in range(z.lon)])


def last_cells(z, wire):
    rows = [a[:, :, : z.nb * TOK].reshape(z.s, z.nblk, z.nb, TOK, LANES)[:, :, :, HALO0:] for a in wire]
    return jnp.stack(rows).reshape(z.lev, z.s, z.nblk, z.rh, LANES)


def on_device(
    inputs, cotangent, grid_sizes, offsets, gain_one, shift_one, qkv_window, out_window, bias_table,
    gain_two, shift_two, qkv_column, out_column, gain_three, shift_three, w_up, w_down,
):
    d = inputs.shape[-1]
    z = Sizes(lax.axis_size("lev"), lax.axis_size("lon"), inputs.shape, bias_table.shape[1], w_up.shape[1])
    p, w = lax.axis_index("lev"), lax.axis_index("lon")
    scal = jnp.concatenate([p[None].astype(jnp.int32), offsets.astype(jnp.int32)])
    swap = lambda a: a.transpose(0, 1, 3, 2, 4)

    half = WLON // 2
    x, c = swap(inputs), swap(cotangent)
    halo_x = lon_shift(z, x[:, :, :half], -1)
    halo_c = lon_shift(z, c[:, :, :half], -1)
    bias = bias_of(z, bias_table, p)
    wire_x = lev_exchange(z, pack(z, x, halo_x, scal))
    wire_c = lev_exchange(z, pack(z, c, halo_c, scal))
    cell = (w * z.cells + offsets[:, None] + jnp.arange(WLON)[None, :]) % (z.cells * z.lon)
    row = (p * z.nb + jnp.arange(z.nb))[:, None] * WLAT + jnp.arange(WLAT)[None, :]
    cell_ok = cell < grid_sizes[:, 1:2]
    row_ok = row[None] < grid_sizes[:, 0][:, None, None]
    valid = cell_ok[:, None, :, None] & row_ok[:, :, None, :]
    mask = jnp.where(valid, 0.0, NEGATIVE).astype(F32).reshape(z.s, z.nb, TOK, 1)
    of_key = np.arange(z.lt * GROUP) % GROUP
    of_query = np.tile(of_key, z.heads // 2)
    column_mask = jnp.asarray(
        np.where(of_key[:, None] == of_query[None, :], 0.0, NEGATIVE).astype(np.float32)
    )

    norms = [v[None] for v in (gain_one, shift_one, gain_two, shift_two, gain_three, shift_three)]
    room = ((0, 0), (0, 0), (0, LANES - d // 2))
    wide = lambda a: jnp.pad(a.reshape(d, 6, d // 2), room).reshape(d, 6 * LANES)
    tall = lambda a: jnp.pad(a.reshape(2, d // 2, d), (room[0], room[2], room[0])).reshape(2 * LANES, d)
    weights = [wide(qkv_window), tall(out_window), wide(qkv_column), tall(out_column), w_up, w_down.T]

    places = jnp.stack([p, w % 2]).astype(jnp.int32)
    wire_r, residuals = forward(z, wire_x, bias, mask, column_mask, norms, weights)
    wire_r = lev_exchange(z, wire_r)
    wire_g, mine, other = backward(z, places, wire_c, residuals, norms, weights)
    wire_g = lev_exchange(z, wire_g)
    result = unpack(z, wire_r, lon_shift(z, last_cells(z, wire_r), 1), scal)
    input_grad = unpack(z, wire_g, lon_shift(z, last_cells(z, wire_g), 1), scal)
    own, other = sum_wire(z, mine, other)
    named, vec, table = finish(z, places, own, other)
    return (
        swap(result), swap(input_grad),
        vec[0], vec[1], named["qkv1"], named["o1"], table,
        vec[2], vec[3], named["qkv2"], named["o2"],
        vec[4], vec[5], named["up"], named["down_t"].T,
    )


def solution(mesh):
    tokens = P(None, "lev", None, "lon", None)
    return jax.shard_map(
        on_device,
        mesh=mesh,
        in_specs=(tokens, tokens) + (P(),) * 15,
        out_specs=(tokens, tokens) + (P(),) * 13,
        check_vma=False,
    )
```

```python
import functools

import jax
import jax.numpy as jnp
import numpy as np
from jax import lax
from jax.experimental import pallas as pl
from jax.experimental.pallas import tpu as pltpu
from jax.sharding import PartitionSpec as P

WLAT = 6
WLON = 12
TOK = WLAT * WLON
HALF = TOK // 2
HALO0 = 32
HALO = TOK - HALO0
GROUP = 8
CHUNK = 2
EPSILON = 1e-05
NEGATIVE = -1000000000.0
F32 = jnp.float32
BF16 = jnp.bfloat16
LANES = 128
UNIT = 16


def up16(n):
    return (n + 15) // 16 * 16


def nn(a, b, **kw):
    return lax.dot_general(a, b, (((1,), (0,)), ((), ())), preferred_element_type=F32, **kw)


def nt(a, b):
    return lax.dot_general(a, b, (((1,), (1,)), ((), ())), preferred_element_type=F32)


def tn(a, b):
    return lax.dot_general(a, b, (((0,), (0,)), ((), ())), preferred_element_type=F32)


class Sizes:
    def __init__(self, lev, lon, shape, heads, hidden):
        self.lev, self.lon = lev, lon
        self.s, self.l, self.rows, self.cells, self.d = shape
        self.heads, self.ff = heads, hidden
        self.bands = self.rows // WLAT
        self.nb = self.bands // lev
        self.lt = self.l * lev
        self.n = self.lt * TOK
        self.ro = up16(self.nb * TOK)
        self.rh = self.nb * HALO
        self.nblk = self.l + (self.l + 1) // 2
        self.tokens = self.cells * self.rows
        self.np = 2 * lev
        self.blocks = 2 * (2 * hidden // 2 + 3 * self.d + self.d) // LANES * (self.d // 96)
        self.hb = self.blocks // self.np
        self.units = self.bands * 4 + 2
        self.upp = -(-self.units // self.np)
        self.pr = self.hb * 96 + self.upp * UNIT


def slot_rows(z):
    own = np.full((z.ro,), -(10**6), np.int32)
    halo = np.full((z.rh,), -(10**6), np.int32)
    for b in range(z.nb):
        for t in range(TOK):
            own[b * TOK + t] = (t // WLAT) * z.rows + b * WLAT + t % WLAT
            if t >= HALF:
                halo[b * HALO + t - HALO0] = own[b * TOK + t] - z.tokens
    return own, halo


def lane_parts(z, levels):
    parts = [v[:, :LANES] for v in levels]
    high = [v[:, LANES:] for v in levels]
    if z.l % 2:
        high.append(jnp.zeros_like(high[0]))
    for l in range(0, len(high), 2):
        parts.append(jnp.concatenate([high[l], high[l + 1]], axis=1))
    return parts


def pack_kernel(z, offsets, base, x_ref, halo_ref, *rest):
    outs, onehot = rest[: z.lev], rest[z.lev]
    p = lax.axis_index("lev")
    rows = z.tokens + halo_ref.shape[2] * z.rows
    column = lax.broadcasted_iota(jnp.int32, (z.ro, rows), 1)
    for s in range(z.s):
        for k in range(z.lev):
            hit = column == base[...] + (offsets[s] * z.rows + (p ^ k) * (z.nb * WLAT))
            onehot[s, k * z.ro : (k + 1) * z.ro] = jnp.where(hit, 1.0, 0.0).astype(BF16)
        levels = []
        for l in range(z.l):
            cells = [r[s, l].reshape(r.shape[2] * z.rows, z.d) for r in (x_ref, halo_ref)]
            levels.append(jnp.concatenate(cells, axis=0))
        moved = nn(onehot[s], jnp.concatenate(lane_parts(z, levels), axis=1)).astype(BF16)
        for k in range(z.lev):
            for j in range(z.nblk):
                outs[k][s, j] = moved[k * z.ro : (k + 1) * z.ro, j * LANES : (j + 1) * LANES]


def in_vmem(count):
    return [pl.BlockSpec(memory_space=pltpu.VMEM)] * count


def in_smem(count):
    return [pl.BlockSpec(memory_space=pltpu.SMEM)] * count


def pack(z, x, halo, offsets):
    own, _ = slot_rows(z)
    rows = z.tokens + halo.shape[2] * z.rows
    return pl.pallas_call(
        functools.partial(pack_kernel, z),
        in_specs=in_smem(1) + in_vmem(3),
        out_specs=in_vmem(z.lev),
        scratch_shapes=[pltpu.VMEM((z.s, z.lev * z.ro, rows), BF16)],
        out_shape=[jax.ShapeDtypeStruct((z.s, z.nblk, z.ro, LANES), BF16)] * z.lev,
        compiler_params=pltpu.CompilerParams(vmem_limit_bytes=40 * 2**20),
        cost_estimate=cost(4),
        name="pack",
    )(offsets, jnp.asarray(own)[:, None], x, halo)


def unpack_kernel(z, merged, offsets, *rest):
    count = 1 if merged else 2
    bases, pieces = rest[:count], rest[count : count + z.lev]
    halo_ref, out_ref, onehot = rest[-3], rest[-2], rest[-1]
    p = lax.axis_index("lev")
    for s in range(z.s):
        at = 0
        for base, size in zip(bases, (z.ro, z.rh)):
            row = lax.broadcasted_iota(jnp.int32, (z.tokens, size), 0)
            for k in range(z.lev):
                place = base[...] + (offsets[s] * z.rows + (p ^ k) * (z.nb * WLAT))
                if merged:
                    place = jnp.where(place >= z.tokens, place - z.tokens, place)
                onehot[s, :, at : at + size] = jnp.where(row == place, 1.0, 0.0).astype(BF16)
                at += size
        columns = []
        for j in range(z.nblk):
            rows = [r[s, j] for r in pieces]
            if not merged:
                rows += [halo_ref[k, s, j] for k in range(z.lev)]
            columns.append(jnp.concatenate(rows, axis=0))
        moved = nn(onehot[s], jnp.concatenate(columns, axis=1))
        half = z.d - LANES
        for l in range(z.l):
            low = moved[:, l * LANES : (l + 1) * LANES]
            at = (z.l + l // 2) * LANES + (l % 2) * half
            tokens = jnp.concatenate([low, moved[:, at : at + half]], axis=1)
            out_ref[s, l] = tokens.reshape(z.cells, z.rows, z.d).astype(BF16)


def unpack(z, own, halo, offsets):
    merged = halo is None
    bases = [jnp.asarray(v)[None] for v in slot_rows(z)][: 1 if merged else 2]
    slots = z.ro if merged else z.ro + z.rh
    arrays = bases + list(own) + ([] if merged else [halo])
    return pl.pallas_call(
        functools.partial(unpack_kernel, z, merged),
        in_specs=in_smem(1) + in_vmem(len(arrays)),
        out_specs=pl.BlockSpec(memory_space=pltpu.VMEM),
        scratch_shapes=[pltpu.VMEM((z.s, z.tokens, z.lev * slots), BF16)],
        out_shape=jax.ShapeDtypeStruct((z.s, z.l, z.cells, z.rows, z.d), BF16),
        compiler_params=pltpu.CompilerParams(vmem_limit_bytes=40 * 2**20),
        cost_estimate=cost(4),
        name="unpack",
    )(offsets, *arrays)


def cost(microseconds):
    return pl.CostEstimate(
        flops=int(microseconds * 5e8), transcendentals=0, bytes_accessed=int(microseconds * 3e6)
    )


def loop(n, body, unroll=None):
    unroll = n if unroll is None else unroll

    def some(i, c):
        for j in range(unroll):
            body(i * unroll + j)
        return c

    if n == unroll:
        some(0, 0)
    else:
        lax.fori_loop(0, n // unroll, some, 0)


def head_masks(z, weight=1.0):
    lane = lax.broadcasted_iota(jnp.int32, (1, LANES), 1)
    size = z.d // z.heads
    inside = [(lane >= h * size) & (lane < (h + 1) * size) for h in range(z.heads // 2)]
    return [jnp.where(m, weight, 0.0) for m in inside]


def spread(values, factors):
    return jnp.concatenate([values * f for f in factors], axis=0).astype(BF16)


def gather_heads(stacked, factors):
    n = stacked.shape[0] // len(factors)
    total = stacked[:n] * factors[0]
    for h in range(1, len(factors)):
        total = total + stacked[h * n : (h + 1) * n] * factors[h]
    return total


def pipelined(n, first, second, third):
    one, two = {}, {}
    for i in range(n + 2):
        if i < n:
            one[i] = first(i)
        if 0 <= i - 1 < n:
            two[i - 1] = second(i - 1, one.pop(i - 1))
        if i >= 2:
            third(i - 2, two.pop(i - 2))


def score(q, k, ones):
    return nt(k.astype(BF16), spread(q, ones))


def soften(scores):
    exps = jnp.exp2(scores - jnp.max(scores, axis=0, keepdims=True))
    return (exps * (1.0 / jnp.sum(exps, axis=0, keepdims=True))).astype(BF16)


def mix(probs, v, ones):
    return gather_heads(tn(probs, v.astype(BF16)), ones)


def grad_scores_of(probs, grad_probs):
    wide = probs.astype(F32)
    inner = jnp.sum(grad_probs * wide, axis=0, keepdims=True)
    return (wide * (grad_probs - inner)).astype(BF16)


def centered(values):
    return values - jnp.mean(values, axis=-1, keepdims=True)


def rstd_of(center):
    return lax.rsqrt(jnp.mean(center * center, axis=-1, keepdims=True) + EPSILON)


def norm_levels(n, load, store):
    def first(i):
        values = load(i)
        return values, centered(values)

    def second(i, got):
        return got + (rstd_of(got[1]),)

    def third(i, got):
        values, center, rstd = got
        store(i, values, center * rstd, rstd)

    pipelined(n, first, second, third)


def fold_rows(values):
    return jnp.sum(values.reshape(values.shape[0] // 8, 8, values.shape[1]), axis=0)


def load_wire(z, refs, wire_s):
    for k in range(z.lev):
        wire_s[k] = refs[k][0].astype(F32)


def wire_level(z, wire_s, k, l, b):
    half = z.d - LANES
    at = (l % 2) * half
    rows = pl.ds(pl.multiple_of(b * TOK, 8), TOK)
    low, high = wire_s[k, l, rows, :], wire_s[k, z.l + l // 2, rows, :]
    return jnp.concatenate([low, high[:, at : at + half]], axis=1)


def store_wire_levels(z, wire_s, b, level):
    for k in range(z.lev):
        parts = lane_parts(z, [level(k * z.l + l) for l in range(z.l)])
        for j, part in enumerate(parts):
            wire_s[k, j, pl.ds(pl.multiple_of(b * TOK, 8), TOK), :] = part


def flush_wire(z, wire_s, refs):
    if z.ro > z.nb * TOK:
        wire_s[:, :, z.nb * TOK :, :] = jnp.zeros_like(wire_s[:, :, z.nb * TOK :, :])
    for k in range(z.lev):
        refs[k][0] = wire_s[k].astype(BF16)


def bf16_rows(z, ref):
    return ref[...].reshape(z.n, ref.shape[-1]).astype(BF16)


def put_rows(z, ref, values):
    ref[...] = values.reshape(z.lt, TOK, values.shape[-1])


def some_rows(z, ref, i):
    rows = ref[i * CHUNK : (i + 1) * CHUNK]
    return rows.reshape(CHUNK * TOK, ref.shape[-1]).astype(BF16)


def tile(j, t):
    return slice((2 * j + t) * LANES, (2 * j + t + 1) * LANES)


def put(ref, at, value):
    ref[at] = value


def group(g):
    return slice(g * GROUP, (g + 1) * GROUP)


def attention(n, qkv, bias, probs_at, store, ones, factor):
    def first(i):
        return [
            (score(qkv(i, 0, t), qkv(i, 1, t), ones) * factor + bias(t), qkv(i, 2, t)) for t in range(2)
        ]

    def second(i, got):
        return [(soften(scores), v) for scores, v in got]

    def third(i, got):
        outs = [mix(probs, v, ones) for probs, v in got]
        for t in range(2):
            probs_at(i, t)[...] = got[t][0]
            store(i, t, outs[t])

    pipelined(n, first, second, third)


def attention_back(n, qkv, grad, probs_at, store, ones, scales, scale):
    def first(i):
        out = []
        for t in range(2):
            q, k, v = (qkv(i, j, t) for j in range(3))
            g_rows = spread(grad(i, t), ones)
            out.append(
                (probs_at(i, t)[...], nt(v.astype(BF16), g_rows), g_rows, spread(q, ones), k.astype(BF16))
            )
        return out

    def second(i, got):
        return [(item[0], grad_scores_of(item[0], item[1])) + item[2:] for item in got]

    def third(i, got):
        outs = []
        for probs, grad_scores, g_rows, q_rows, k in got:
            outs.append(
                (
                    gather_heads(tn(grad_scores, k), scales),
                    nn(grad_scores, q_rows) * scale,
                    nn(probs, g_rows),
                    grad_scores,
                )
            )
        for t in range(2):
            store(i, t, outs[t])

    pipelined(n, first, second, third)


def score_factor(z):
    return np.float32((z.d // z.heads) ** (-0.5) * np.log2(np.e))


def forward_kernel(z, *refs):
    it = iter(refs)
    take = lambda n: [next(it) for _ in range(n)]
    wire_in = take(z.lev)
    offsets, sizes, bias_ref, column_mask = take(4)
    gain1, shift1, gain2, shift2, gain3, shift3 = take(6)
    w_qkv1, wo1, w_qkv2, wo2, w_up, w_down_t = take(6)
    wire_out = take(z.lev)
    norm1_ref, norm2_ref, norm3_ref, att_ref, co_ref, act_ref, slope_ref, probs_ref, probs2_ref = take(9)
    wire_s, x_s, n_s, o_s, a_s, qkv_s, bias_s = take(7)
    ones = head_masks(z)
    b = pl.program_id(1)

    @pl.when(b == 0)
    def _():
        load_wire(z, wire_in, wire_s)

    s = pl.program_id(0)
    token = lax.broadcasted_iota(jnp.int32, (TOK, 1), 0)
    cell = (token * 43) >> 8
    row = token - cell * WLAT + (lax.axis_index("lev") * z.nb + b) * WLAT
    cell = cell + (lax.axis_index("lon") * z.cells + offsets[s])
    cell = jnp.where(cell >= z.cells * z.lon, cell - z.cells * z.lon, cell)
    valid = (row < sizes[s, 0]) & (cell < sizes[s, 1])
    bias_s[...] = bias_ref[0] + jnp.where(valid, 0.0, NEGATIVE)

    def keep(ref, gain, shift):
        def store(lv, values, normed, rstd):
            x_s[lv] = values
            n_s[lv] = normed * gain[...] + shift[...]
            room = jnp.broadcast_to(rstd, (TOK, 2 * LANES - z.d))
            ref[0, 0, lv] = jnp.concatenate([normed, room], axis=1)

        return store

    norm_levels(
        z.lt, lambda lv: wire_level(z, wire_s, lv // z.l, lv % z.l, b), keep(norm1_ref, gain1, shift1)
    )
    put_rows(z, qkv_s, nn(bf16_rows(z, n_s), w_qkv1[...]))

    attention(
        z.lt,
        lambda lv, j, t: qkv_s[lv, :, tile(j, t)],
        lambda t: bias_s[t],
        lambda lv, t: probs_ref.at[0, 0, lv, t],
        lambda lv, t, out: put(a_s, (lv, slice(None), tile(0, t)), out),
        ones,
        score_factor(z),
    )
    att = bf16_rows(z, a_s)
    att_ref[0, 0] = att
    put_rows(z, o_s, nn(att, wo1[...]))

    norm_levels(z.lt, lambda lv: x_s[lv] + o_s[lv], keep(norm2_ref, gain2, shift2))
    put_rows(z, qkv_s, nn(bf16_rows(z, n_s), w_qkv2[...]))

    attention(
        TOK // GROUP,
        lambda g, j, t: qkv_s[:, group(g), tile(j, t)].reshape(z.lt * GROUP, LANES),
        lambda t: column_mask[...],
        lambda g, t: probs2_ref.at[0, 0, g, t],
        lambda g, t, out: put(a_s, (slice(None), group(g), tile(0, t)), out.reshape(z.lt, GROUP, LANES)),
        ones,
        score_factor(z),
    )
    co = bf16_rows(z, a_s)
    co_ref[0, 0] = co
    put_rows(z, o_s, nn(co, wo2[...]))

    norm_levels(z.lt, lambda lv: x_s[lv] + o_s[lv], keep(norm3_ref, gain3, shift3))

    def up(i):
        return nn(some_rows(z, n_s, i), w_up[...])

    def gelu(i, hidden):
        share = 0.5 + 0.5 * lax.erf(hidden * (0.5**0.5))
        density = jnp.exp(hidden * hidden * -0.5) * ((2.0 * np.pi) ** -0.5)
        return (hidden * share).astype(BF16), (share + hidden * density).astype(BF16)

    def down(i, got):
        act, slope = got
        out = nt(act, w_down_t[...])
        rows = slice(i * CHUNK * TOK, (i + 1) * CHUNK * TOK)
        act_ref[0, 0, rows], slope_ref[0, 0, rows] = act, slope
        o_s[i * CHUNK : (i + 1) * CHUNK] = out.reshape(CHUNK, TOK, z.d)

    pipelined(z.lt // CHUNK, up, gelu, down)

    store_wire_levels(z, wire_s, b, lambda lv: x_s[lv] + o_s[lv])

    @pl.when(b == z.nb - 1)
    def _():
        flush_wire(z, wire_s, wire_out)


def wire_specs(z):
    return [pl.BlockSpec((1, z.nblk, z.ro, LANES), lambda s, b: (s, 0, 0, 0))] * z.lev


def wire_shapes(z):
    return [jax.ShapeDtypeStruct((z.s, z.nblk, z.ro, LANES), BF16)] * z.lev


def unit_spec(shape):
    return pl.BlockSpec((1, 1) + shape, lambda s, b: (s, b) + (0,) * len(shape))


def whole_spec(array):
    return pl.BlockSpec(array.shape, lambda s, b: (0,) * array.ndim)


def residual_shapes(z):
    return [
        ((z.lt, TOK, 2 * LANES), F32),
        ((z.lt, TOK, 2 * LANES), F32),
        ((z.lt, TOK, 2 * LANES), F32),
        ((z.n, 2 * LANES), BF16),
        ((z.n, 2 * LANES), BF16),
        ((z.n, z.ff), BF16),
        ((z.n, z.ff), BF16),
        ((z.lt, 2, TOK, z.heads // 2 * TOK), BF16),
        ((TOK // GROUP, 2, z.lt * GROUP, z.heads // 2 * z.lt * GROUP), BF16),
    ]


def forward(z, wire, offsets, sizes, bias, column_mask, norms, weights):
    res = residual_shapes(z)
    rows3 = (z.lt, TOK, z.d)
    out = pl.pallas_call(
        functools.partial(forward_kernel, z),
        grid=(z.s, z.nb),
        in_specs=wire_specs(z)
        + [
            *in_smem(2),
            pl.BlockSpec((1, 2, TOK, z.heads // 2 * TOK), lambda s, b: (b, 0, 0, 0)),
            whole_spec(column_mask),
        ]
        + [whole_spec(a) for a in norms]
        + [whole_spec(a) for a in weights],
        out_specs=wire_specs(z) + [unit_spec(shape) for shape, _ in res],
        out_shape=wire_shapes(z) + [jax.ShapeDtypeStruct((z.s, z.nb) + shape, t) for shape, t in res],
        scratch_shapes=[pltpu.VMEM((z.lev, z.nblk, z.ro, LANES), F32)]
        + [pltpu.VMEM(rows3, F32)] * 3
        + [
            pltpu.VMEM((z.lt, TOK, 2 * LANES), F32),
            pltpu.VMEM((z.lt, TOK, 6 * LANES), F32),
            pltpu.VMEM((2, TOK, z.heads // 2 * TOK), F32),
        ],
        compiler_params=pltpu.CompilerParams(vmem_limit_bytes=60 * 2**20),
        cost_estimate=cost(30),
        name="forward",
    )(*wire, offsets, sizes, bias, column_mask, *norms, *weights)
    return out[: z.lev], out[z.lev :]


def grad_list(z):
    return [
        ("up", z.ff), ("down_t", z.ff),
        ("qkv1", 3 * z.d), ("qkv2", 3 * z.d),
        ("o1", z.d), ("o2", z.d),
    ]


def half_blocks(z):
    full, rest = [], []
    for name, columns in grad_list(z):
        for row in range(0, z.d, 96):
            for col in range(0, columns, LANES):
                width = min(LANES, columns - col)
                (full if width == LANES else rest).append((name, row, col, width))
    out = [[piece + (0,)] for piece in full]
    for i in range(0, len(rest), 2):
        out.append([rest[i] + (0,), rest[i + 1] + (rest[i][3],)])
    return out


def grad_buffer(z, name, columns):
    if name[:3] == "qkv":
        return (z.d, 6 * LANES)
    if name[0] == "o":
        return (2 * LANES, columns)
    return (z.d, columns)


def grad_block(z, name, ref, row, col, width):
    half = z.d // 2
    if name[0] == "o":
        start = row // half * LANES
        return ref[start : start + 96, col : col + width]
    if name[:3] != "qkv":
        return ref[row : row + 96, col : col + width]
    pieces = []
    while width:
        t, lane = col // half, col % half
        count = min(width, half - lane)
        pieces.append(ref[row : row + 96, t * LANES + lane : t * LANES + lane + count])
        col, width = col + count, width - count
    return pieces[0] if len(pieces) == 1 else jnp.concatenate(pieces, axis=1)


def bias_rows(z):
    pick = np.zeros((WLON * 8, TOK), np.float32)
    for a in range(WLON):
        for i in range(WLAT):
            pick[a * 8 + i, a * WLAT + i] = 1.0
    return pick


def backward_kernel(z, *refs):
    it = iter(refs)
    take = lambda n: [next(it) for _ in range(n)]
    wire_in = take(z.lev)
    norm1_ref, norm2_ref, norm3_ref, att_ref, co_ref, act_ref, slope_ref, probs_ref, probs2_ref = take(9)
    (pick_ref,) = take(1)
    gain1, shift1, gain2, shift2, gain3, shift3 = take(6)
    w_qkv1, wo1, w_qkv2, wo2, w_up, w_down_t = take(6)
    wire_out = take(z.lev)
    late_ref, mine_ref, other_ref = take(3)
    wire_s, late_s, g_s, o_s, a_s, qkv_s, grad_s, gh_s, db_s, vec_s, sums_s = take(11)
    grads = {name: ref for (name, _), ref in zip(grad_list(z), take(len(grad_list(z))))}
    scale = np.float32((z.d // z.heads) ** (-0.5))
    ones, scales = head_masks(z), head_masks(z, scale)
    s, b = pl.program_id(0), pl.program_id(1)

    @pl.when((s == 0) & (b == 0))
    def _():
        for ref in list(grads.values()) + [db_s, vec_s]:
            ref[...] = jnp.zeros_like(ref)

    @pl.when(b == 0)
    def _():
        load_wire(z, wire_in, wire_s)

    for k in range(z.lev):
        got = [wire_level(z, wire_s, k, l, b) for l in range(z.l)]
        for l in range(z.l):
            g_s[k * z.l + l] = got[l]

    def normed_tokens(ref, gain, shift):
        normed = ref[0, 0][:, :, : z.d] * gain[...] + shift[...]
        return normed.reshape(z.n, z.d).astype(BF16)

    def back_down(i):
        rows = slice(i * CHUNK * TOK, (i + 1) * CHUNK * TOK)
        return nn(some_rows(z, g_s, i), w_down_t[...]), slope_ref[0, 0, rows, :].astype(F32)

    def back_gelu(i, got):
        return (got[0] * got[1]).astype(BF16)

    def back_up(i, grad):
        out = nt(grad, w_up[...])
        gh_s[i * CHUNK * TOK : (i + 1) * CHUNK * TOK] = grad
        o_s[i * CHUNK : (i + 1) * CHUNK] = out.reshape(CHUNK, TOK, z.d)

    pipelined(z.lt // CHUNK, back_down, back_gelu, back_up)
    grads["down_t"][...] += tn(bf16_rows(z, g_s), act_ref[0, 0])
    grads["up"][...] += tn(normed_tokens(norm3_ref, gain3, shift3), gh_s[...])

    def norm_step(ref, gain, at, target):
        sums = [vec_s[at], vec_s[at + 1]]

        def first(lv):
            grad, normed, rstd = o_s[lv], ref[0, 0, lv, :, : z.d], ref[0, 0, lv, :, z.d : z.d + 1]
            sums[0] += fold_rows(grad * normed)
            sums[1] += fold_rows(grad)
            return target[lv], normed, rstd, grad * gain[...]

        def second(lv, got):
            old, normed, rstd, gained = got
            one = jnp.mean(gained, axis=-1, keepdims=True)
            two = jnp.mean(gained * normed, axis=-1, keepdims=True)
            return old, normed, rstd, gained, one, two

        def third(lv, got):
            old, normed, rstd, gained, one, two = got
            target[lv] = old + rstd * (gained - one - normed * two)

        pipelined(z.lt, first, second, third)
        vec_s[at], vec_s[at + 1] = sums

    norm_step(norm3_ref, gain3, 4, g_s)

    branch = bf16_rows(z, g_s)
    grads["o2"][...] += tn(co_ref[0, 0], branch)
    put_rows(z, a_s, nt(branch, wo2[...]))
    tokens = normed_tokens(norm2_ref, gain2, shift2)
    put_rows(z, qkv_s, nn(tokens, w_qkv2[...]))

    def keep_column(g, t, got):
        for j in range(3):
            grad_s[:, group(g), tile(j, t)] = got[j].reshape(z.lt, GROUP, LANES)

    attention_back(
        TOK // GROUP,
        lambda g, j, t: qkv_s[:, group(g), tile(j, t)].reshape(z.lt * GROUP, LANES),
        lambda g, t: a_s[:, group(g), tile(0, t)].reshape(z.lt * GROUP, LANES),
        lambda g, t: probs2_ref.at[0, 0, g, t],
        keep_column,
        ones,
        scales,
        scale,
    )

    def project_back(tokens, name, w):
        grad = bf16_rows(z, grad_s)
        grads[name][...] += tn(tokens, grad)
        put_rows(z, o_s, nt(grad, w[...]))

    project_back(tokens, "qkv2", w_qkv2)
    norm_step(norm2_ref, gain2, 2, g_s)

    branch = bf16_rows(z, g_s)
    grads["o1"][...] += tn(att_ref[0, 0], branch)
    put_rows(z, a_s, nt(branch, wo1[...]))
    tokens = normed_tokens(norm1_ref, gain1, shift1)
    put_rows(z, qkv_s, nn(tokens, w_qkv1[...]))

    def keep_window(lv, t, got):
        for j in range(3):
            grad_s[lv, :, tile(j, t)] = got[j]
        db_s[b, t] += got[3].astype(F32)

    attention_back(
        z.lt,
        lambda lv, j, t: qkv_s[lv, :, tile(j, t)],
        lambda lv, t: a_s[lv, :, tile(0, t)],
        lambda lv, t: probs_ref.at[0, 0, lv, t],
        keep_window,
        ones,
        scales,
        scale,
    )
    project_back(tokens, "qkv1", w_qkv1)
    norm_step(norm1_ref, gain1, 0, g_s)

    store_wire_levels(z, wire_s, b, lambda lv: g_s[lv])

    @pl.when(b == z.nb - 1)
    def _():
        flush_wire(z, wire_s, wire_out)
        for band in range(z.nb):
            rows = wire_s[:, :, band * TOK + HALO0 : (band + 1) * TOK, :]
            late_s[:, :, band * HALO : (band + 1) * HALO, :] = rows
        late_ref[:, 0] = late_s[...].astype(BF16)

    @pl.when((s == z.s - 1) & (b == z.nb - 1))
    def _():
        p, core = lax.axis_index("lev"), lax.axis_index("lon") % 2

        def place(i):
            return ((i // z.lev) ^ core) * z.lev + ((i % z.lev) ^ p)

        for at, pieces in enumerate(half_blocks(z)):
            values = [grad_block(z, n, grads[n], r, c, width) for n, r, c, width, _ in pieces]
            block = values[0] if len(values) == 1 else jnp.concatenate(values, axis=1)
            start = (at % z.hb) * 96
            sums_s[place(at // z.hb), start : start + 96, :] = block.astype(BF16)
        extra = z.hb * 96
        sums_s[:, extra:, :] = jnp.zeros_like(sums_s[:, extra:, :])
        vectors = [jnp.sum(vec_s[i], axis=0, keepdims=True) for i in range(6)]
        vectors = jnp.concatenate(vectors + [jnp.zeros((UNIT - 6, z.d), F32)], axis=0)
        vectors = jnp.concatenate([vectors, jnp.zeros((UNIT, 2 * LANES - z.d), F32)], axis=1)

        def put_unit(u, value):
            start = extra + (u % z.upp) * UNIT
            if not isinstance(u, int):
                start = pl.multiple_of(start, UNIT)
            sums_s[place(u // z.upp), pl.ds(start, UNIT), :] = value.astype(BF16)

        for j in range(2):
            put_unit(z.bands * 4 + j, vectors[:, j * LANES : (j + 1) * LANES])
        lane = lax.broadcasted_iota(jnp.int32, (1, z.heads * TOK), 1)
        odd = jnp.zeros(lane.shape, jnp.bool_)
        for h in range(1, z.heads, 2):
            odd = odd | ((lane >= h * TOK) & (lane < (h + 1) * TOK))
        width = -(-(z.heads * TOK) // LANES) * LANES
        for band in range(z.nb):
            rows = [nn(pick_ref[...], db_s[band, t], precision=lax.Precision.HIGHEST) for t in range(2)]
            rows = jnp.concatenate(rows, axis=1)
            halves = []
            for parity in range(2):
                kept = jnp.where(odd if parity else ~odd, rows, 0.0)
                kept = jnp.concatenate(
                    [kept, jnp.zeros((rows.shape[0], width - z.heads * TOK), F32)], axis=1
                )
                total = None
                for a in range(WLON):
                    part = kept[a * 8 : (a + 1) * 8]
                    shift = (WLON - 1 - a) * WLAT
                    if shift:
                        part = pltpu.roll(part, shift, 1)
                    total = part if total is None else total + part
                halves.append(total)
            both = jnp.concatenate(halves, axis=0)
            for j in range(4):
                put_unit((p * z.nb + band) * 4 + j, both[:, j * LANES : (j + 1) * LANES])
        mine_ref[...] = sums_s[: z.lev]
        other_ref[...] = sums_s[z.lev :]


def backward(z, wire, residuals, norms, weights):
    res = residual_shapes(z)
    rows3 = (z.lt, TOK, z.d)
    pick = jnp.asarray(bias_rows(z))
    half = (z.lev, z.pr, LANES)
    out = pl.pallas_call(
        functools.partial(backward_kernel, z),
        **dict(
            grid=(z.s, z.nb),
            in_specs=[
                spec
                for spec in wire_specs(z)
                + [unit_spec(shape) for shape, _ in res]
                + [whole_spec(pick)]
                + [whole_spec(a) for a in norms]
                + [whole_spec(a) for a in weights]
            ],
            out_specs=[spec for spec in wire_specs(z)]
            + [pl.BlockSpec((z.lev, 1, z.nblk, z.rh, LANES), lambda s, b: (0, s, 0, 0, 0))]
            + [pl.BlockSpec(half, lambda s, b: (0, 0, 0))] * 2,
            scratch_shapes=[
                pltpu.VMEM((z.lev, z.nblk, z.ro, LANES), F32),
                pltpu.VMEM((z.lev, z.nblk, z.rh, LANES), F32),
            ]
            + [pltpu.VMEM(rows3, F32)] * 2
            + [
                pltpu.VMEM((z.lt, TOK, 2 * LANES), F32),
                pltpu.VMEM((z.lt, TOK, 6 * LANES), F32),
                pltpu.VMEM((z.lt, TOK, 6 * LANES), F32),
                pltpu.VMEM((z.n, z.ff), BF16),
                pltpu.VMEM((z.nb, 2, TOK, z.heads // 2 * TOK), F32),
                pltpu.VMEM((6, 8, z.d), F32),
                pltpu.VMEM((z.np, z.pr, LANES), BF16),
            ]
            + [pltpu.VMEM(grad_buffer(z, *item), F32) for item in grad_list(z)],
        ),
        out_shape=wire_shapes(z)
        + [jax.ShapeDtypeStruct((z.lev, z.s, z.nblk, z.rh, LANES), BF16)]
        + [jax.ShapeDtypeStruct(half, BF16)] * 2,
        compiler_params=pltpu.CompilerParams(vmem_limit_bytes=62 * 2**20),
        cost_estimate=cost(40),
        name="backward",
    )(*wire, *residuals, pick, *norms, *weights)
    return out[: z.lev], out[z.lev], out[z.lev + 1], out[z.lev + 2]


def tree(parts):
    while len(parts) > 1:
        parts = [parts[i] + parts[i + 1] for i in range(0, len(parts), 2)]
    return parts[0]


def lev_swap(z, array, k):
    return lax.ppermute(array, "lev", [(i, i ^ k) for i in range(z.lev)])


def lon_swap(z, array, k):
    return lax.ppermute(array, "lon", [(i, i ^ k) for i in range(z.lon)])


def merge_kernel(z, offsets, *refs):
    wire, late_ref, outs = refs[: z.lev], refs[z.lev], refs[z.lev + 1 :]
    row = lax.broadcasted_iota(jnp.int32, (HALO, LANES), 0) + HALO0
    for s in range(z.s):
        moved = row >= (z.cells - offsets[s]) * WLAT
        for k in range(z.lev):
            for j in range(z.nblk):
                rows, late = wire[k][s, j].astype(F32), late_ref[k, s, j].astype(F32)
                parts = []
                for b in range(z.nb):
                    own = rows[b * TOK : (b + 1) * TOK]
                    got = late[b * HALO : (b + 1) * HALO]
                    parts += [own[:HALO0], jnp.where(moved, got, own[HALO0:])]
                if z.ro > z.nb * TOK:
                    parts.append(rows[z.nb * TOK :])
                outs[k][s, j] = jnp.concatenate(parts, axis=0).astype(BF16)


def merge_cells(z, wire, late, offsets):
    return pl.pallas_call(
        functools.partial(merge_kernel, z),
        in_specs=in_smem(1) + in_vmem(z.lev + 1),
        out_specs=in_vmem(z.lev),
        out_shape=[jax.ShapeDtypeStruct((z.s, z.nblk, z.ro, LANES), BF16)] * z.lev,
        compiler_params=pltpu.CompilerParams(vmem_limit_bytes=40 * 2**20),
        cost_estimate=cost(3),
        name="merge",
    )(offsets, *wire, late)


def tie(values, *others):
    return lax.optimization_barrier((values,) + others)[0]


def sum_cores(z, mine, other):
    got = lon_swap(z, other, 1)
    return [(mine[k].astype(F32) + got[k].astype(F32)).astype(BF16) for k in range(z.lev)]


def sum_levels(z, half):
    parts = [half[0]] + [lev_swap(z, half[k], k) for k in range(1, z.lev)]
    return tree([v.astype(F32) for v in parts]).astype(BF16)


def sum_slabs(z, quarter):
    parts = [quarter] + [lon_swap(z, quarter, 2 * k) for k in range(1, z.lon // 2)]
    return tree([v.astype(F32) for v in parts]).astype(BF16)


def share_levels(z, done):
    return [done] + [lev_swap(z, done, k) for k in range(1, z.lev)]


def table_lanes(z, h):
    lanes = np.full((WLAT, 32), -1, np.int32)
    for i in range(WLAT):
        lanes[i, : 2 * WLON - 1] = h * TOK + np.arange(2 * WLON - 1) * WLAT + i
    return lanes.reshape(1, WLAT * 32)


def finish_kernel(z, lanes, order, own, other, *outs):
    p, core = lax.axis_index("lev"), lax.axis_index("lon") % 2
    named = {name: ref for (name, _), ref in zip(grad_list(z), outs)}
    vec_refs, bias_ref = outs[len(named) : len(named) + 6], outs[len(named) + 6]

    def read(piece, start, size):
        half, j = piece // z.lev, piece % z.lev
        rows = slice(start, start + size)
        return jnp.where(core == half, own[p ^ j, rows, :], other[p ^ j, rows, :])

    for at, pieces in enumerate(half_blocks(z)):
        block = read(at // z.hb, (at % z.hb) * 96, 96).astype(F32)
        for n, r, c, width, lane in pieces:
            named[n][r : r + 96, c : c + width] = block[:, lane : lane + width]
    extra = z.hb * 96
    units = [read(u // z.upp, extra + (u % z.upp) * UNIT, UNIT) for u in range(z.units)]
    vectors = jnp.concatenate(units[z.bands * 4 :], axis=1).astype(F32)
    for i in range(6):
        vec_refs[i][...] = vectors[i : i + 1, : z.d]
    table = [jnp.concatenate(units[4 * k : 4 * k + 4], axis=1) for k in range(z.bands)]
    table = nn(order[...], jnp.concatenate(table, axis=0)).astype(BF16)
    half = table.shape[0] // 2
    for h in range(z.heads):
        at = lax.broadcasted_iota(jnp.int32, (4 * LANES, WLAT * 32), 0)
        pick = jnp.where(at == lanes[h : h + 1, :], 1.0, 0.0).astype(BF16)
        rows = table[(h % 2) * half : (h % 2) * half + half]
        got = nn(rows, pick)
        for i in range(WLAT):
            values = got[: WLAT * z.bands, i * 32 : i * 32 + 2 * WLON - 1]
            bias_ref[h, i] = values.reshape(WLAT, z.bands, 2 * WLON - 1)


def finish(z, own, other):
    shapes = [jax.ShapeDtypeStruct((z.d, columns), F32) for _, columns in grad_list(z)]
    shapes += [jax.ShapeDtypeStruct((1, z.d), F32)] * 6
    shapes += [jax.ShapeDtypeStruct((z.heads, WLAT, WLAT, z.bands, 2 * WLON - 1), F32)]
    lanes = jnp.asarray(np.concatenate([table_lanes(z, h) for h in range(z.heads)]))
    order = np.zeros((2 * 8 * z.bands, z.bands * UNIT), np.float32)
    for parity in range(2):
        for i in range(8):
            for k in range(z.bands):
                order[parity * 8 * z.bands + i * z.bands + k, k * UNIT + parity * 8 + i] = 1.0
    order = jnp.asarray(order, BF16)
    out = pl.pallas_call(
        functools.partial(finish_kernel, z),
        in_specs=in_vmem(4),
        out_specs=in_vmem(len(shapes)),
        out_shape=shapes,
        compiler_params=pltpu.CompilerParams(vmem_limit_bytes=40 * 2**20),
        cost_estimate=cost(4),
        name="finish",
    )(lanes, order, own, other)
    named = {name: value for (name, _), value in zip(grad_list(z), out)}
    vectors = [v.reshape(z.d) for v in out[len(named) : len(named) + 6]]
    return named, vectors, out[-1].transpose(3, 0, 1, 2, 4)


def bias_kernel(z, table_ref, pick_ref, qkv1, out1, qkv2, out2, out_ref, *rest):
    even_s, odd_s = rest[4:]
    side = z.d // 2
    for source, target in ((qkv1, rest[0]), (qkv2, rest[2])):
        room = jnp.zeros((z.d, LANES - side), BF16)
        for t in range(6):
            part = source[:, t * side : (t + 1) * side]
            target[:, t * LANES : (t + 1) * LANES] = jnp.concatenate([part, room], axis=1)
    for source, target in ((out1, rest[1]), (out2, rest[3])):
        for t in range(2):
            target[t * LANES : t * LANES + side] = source[t * side : (t + 1) * side]
            target[t * LANES + side : (t + 1) * LANES] = jnp.zeros((LANES - side, z.d), BF16)
    width = 4 * LANES
    lane = lax.broadcasted_iota(jnp.int32, (2 * WLON - 1, width), 1)
    step = lax.broadcasted_iota(jnp.int32, (2 * WLON - 1, width), 0) * WLAT
    for parity, ref in ((0, even_s), (1, odd_s)):
        total = None
        for h in range(parity, z.heads, 2):
            for i in range(WLAT):
                place = jnp.where(lane == step + (h * TOK + i), 1.0, 0.0).astype(BF16)
                values = table_ref[h, i]
                high = values.astype(BF16)
                low = (values - high.astype(F32)).astype(BF16)
                part = nn(jnp.concatenate([high, low], axis=0), place)
                total = part if total is None else total + part
        rows = z.nb * 8
        ref[...] = total[:rows] + total[rows:]
    head = lax.broadcasted_iota(jnp.int32, (1, width), 1)
    odd = jnp.zeros(head.shape, jnp.bool_)
    for h in range(1, z.heads, 2):
        odd = odd | ((head >= h * TOK) & (head < (h + 1) * TOK))
    side = z.heads // 2 * TOK
    for b in range(z.nb):
        even, uneven = even_s[b * 8 : (b + 1) * 8], odd_s[b * 8 : (b + 1) * 8]
        rows = []
        for a in range(WLON):
            shift = (width - (WLON - 1 - a) * WLAT) % width
            turned = [pltpu.roll(v, shift, 1) if shift else v for v in (even, uneven)]
            rows.append(jnp.where(odd, turned[1], turned[0]))
        rows = jnp.concatenate(rows, axis=0)
        full = lax.dot_general(
            pick_ref[...], rows, (((0,), (0,)), ((), ())),
            precision=lax.Precision.HIGHEST, preferred_element_type=F32,
        ) * np.float32(np.log2(np.e))
        out_ref[b, 0] = full[:, :side]
        out_ref[b, 1] = full[:, side : 2 * side]


def bias_of(z, bias_table, p, weights):
    table = lax.dynamic_slice_in_dim(bias_table, p * z.nb, z.nb, axis=0)
    table = jnp.pad(table.transpose(1, 2, 0, 3, 4), ((0, 0),) * 3 + ((0, 2), (0, 0)))
    table = table.reshape(z.heads, WLAT, z.nb * 8, 2 * WLON - 1)
    wide = jax.ShapeDtypeStruct((z.d, 6 * LANES), BF16)
    tall = jax.ShapeDtypeStruct((2 * LANES, z.d), BF16)
    bias = jax.ShapeDtypeStruct((z.nb, 2, TOK, z.heads // 2 * TOK), F32)
    out = pl.pallas_call(
        functools.partial(bias_kernel, z),
        out_shape=[bias, wide, tall, wide, tall],
        scratch_shapes=[pltpu.VMEM((z.nb * 8, 4 * LANES), F32)] * 2,
        compiler_params=pltpu.CompilerParams(vmem_limit_bytes=40 * 2**20),
        cost_estimate=cost(4),
        name="bias",
    )(table, jnp.asarray(bias_rows(z)), *weights)
    return out[0], list(out[1:])


def lev_exchange(z, wire):
    return [wire[0]] + [lev_swap(z, wire[k], k) for k in range(1, z.lev)]


def lon_shift(z, array, distance):
    return lax.ppermute(array, "lon", [(w, (w + distance) % z.lon) for w in range(z.lon)])


def last_cells(z, wire):
    rows = [a[:, :, : z.nb * TOK].reshape(z.s, z.nblk, z.nb, TOK, LANES)[:, :, :, HALO0:] for a in wire]
    return jnp.stack(rows).reshape(z.lev, z.s, z.nblk, z.rh, LANES)


def on_device(
    inputs, cotangent, grid_sizes, offsets, gain_one, shift_one, qkv_window, out_window, bias_table,
    gain_two, shift_two, qkv_column, out_column, gain_three, shift_three, w_up, w_down,
):
    d = inputs.shape[-1]
    z = Sizes(lax.axis_size("lev"), lax.axis_size("lon"), inputs.shape, bias_table.shape[1], w_up.shape[1])
    p = lax.axis_index("lev")
    swap = lambda a: a.transpose(0, 1, 3, 2, 4)

    half = WLON // 2
    x, c = swap(inputs), swap(cotangent)
    halo_x = lon_shift(z, x[:, :, :half], -1)
    raw = (qkv_window, out_window, qkv_column, out_column)
    bias, weights = bias_of(z, bias_table, p, raw)
    weights = weights + [w_up, w_down.T]
    halo_x, bias = lax.optimization_barrier((halo_x, bias))
    halo_c = lon_shift(z, tie(c[:, :, :half], halo_x), -1)
    wire_x = pack(z, x, halo_x, offsets)
    halo_c = tie(halo_c, *wire_x)
    wire_x = lev_exchange(z, wire_x)
    wire_c = lev_exchange(z, pack(z, c, halo_c, offsets))
    of_key = np.arange(z.lt * GROUP) % GROUP
    of_query = np.tile(of_key, z.heads // 2)
    column_mask = jnp.asarray(
        np.where(of_key[:, None] == of_query[None, :], 0.0, NEGATIVE).astype(np.float32)
    )

    norms = [v[None] for v in (gain_one, shift_one, gain_two, shift_two, gain_three, shift_three)]
    wire_r, residuals = forward(z, wire_x, offsets, grid_sizes, bias, column_mask, norms, weights)
    wire_r = lev_exchange(z, wire_r)
    grads = backward(z, wire_c, residuals, norms, weights)
    (wire_g, late, mine, other), wire_r = lax.optimization_barrier((grads, wire_r))
    halo_r = lon_shift(z, last_cells(z, wire_r), 1)
    late = lon_shift(z, late, 1)
    sums = sum_cores(z, mine, other)
    sums = sum_levels(z, sums)
    wire_g = lev_exchange(z, merge_cells(z, wire_g, late, offsets))
    result = unpack(z, wire_r, halo_r, offsets)
    sums = sum_slabs(z, tie(sums, halo_r, late))
    sums = share_levels(z, tie(sums, result))
    input_grad = unpack(z, wire_g, None, offsets)
    own = jnp.stack(tie(sums, input_grad))
    other = lon_swap(z, own, 1)
    named, vec, table = finish(z, own, other)
    return (
        swap(result), swap(input_grad),
        vec[0], vec[1], named["qkv1"], named["o1"], table,
        vec[2], vec[3], named["qkv2"], named["o2"],
        vec[4], vec[5], named["up"], named["down_t"].T,
    )


def solution(mesh):
    tokens = P(None, "lev", None, "lon", None)
    return jax.shard_map(
        on_device,
        mesh=mesh,
        in_specs=(tokens, tokens) + (P(),) * 15,
        out_specs=(tokens, tokens) + (P(),) * 13,
        check_vma=False,
    )
```

```python
import functools

import jax
import jax.numpy as jnp
import numpy as np
from jax import lax
from jax.experimental import pallas as pl
from jax.experimental.pallas import tpu as pltpu
from jax.sharding import PartitionSpec as P

WLAT = 6
WLON = 12
TOK = WLAT * WLON
HALF = TOK // 2
HALO0 = 32
HALO = TOK - HALO0
GROUP = 8
CHUNK = 2
STOP = object()
LAG_F = 0
LAG_B = 0
EPSILON = 1e-05
NEGATIVE = -1000000000.0
F32 = jnp.float32
BF16 = jnp.bfloat16
LANES = 128
UNIT = 16


def up16(n):
    return (n + 15) // 16 * 16


def nn(a, b, **kw):
    return lax.dot_general(a, b, (((1,), (0,)), ((), ())), preferred_element_type=F32, **kw)


def nt(a, b):
    return lax.dot_general(a, b, (((1,), (1,)), ((), ())), preferred_element_type=F32)


def tn(a, b):
    return lax.dot_general(a, b, (((0,), (0,)), ((), ())), preferred_element_type=F32)


class Sizes:
    def __init__(self, lev, lon, shape, heads, hidden):
        self.lev, self.lon = lev, lon
        self.s, self.l, self.rows, self.cells, self.d = shape
        self.heads, self.ff = heads, hidden
        self.bands = self.rows // WLAT
        self.nb = self.bands // lev
        self.lt = self.l * lev
        self.n = self.lt * TOK
        self.ro = up16(self.nb * TOK)
        self.rh = self.nb * HALO
        self.nblk = self.l + (self.l + 1) // 2
        self.tokens = self.cells * self.rows
        self.np = 2 * lev
        self.blocks = 2 * (2 * hidden // 2 + 3 * self.d + self.d) // LANES * (self.d // 96)
        self.hb = self.blocks // self.np
        self.units = self.bands * 4 + 2
        self.upp = -(-self.units // self.np)
        self.pr = self.hb * 96 + self.upp * UNIT


def slot_rows(z):
    own = np.full((z.ro,), -(10**6), np.int32)
    halo = np.full((z.rh,), -(10**6), np.int32)
    for b in range(z.nb):
        for t in range(TOK):
            own[b * TOK + t] = (t // WLAT) * z.rows + b * WLAT + t % WLAT
            if t >= HALF:
                halo[b * HALO + t - HALO0] = own[b * TOK + t] - z.tokens
    return own, halo


def lane_parts(z, levels):
    parts = [v[:, :LANES] for v in levels]
    high = [v[:, LANES:] for v in levels]
    if z.l % 2:
        high.append(jnp.zeros_like(high[0]))
    for l in range(0, len(high), 2):
        parts.append(jnp.concatenate([high[l], high[l + 1]], axis=1))
    return parts


def pack_kernel(z, offsets, base, x_ref, halo_ref, *rest):
    outs, onehot = rest[: z.lev], rest[z.lev]
    p = lax.axis_index("lev")
    rows = z.tokens + halo_ref.shape[2] * z.rows
    column = lax.broadcasted_iota(jnp.int32, (z.ro, rows), 1)
    for s in range(z.s):
        for k in range(z.lev):
            hit = column == base[...] + (offsets[s] * z.rows + (p ^ k) * (z.nb * WLAT))
            onehot[s, k * z.ro : (k + 1) * z.ro] = jnp.where(hit, 1.0, 0.0).astype(BF16)
        levels = []
        for l in range(z.l):
            cells = [r[s, l].reshape(r.shape[2] * z.rows, z.d) for r in (x_ref, halo_ref)]
            levels.append(jnp.concatenate(cells, axis=0))
        moved = nn(onehot[s], jnp.concatenate(lane_parts(z, levels), axis=1)).astype(BF16)
        for k in range(z.lev):
            for j in range(z.nblk):
                outs[k][s, j] = moved[k * z.ro : (k + 1) * z.ro, j * LANES : (j + 1) * LANES]


def in_vmem(count):
    return [pl.BlockSpec(memory_space=pltpu.VMEM)] * count


def in_smem(count):
    return [pl.BlockSpec(memory_space=pltpu.SMEM)] * count


def pack(z, x, halo, offsets):
    own, _ = slot_rows(z)
    rows = z.tokens + halo.shape[2] * z.rows
    return pl.pallas_call(
        functools.partial(pack_kernel, z),
        in_specs=in_smem(1) + in_vmem(3),
        out_specs=in_vmem(z.lev),
        scratch_shapes=[pltpu.VMEM((z.s, z.lev * z.ro, rows), BF16)],
        out_shape=[jax.ShapeDtypeStruct((z.s, z.nblk, z.ro, LANES), BF16)] * z.lev,
        compiler_params=pltpu.CompilerParams(vmem_limit_bytes=40 * 2**20),
        cost_estimate=cost(4),
        name="pack",
    )(offsets, jnp.asarray(own)[:, None], x, halo)


def unpack_kernel(z, merged, offsets, *rest):
    count = 1 if merged else 2
    bases, pieces = rest[:count], rest[count : count + z.lev]
    halo_ref, out_ref, onehot = rest[-3], rest[-2], rest[-1]
    p = lax.axis_index("lev")
    for s in range(z.s):
        at = 0
        for base, size in zip(bases, (z.ro, z.rh)):
            row = lax.broadcasted_iota(jnp.int32, (z.tokens, size), 0)
            for k in range(z.lev):
                place = base[...] + (offsets[s] * z.rows + (p ^ k) * (z.nb * WLAT))
                if merged:
                    place = jnp.where(place >= z.tokens, place - z.tokens, place)
                onehot[s, :, at : at + size] = jnp.where(row == place, 1.0, 0.0).astype(BF16)
                at += size
        columns = []
        for j in range(z.nblk):
            rows = [r[s, j] for r in pieces]
            if not merged:
                rows += [halo_ref[k, s, j] for k in range(z.lev)]
            columns.append(jnp.concatenate(rows, axis=0))
        moved = nn(onehot[s], jnp.concatenate(columns, axis=1))
        half = z.d - LANES
        for l in range(z.l):
            low = moved[:, l * LANES : (l + 1) * LANES]
            at = (z.l + l // 2) * LANES + (l % 2) * half
            tokens = jnp.concatenate([low, moved[:, at : at + half]], axis=1)
            out_ref[s, l] = tokens.reshape(z.cells, z.rows, z.d).astype(BF16)


def unpack(z, own, halo, offsets):
    merged = halo is None
    bases = [jnp.asarray(v)[None] for v in slot_rows(z)][: 1 if merged else 2]
    slots = z.ro if merged else z.ro + z.rh
    arrays = bases + list(own) + ([] if merged else [halo])
    return pl.pallas_call(
        functools.partial(unpack_kernel, z, merged),
        in_specs=in_smem(1) + in_vmem(len(arrays)),
        out_specs=pl.BlockSpec(memory_space=pltpu.VMEM),
        scratch_shapes=[pltpu.VMEM((z.s, z.tokens, z.lev * slots), BF16)],
        out_shape=jax.ShapeDtypeStruct((z.s, z.l, z.cells, z.rows, z.d), BF16),
        compiler_params=pltpu.CompilerParams(vmem_limit_bytes=40 * 2**20),
        cost_estimate=cost(4),
        name="unpack",
    )(offsets, *arrays)


def cost(microseconds):
    return pl.CostEstimate(
        flops=int(microseconds * 5e8), transcendentals=0, bytes_accessed=int(microseconds * 3e6)
    )


def loop(n, body, unroll=None):
    unroll = n if unroll is None else unroll

    def some(i, c):
        for j in range(unroll):
            body(i * unroll + j)
        return c

    if n == unroll:
        some(0, 0)
    else:
        lax.fori_loop(0, n // unroll, some, 0)


def head_masks(z, weight=1.0):
    lane = lax.broadcasted_iota(jnp.int32, (1, LANES), 1)
    size = z.d // z.heads
    inside = [(lane >= h * size) & (lane < (h + 1) * size) for h in range(z.heads // 2)]
    return [jnp.where(m, weight, 0.0) for m in inside]


def spread(values, factors):
    return jnp.concatenate([values * f for f in factors], axis=0).astype(BF16)


def gather_heads(stacked, factors):
    n = stacked.shape[0] // len(factors)
    total = stacked[:n] * factors[0]
    for h in range(1, len(factors)):
        total = total + stacked[h * n : (h + 1) * n] * factors[h]
    return total


def pipelined(n, first, second, third):
    one, two = {}, {}
    for i in range(n + 2):
        if i < n:
            one[i] = first(i)
        if 0 <= i - 1 < n:
            two[i - 1] = second(i - 1, one.pop(i - 1))
        if i >= 2:
            third(i - 2, two.pop(i - 2))
        yield


def interleave(programs, lag):
    programs = [(i * lag, p) for i, p in enumerate(programs)]
    at = 0
    while programs:
        programs = [(start, p) for start, p in programs if at < start or next(p, STOP) is not STOP]
        at += 1


def score(q, k, ones):
    return nt(k.astype(BF16), spread(q, ones))


def soften(scores):
    exps = jnp.exp2(scores - jnp.max(scores, axis=0, keepdims=True))
    return (exps * (1.0 / jnp.sum(exps, axis=0, keepdims=True))).astype(BF16)


def mix(probs, v, ones):
    return gather_heads(tn(probs, v.astype(BF16)), ones)


def grad_scores_of(probs, grad_probs):
    wide = probs.astype(F32)
    inner = jnp.sum(grad_probs * wide, axis=0, keepdims=True)
    return (wide * (grad_probs - inner)).astype(BF16)


def centered(values):
    return values - jnp.mean(values, axis=-1, keepdims=True)


def rstd_of(center):
    return lax.rsqrt(jnp.mean(center * center, axis=-1, keepdims=True) + EPSILON)


def norm_levels(n, load, store):
    def first(i):
        values = load(i)
        return values, centered(values)

    def second(i, got):
        return got + (rstd_of(got[1]),)

    def third(i, got):
        values, center, rstd = got
        store(i, values, center * rstd, rstd)

    yield from pipelined(n, first, second, third)


def fold_rows(values):
    return jnp.sum(values.reshape(values.shape[0] // 8, 8, values.shape[1]), axis=0)


def load_wire(z, refs, wire_s):
    for k in range(z.lev):
        wire_s[k] = refs[k][0].astype(F32)


def wire_level(z, wire_s, k, l, b):
    half = z.d - LANES
    at = (l % 2) * half
    rows = slice(b * TOK, (b + 1) * TOK)
    low, high = wire_s[k, l, rows, :], wire_s[k, z.l + l // 2, rows, :]
    return jnp.concatenate([low, high[:, at : at + half]], axis=1)


def store_wire_levels(z, wire_s, b, level):
    for k in range(z.lev):
        parts = lane_parts(z, [level(k * z.l + l) for l in range(z.l)])
        for j, part in enumerate(parts):
            wire_s[k, j, b * TOK : (b + 1) * TOK, :] = part


def flush_wire(z, wire_s, refs):
    if z.ro > z.nb * TOK:
        wire_s[:, :, z.nb * TOK :, :] = jnp.zeros_like(wire_s[:, :, z.nb * TOK :, :])
    for k in range(z.lev):
        refs[k][0] = wire_s[k].astype(BF16)


def bf16_rows(z, ref):
    return ref[...].reshape(z.n, ref.shape[-1]).astype(BF16)


def put_rows(z, ref, values):
    ref[...] = values.reshape(z.lt, TOK, values.shape[-1])


def some_rows(z, ref, i):
    rows = ref[i * CHUNK : (i + 1) * CHUNK]
    return rows.reshape(CHUNK * TOK, ref.shape[-1]).astype(BF16)


def tile(j, t):
    return slice((2 * j + t) * LANES, (2 * j + t + 1) * LANES)


def put(ref, at, value):
    ref[at] = value


def group(g):
    return slice(g * GROUP, (g + 1) * GROUP)


def attention(n, qkv, bias, probs_at, store, ones, factor):
    def first(i):
        return [
            (score(qkv(i, 0, t), qkv(i, 1, t), ones) * factor + bias(t), qkv(i, 2, t)) for t in range(2)
        ]

    def second(i, got):
        return [(soften(scores), v) for scores, v in got]

    def third(i, got):
        outs = [mix(probs, v, ones) for probs, v in got]
        for t in range(2):
            probs_at(i, t)[...] = got[t][0]
            store(i, t, outs[t])

    yield from pipelined(n, first, second, third)


def attention_back(n, qkv, grad, probs_at, store, ones, scales, scale):
    def first(i):
        out = []
        for t in range(2):
            q, k, v = (qkv(i, j, t) for j in range(3))
            g_rows = spread(grad(i, t), ones)
            out.append(
                (probs_at(i, t)[...], nt(v.astype(BF16), g_rows), g_rows, spread(q, ones), k.astype(BF16))
            )
        return out

    def second(i, got):
        return [(item[0], grad_scores_of(item[0], item[1])) + item[2:] for item in got]

    def third(i, got):
        outs = []
        for probs, grad_scores, g_rows, q_rows, k in got:
            outs.append(
                (
                    gather_heads(tn(grad_scores, k), scales),
                    nn(grad_scores, q_rows) * scale,
                    nn(probs, g_rows),
                    grad_scores,
                )
            )
        for t in range(2):
            store(i, t, outs[t])

    yield from pipelined(n, first, second, third)


def score_factor(z):
    return np.float32((z.d // z.heads) ** (-0.5) * np.log2(np.e))


def of_band(b, refs):
    return [ref.at[:, b : b + 1] for ref in refs]


def forward_kernel(z, *refs):
    wire_in, wire_out = refs[: z.lev], refs[z.lev + 16 : 2 * z.lev + 16]
    wire_s = refs[2 * z.lev + 25]
    load_wire(z, wire_in, wire_s)
    interleave([forward_band(z, b, *refs) for b in range(z.nb)], LAG_F)
    flush_wire(z, wire_s, wire_out)


def forward_band(z, b, *refs):
    it = iter(refs)
    take = lambda n: [next(it) for _ in range(n)]
    wire_in = take(z.lev)
    offsets, sizes, bias_ref, column_mask = take(4)
    gain1, shift1, gain2, shift2, gain3, shift3 = take(6)
    w_qkv1, wo1, w_qkv2, wo2, w_up, w_down_t = take(6)
    wire_out = take(z.lev)
    kept = of_band(b, take(9))
    norm1_ref, norm2_ref, norm3_ref, att_ref, co_ref, act_ref, slope_ref, probs_ref, probs2_ref = kept
    (wire_s,) = take(1)
    x_s, n_s, o_s, a_s, qkv_s, bias_s = (ref.at[b] for ref in take(6))
    ones = head_masks(z)
    s = pl.program_id(0)
    token = lax.broadcasted_iota(jnp.int32, (TOK, 1), 0)
    cell = (token * 43) >> 8
    row = token - cell * WLAT + (lax.axis_index("lev") * z.nb + b) * WLAT
    cell = cell + (lax.axis_index("lon") * z.cells + offsets[s])
    cell = jnp.where(cell >= z.cells * z.lon, cell - z.cells * z.lon, cell)
    valid = (row < sizes[s, 0]) & (cell < sizes[s, 1])
    bias_s[...] = bias_ref[b] + jnp.where(valid, 0.0, NEGATIVE)

    def keep(ref, gain, shift):
        def store(lv, values, normed, rstd):
            x_s[lv] = values
            n_s[lv] = normed * gain[...] + shift[...]
            room = jnp.broadcast_to(rstd, (TOK, 2 * LANES - z.d))
            ref[0, 0, lv] = jnp.concatenate([normed, room], axis=1)

        return store

    yield from norm_levels(
        z.lt, lambda lv: wire_level(z, wire_s, lv // z.l, lv % z.l, b), keep(norm1_ref, gain1, shift1)
    )
    put_rows(z, qkv_s, nn(bf16_rows(z, n_s), w_qkv1[...]))

    yield from attention(
        z.lt,
        lambda lv, j, t: qkv_s[lv, :, tile(j, t)],
        lambda t: bias_s[t],
        lambda lv, t: probs_ref.at[0, 0, lv, t],
        lambda lv, t, out: put(a_s, (lv, slice(None), tile(0, t)), out),
        ones,
        score_factor(z),
    )
    att = bf16_rows(z, a_s)
    att_ref[0, 0] = att
    put_rows(z, o_s, nn(att, wo1[...]))

    yield from norm_levels(z.lt, lambda lv: x_s[lv] + o_s[lv], keep(norm2_ref, gain2, shift2))
    put_rows(z, qkv_s, nn(bf16_rows(z, n_s), w_qkv2[...]))

    yield from attention(
        TOK // GROUP,
        lambda g, j, t: qkv_s[:, group(g), tile(j, t)].reshape(z.lt * GROUP, LANES),
        lambda t: column_mask[...],
        lambda g, t: probs2_ref.at[0, 0, g, t],
        lambda g, t, out: put(a_s, (slice(None), group(g), tile(0, t)), out.reshape(z.lt, GROUP, LANES)),
        ones,
        score_factor(z),
    )
    co = bf16_rows(z, a_s)
    co_ref[0, 0] = co
    put_rows(z, o_s, nn(co, wo2[...]))

    yield from norm_levels(z.lt, lambda lv: x_s[lv] + o_s[lv], keep(norm3_ref, gain3, shift3))

    def up(i):
        return nn(some_rows(z, n_s, i), w_up[...])

    def gelu(i, hidden):
        share = 0.5 + 0.5 * lax.erf(hidden * (0.5**0.5))
        density = jnp.exp(hidden * hidden * -0.5) * ((2.0 * np.pi) ** -0.5)
        return (hidden * share).astype(BF16), (share + hidden * density).astype(BF16)

    def down(i, got):
        act, slope = got
        out = nt(act, w_down_t[...])
        rows = slice(i * CHUNK * TOK, (i + 1) * CHUNK * TOK)
        act_ref[0, 0, rows], slope_ref[0, 0, rows] = act, slope
        o_s[i * CHUNK : (i + 1) * CHUNK] = out.reshape(CHUNK, TOK, z.d)

    yield from pipelined(z.lt // CHUNK, up, gelu, down)

    store_wire_levels(z, wire_s, b, lambda lv: x_s[lv] + o_s[lv])


def wire_specs(z):
    return [pl.BlockSpec((1, z.nblk, z.ro, LANES), lambda s: (s, 0, 0, 0))] * z.lev


def wire_shapes(z):
    return [jax.ShapeDtypeStruct((z.s, z.nblk, z.ro, LANES), BF16)] * z.lev


def unit_spec(shape):
    return pl.BlockSpec((1,) + shape, lambda s: (s,) + (0,) * len(shape))


def whole_spec(array):
    return pl.BlockSpec(array.shape, lambda s: (0,) * array.ndim)


def residual_shapes(z):
    return [
        ((z.lt, TOK, 2 * LANES), F32),
        ((z.lt, TOK, 2 * LANES), F32),
        ((z.lt, TOK, 2 * LANES), F32),
        ((z.n, 2 * LANES), BF16),
        ((z.n, 2 * LANES), BF16),
        ((z.n, z.ff), BF16),
        ((z.n, z.ff), BF16),
        ((z.lt, 2, TOK, z.heads // 2 * TOK), BF16),
        ((TOK // GROUP, 2, z.lt * GROUP, z.heads // 2 * z.lt * GROUP), BF16),
    ]


def forward(z, wire, offsets, sizes, bias, column_mask, norms, weights):
    res = residual_shapes(z)
    rows3 = (z.nb, z.lt, TOK, z.d)
    out = pl.pallas_call(
        functools.partial(forward_kernel, z),
        grid=(z.s,),
        in_specs=wire_specs(z)
        + [
            *in_smem(2),
            whole_spec(bias),
            whole_spec(column_mask),
        ]
        + [whole_spec(a) for a in norms]
        + [whole_spec(a) for a in weights],
        out_specs=wire_specs(z) + [unit_spec((z.nb,) + shape) for shape, _ in res],
        out_shape=wire_shapes(z) + [jax.ShapeDtypeStruct((z.s, z.nb) + shape, t) for shape, t in res],
        scratch_shapes=[pltpu.VMEM((z.lev, z.nblk, z.ro, LANES), F32)]
        + [pltpu.VMEM(rows3, F32)] * 3
        + [
            pltpu.VMEM((z.nb, z.lt, TOK, 2 * LANES), F32),
            pltpu.VMEM((z.nb, z.lt, TOK, 6 * LANES), F32),
            pltpu.VMEM((z.nb, 2, TOK, z.heads // 2 * TOK), F32),
        ],
        compiler_params=pltpu.CompilerParams(vmem_limit_bytes=60 * 2**20),
        cost_estimate=cost(30),
        name="forward",
    )(*wire, offsets, sizes, bias, column_mask, *norms, *weights)
    return out[: z.lev], out[z.lev :]


def grad_list(z):
    return [
        ("up", z.ff), ("down_t", z.ff),
        ("qkv1", 3 * z.d), ("qkv2", 3 * z.d),
        ("o1", z.d), ("o2", z.d),
    ]


def half_blocks(z):
    full, rest = [], []
    for name, columns in grad_list(z):
        for row in range(0, z.d, 96):
            for col in range(0, columns, LANES):
                width = min(LANES, columns - col)
                (full if width == LANES else rest).append((name, row, col, width))
    out = [[piece + (0,)] for piece in full]
    for i in range(0, len(rest), 2):
        out.append([rest[i] + (0,), rest[i + 1] + (rest[i][3],)])
    return out


def grad_buffer(z, name, columns):
    if name[:3] == "qkv":
        return (z.d, 6 * LANES)
    if name[0] == "o":
        return (2 * LANES, columns)
    return (z.d, columns)


def grad_block(z, name, ref, row, col, width):
    half = z.d // 2
    if name[0] == "o":
        start = row // half * LANES
        return ref[start : start + 96, col : col + width]
    if name[:3] != "qkv":
        return ref[row : row + 96, col : col + width]
    pieces = []
    while width:
        t, lane = col // half, col % half
        count = min(width, half - lane)
        pieces.append(ref[row : row + 96, t * LANES + lane : t * LANES + lane + count])
        col, width = col + count, width - count
    return pieces[0] if len(pieces) == 1 else jnp.concatenate(pieces, axis=1)


def bias_rows(z):
    pick = np.zeros((WLON * 8, TOK), np.float32)
    for a in range(WLON):
        for i in range(WLAT):
            pick[a * 8 + i, a * WLAT + i] = 1.0
    return pick


def backward_band(z, b, kept, norms, weights, wire_s, own, db_s, vec_s, grads):
    norm1_ref, norm2_ref, norm3_ref, att_ref, co_ref, act_ref, slope_ref, probs_ref, probs2_ref = kept
    gain1, shift1, gain2, shift2, gain3, shift3 = norms
    w_qkv1, wo1, w_qkv2, wo2, w_up, w_down_t = weights
    g_s, o_s, a_s, qkv_s, grad_s, gh_s = own
    scale = np.float32((z.d // z.heads) ** (-0.5))
    ones, scales = head_masks(z), head_masks(z, scale)

    for k in range(z.lev):
        got = [wire_level(z, wire_s, k, l, b) for l in range(z.l)]
        for l in range(z.l):
            g_s[k * z.l + l] = got[l]

    def normed_tokens(ref, gain, shift):
        normed = ref[0, 0][:, :, : z.d] * gain[...] + shift[...]
        return normed.reshape(z.n, z.d).astype(BF16)

    def back_down(i):
        rows = slice(i * CHUNK * TOK, (i + 1) * CHUNK * TOK)
        return nn(some_rows(z, g_s, i), w_down_t[...]), slope_ref[0, 0, rows, :].astype(F32)

    def back_gelu(i, got):
        return (got[0] * got[1]).astype(BF16)

    def back_up(i, grad):
        out = nt(grad, w_up[...])
        gh_s[i * CHUNK * TOK : (i + 1) * CHUNK * TOK] = grad
        o_s[i * CHUNK : (i + 1) * CHUNK] = out.reshape(CHUNK, TOK, z.d)

    yield from pipelined(z.lt // CHUNK, back_down, back_gelu, back_up)
    grads["down_t"][...] += tn(bf16_rows(z, g_s), act_ref[0, 0])
    grads["up"][...] += tn(normed_tokens(norm3_ref, gain3, shift3), gh_s[...])

    def norm_step(ref, gain, at, target):
        sums = [vec_s[b, at], vec_s[b, at + 1]]

        def first(lv):
            grad, normed, rstd = o_s[lv], ref[0, 0, lv, :, : z.d], ref[0, 0, lv, :, z.d : z.d + 1]
            sums[0] += fold_rows(grad * normed)
            sums[1] += fold_rows(grad)
            return target[lv], normed, rstd, grad * gain[...]

        def second(lv, got):
            old, normed, rstd, gained = got
            one = jnp.mean(gained, axis=-1, keepdims=True)
            two = jnp.mean(gained * normed, axis=-1, keepdims=True)
            return old, normed, rstd, gained, one, two

        def third(lv, got):
            old, normed, rstd, gained, one, two = got
            target[lv] = old + rstd * (gained - one - normed * two)

        yield from pipelined(z.lt, first, second, third)
        vec_s[b, at], vec_s[b, at + 1] = sums

    yield from norm_step(norm3_ref, gain3, 4, g_s)

    branch = bf16_rows(z, g_s)
    grads["o2"][...] += tn(co_ref[0, 0], branch)
    put_rows(z, a_s, nt(branch, wo2[...]))
    tokens = normed_tokens(norm2_ref, gain2, shift2)
    put_rows(z, qkv_s, nn(tokens, w_qkv2[...]))

    def keep_column(g, t, got):
        for j in range(3):
            grad_s[:, group(g), tile(j, t)] = got[j].reshape(z.lt, GROUP, LANES)

    yield from attention_back(
        TOK // GROUP,
        lambda g, j, t: qkv_s[:, group(g), tile(j, t)].reshape(z.lt * GROUP, LANES),
        lambda g, t: a_s[:, group(g), tile(0, t)].reshape(z.lt * GROUP, LANES),
        lambda g, t: probs2_ref.at[0, 0, g, t],
        keep_column,
        ones,
        scales,
        scale,
    )

    def project_back(tokens, name, w):
        grad = bf16_rows(z, grad_s)
        grads[name][...] += tn(tokens, grad)
        put_rows(z, o_s, nt(grad, w[...]))

    project_back(tokens, "qkv2", w_qkv2)
    yield from norm_step(norm2_ref, gain2, 2, g_s)

    branch = bf16_rows(z, g_s)
    grads["o1"][...] += tn(att_ref[0, 0], branch)
    put_rows(z, a_s, nt(branch, wo1[...]))
    tokens = normed_tokens(norm1_ref, gain1, shift1)
    put_rows(z, qkv_s, nn(tokens, w_qkv1[...]))

    def keep_window(lv, t, got):
        for j in range(3):
            grad_s[lv, :, tile(j, t)] = got[j]
        db_s[b, t] += got[3].astype(F32)

    yield from attention_back(
        z.lt,
        lambda lv, j, t: qkv_s[lv, :, tile(j, t)],
        lambda lv, t: a_s[lv, :, tile(0, t)],
        lambda lv, t: probs_ref.at[0, 0, lv, t],
        keep_window,
        ones,
        scales,
        scale,
    )
    project_back(tokens, "qkv1", w_qkv1)
    yield from norm_step(norm1_ref, gain1, 0, g_s)

    store_wire_levels(z, wire_s, b, lambda lv: g_s[lv])


def backward_kernel(z, *refs):
    it = iter(refs)
    take = lambda n: [next(it) for _ in range(n)]
    wire_in = take(z.lev)
    kept = take(9)
    (pick_ref,) = take(1)
    gain1, shift1, gain2, shift2, gain3, shift3 = take(6)
    w_qkv1, wo1, w_qkv2, wo2, w_up, w_down_t = take(6)
    wire_out = take(z.lev)
    late_ref, mine_ref, other_ref = take(3)
    wire_s, late_s, g_s, o_s, a_s, qkv_s, grad_s, gh_s, db_s, vec_s, sums_s = take(11)
    grads = {name: ref for (name, _), ref in zip(grad_list(z), take(len(grad_list(z))))}
    s = pl.program_id(0)

    @pl.when(s == 0)
    def _():
        for ref in list(grads.values()) + [db_s, vec_s]:
            ref[...] = jnp.zeros_like(ref)

    load_wire(z, wire_in, wire_s)
    bands = []
    for b in range(z.nb):
        own = [ref.at[b] for ref in (g_s, o_s, a_s, qkv_s, grad_s, gh_s)]
        norms = (gain1, shift1, gain2, shift2, gain3, shift3)
        weights = (w_qkv1, wo1, w_qkv2, wo2, w_up, w_down_t)
        bands.append(
            backward_band(z, b, of_band(b, kept), norms, weights, wire_s, own, db_s, vec_s, grads)
        )
    interleave(bands, LAG_B)
    flush_wire(z, wire_s, wire_out)
    for band in range(z.nb):
        rows = wire_s[:, :, band * TOK + HALO0 : (band + 1) * TOK, :]
        late_s[:, :, band * HALO : (band + 1) * HALO, :] = rows
    late_ref[:, 0] = late_s[...].astype(BF16)

    @pl.when(s == z.s - 1)
    def _():
        p, core = lax.axis_index("lev"), lax.axis_index("lon") % 2

        def place(i):
            return ((i // z.lev) ^ core) * z.lev + ((i % z.lev) ^ p)

        for at, pieces in enumerate(half_blocks(z)):
            values = [grad_block(z, n, grads[n], r, c, width) for n, r, c, width, _ in pieces]
            block = values[0] if len(values) == 1 else jnp.concatenate(values, axis=1)
            start = (at % z.hb) * 96
            sums_s[place(at // z.hb), start : start + 96, :] = block.astype(BF16)
        extra = z.hb * 96
        sums_s[:, extra:, :] = jnp.zeros_like(sums_s[:, extra:, :])
        vectors = [jnp.sum(jnp.sum(vec_s[:, i], axis=0), axis=0, keepdims=True) for i in range(6)]
        vectors = jnp.concatenate(vectors + [jnp.zeros((UNIT - 6, z.d), F32)], axis=0)
        vectors = jnp.concatenate([vectors, jnp.zeros((UNIT, 2 * LANES - z.d), F32)], axis=1)

        def put_unit(u, value):
            start = extra + (u % z.upp) * UNIT
            if not isinstance(u, int):
                start = pl.multiple_of(start, UNIT)
            sums_s[place(u // z.upp), pl.ds(start, UNIT), :] = value.astype(BF16)

        for j in range(2):
            put_unit(z.bands * 4 + j, vectors[:, j * LANES : (j + 1) * LANES])
        lane = lax.broadcasted_iota(jnp.int32, (1, z.heads * TOK), 1)
        odd = jnp.zeros(lane.shape, jnp.bool_)
        for h in range(1, z.heads, 2):
            odd = odd | ((lane >= h * TOK) & (lane < (h + 1) * TOK))
        width = -(-(z.heads * TOK) // LANES) * LANES
        for band in range(z.nb):
            rows = [nn(pick_ref[...], db_s[band, t], precision=lax.Precision.HIGHEST) for t in range(2)]
            rows = jnp.concatenate(rows, axis=1)
            halves = []
            for parity in range(2):
                kept = jnp.where(odd if parity else ~odd, rows, 0.0)
                kept = jnp.concatenate(
                    [kept, jnp.zeros((rows.shape[0], width - z.heads * TOK), F32)], axis=1
                )
                total = None
                for a in range(WLON):
                    part = kept[a * 8 : (a + 1) * 8]
                    shift = (WLON - 1 - a) * WLAT
                    if shift:
                        part = pltpu.roll(part, shift, 1)
                    total = part if total is None else total + part
                halves.append(total)
            both = jnp.concatenate(halves, axis=0)
            for j in range(4):
                put_unit((p * z.nb + band) * 4 + j, both[:, j * LANES : (j + 1) * LANES])
        mine_ref[...] = sums_s[: z.lev]
        other_ref[...] = sums_s[z.lev :]


def backward(z, wire, residuals, norms, weights):
    res = residual_shapes(z)
    rows3 = (z.nb, z.lt, TOK, z.d)
    pick = jnp.asarray(bias_rows(z))
    half = (z.lev, z.pr, LANES)
    out = pl.pallas_call(
        functools.partial(backward_kernel, z),
        **dict(
            grid=(z.s,),
            in_specs=[
                spec
                for spec in wire_specs(z)
                + [unit_spec((z.nb,) + shape) for shape, _ in res]
                + [whole_spec(pick)]
                + [whole_spec(a) for a in norms]
                + [whole_spec(a) for a in weights]
            ],
            out_specs=[spec for spec in wire_specs(z)]
            + [pl.BlockSpec((z.lev, 1, z.nblk, z.rh, LANES), lambda s: (0, s, 0, 0, 0))]
            + [pl.BlockSpec(half, lambda s: (0, 0, 0))] * 2,
            scratch_shapes=[
                pltpu.VMEM((z.lev, z.nblk, z.ro, LANES), F32),
                pltpu.VMEM((z.lev, z.nblk, z.rh, LANES), F32),
            ]
            + [pltpu.VMEM(rows3, F32)] * 2
            + [
                pltpu.VMEM((z.nb, z.lt, TOK, 2 * LANES), F32),
                pltpu.VMEM((z.nb, z.lt, TOK, 6 * LANES), F32),
                pltpu.VMEM((z.nb, z.lt, TOK, 6 * LANES), F32),
                pltpu.VMEM((z.nb, z.n, z.ff), BF16),
                pltpu.VMEM((z.nb, 2, TOK, z.heads // 2 * TOK), F32),
                pltpu.VMEM((z.nb, 6, 8, z.d), F32),
                pltpu.VMEM((z.np, z.pr, LANES), BF16),
            ]
            + [pltpu.VMEM(grad_buffer(z, *item), F32) for item in grad_list(z)],
        ),
        out_shape=wire_shapes(z)
        + [jax.ShapeDtypeStruct((z.lev, z.s, z.nblk, z.rh, LANES), BF16)]
        + [jax.ShapeDtypeStruct(half, BF16)] * 2,
        compiler_params=pltpu.CompilerParams(vmem_limit_bytes=62 * 2**20),
        cost_estimate=cost(40),
        name="backward",
    )(*wire, *residuals, pick, *norms, *weights)
    return out[: z.lev], out[z.lev], out[z.lev + 1], out[z.lev + 2]


def tree(parts):
    while len(parts) > 1:
        parts = [parts[i] + parts[i + 1] for i in range(0, len(parts), 2)]
    return parts[0]


def lev_swap(z, array, k):
    return lax.ppermute(array, "lev", [(i, i ^ k) for i in range(z.lev)])


def lon_swap(z, array, k):
    return lax.ppermute(array, "lon", [(i, i ^ k) for i in range(z.lon)])


def merge_kernel(z, offsets, *refs):
    wire, late_ref, outs = refs[: z.lev], refs[z.lev], refs[z.lev + 1 :]
    row = lax.broadcasted_iota(jnp.int32, (HALO, LANES), 0) + HALO0
    for s in range(z.s):
        moved = row >= (z.cells - offsets[s]) * WLAT
        for k in range(z.lev):
            for j in range(z.nblk):
                rows, late = wire[k][s, j].astype(F32), late_ref[k, s, j].astype(F32)
                parts = []
                for b in range(z.nb):
                    own = rows[b * TOK : (b + 1) * TOK]
                    got = late[b * HALO : (b + 1) * HALO]
                    parts += [own[:HALO0], jnp.where(moved, got, own[HALO0:])]
                if z.ro > z.nb * TOK:
                    parts.append(rows[z.nb * TOK :])
                outs[k][s, j] = jnp.concatenate(parts, axis=0).astype(BF16)


def merge_cells(z, wire, late, offsets):
    return pl.pallas_call(
        functools.partial(merge_kernel, z),
        in_specs=in_smem(1) + in_vmem(z.lev + 1),
        out_specs=in_vmem(z.lev),
        out_shape=[jax.ShapeDtypeStruct((z.s, z.nblk, z.ro, LANES), BF16)] * z.lev,
        compiler_params=pltpu.CompilerParams(vmem_limit_bytes=40 * 2**20),
        cost_estimate=cost(3),
        name="merge",
    )(offsets, *wire, late)


def tie(values, *others):
    return lax.optimization_barrier((values,) + others)[0]


def sum_cores(z, mine, other):
    got = lon_swap(z, other, 1)
    return [(mine[k].astype(F32) + got[k].astype(F32)).astype(BF16) for k in range(z.lev)]


def sum_levels(z, half):
    parts = [half[0]] + [lev_swap(z, half[k], k) for k in range(1, z.lev)]
    return tree([v.astype(F32) for v in parts]).astype(BF16)


def sum_slabs(z, quarter):
    parts = [quarter] + [lon_swap(z, quarter, 2 * k) for k in range(1, z.lon // 2)]
    return tree([v.astype(F32) for v in parts]).astype(BF16)


def share_levels(z, done):
    return [done] + [lev_swap(z, done, k) for k in range(1, z.lev)]


def table_lanes(z, h):
    lanes = np.full((WLAT, 32), -1, np.int32)
    for i in range(WLAT):
        lanes[i, : 2 * WLON - 1] = h * TOK + np.arange(2 * WLON - 1) * WLAT + i
    return lanes.reshape(1, WLAT * 32)


def finish_kernel(z, lanes, order, own, other, *outs):
    p, core = lax.axis_index("lev"), lax.axis_index("lon") % 2
    named = {name: ref for (name, _), ref in zip(grad_list(z), outs)}
    vec_refs, bias_ref = outs[len(named) : len(named) + 6], outs[len(named) + 6]

    def read(piece, start, size):
        half, j = piece // z.lev, piece % z.lev
        rows = slice(start, start + size)
        return jnp.where(core == half, own[p ^ j, rows, :], other[p ^ j, rows, :])

    for at, pieces in enumerate(half_blocks(z)):
        block = read(at // z.hb, (at % z.hb) * 96, 96).astype(F32)
        for n, r, c, width, lane in pieces:
            named[n][r : r + 96, c : c + width] = block[:, lane : lane + width]
    extra = z.hb * 96
    units = [read(u // z.upp, extra + (u % z.upp) * UNIT, UNIT) for u in range(z.units)]
    vectors = jnp.concatenate(units[z.bands * 4 :], axis=1).astype(F32)
    for i in range(6):
        vec_refs[i][...] = vectors[i : i + 1, : z.d]
    table = [jnp.concatenate(units[4 * k : 4 * k + 4], axis=1) for k in range(z.bands)]
    table = nn(order[...], jnp.concatenate(table, axis=0)).astype(BF16)
    half = table.shape[0] // 2
    for h in range(z.heads):
        at = lax.broadcasted_iota(jnp.int32, (4 * LANES, WLAT * 32), 0)
        pick = jnp.where(at == lanes[h : h + 1, :], 1.0, 0.0).astype(BF16)
        rows = table[(h % 2) * half : (h % 2) * half + half]
        got = nn(rows, pick)
        for i in range(WLAT):
            values = got[: WLAT * z.bands, i * 32 : i * 32 + 2 * WLON - 1]
            bias_ref[h, i] = values.reshape(WLAT, z.bands, 2 * WLON - 1)


def finish(z, own, other):
    shapes = [jax.ShapeDtypeStruct((z.d, columns), F32) for _, columns in grad_list(z)]
    shapes += [jax.ShapeDtypeStruct((1, z.d), F32)] * 6
    shapes += [jax.ShapeDtypeStruct((z.heads, WLAT, WLAT, z.bands, 2 * WLON - 1), F32)]
    lanes = jnp.asarray(np.concatenate([table_lanes(z, h) for h in range(z.heads)]))
    order = np.zeros((2 * 8 * z.bands, z.bands * UNIT), np.float32)
    for parity in range(2):
        for i in range(8):
            for k in range(z.bands):
                order[parity * 8 * z.bands + i * z.bands + k, k * UNIT + parity * 8 + i] = 1.0
    order = jnp.asarray(order, BF16)
    out = pl.pallas_call(
        functools.partial(finish_kernel, z),
        in_specs=in_vmem(4),
        out_specs=in_vmem(len(shapes)),
        out_shape=shapes,
        compiler_params=pltpu.CompilerParams(vmem_limit_bytes=40 * 2**20),
        cost_estimate=cost(4),
        name="finish",
    )(lanes, order, own, other)
    named = {name: value for (name, _), value in zip(grad_list(z), out)}
    vectors = [v.reshape(z.d) for v in out[len(named) : len(named) + 6]]
    return named, vectors, out[-1].transpose(3, 0, 1, 2, 4)


def bias_kernel(z, table_ref, pick_ref, qkv1, out1, qkv2, out2, out_ref, *rest):
    even_s, odd_s = rest[4:]
    side = z.d // 2
    for source, target in ((qkv1, rest[0]), (qkv2, rest[2])):
        room = jnp.zeros((z.d, LANES - side), BF16)
        for t in range(6):
            part = source[:, t * side : (t + 1) * side]
            target[:, t * LANES : (t + 1) * LANES] = jnp.concatenate([part, room], axis=1)
    for source, target in ((out1, rest[1]), (out2, rest[3])):
        for t in range(2):
            target[t * LANES : t * LANES + side] = source[t * side : (t + 1) * side]
            target[t * LANES + side : (t + 1) * LANES] = jnp.zeros((LANES - side, z.d), BF16)
    width = 4 * LANES
    lane = lax.broadcasted_iota(jnp.int32, (2 * WLON - 1, width), 1)
    step = lax.broadcasted_iota(jnp.int32, (2 * WLON - 1, width), 0) * WLAT
    for parity, ref in ((0, even_s), (1, odd_s)):
        total = None
        for h in range(parity, z.heads, 2):
            for i in range(WLAT):
                place = jnp.where(lane == step + (h * TOK + i), 1.0, 0.0).astype(BF16)
                values = table_ref[h, i]
                high = values.astype(BF16)
                low = (values - high.astype(F32)).astype(BF16)
                part = nn(jnp.concatenate([high, low], axis=0), place)
                total = part if total is None else total + part
        rows = z.nb * 8
        ref[...] = total[:rows] + total[rows:]
    head = lax.broadcasted_iota(jnp.int32, (1, width), 1)
    odd = jnp.zeros(head.shape, jnp.bool_)
    for h in range(1, z.heads, 2):
        odd = odd | ((head >= h * TOK) & (head < (h + 1) * TOK))
    side = z.heads // 2 * TOK
    for b in range(z.nb):
        even, uneven = even_s[b * 8 : (b + 1) * 8], odd_s[b * 8 : (b + 1) * 8]
        rows = []
        for a in range(WLON):
            shift = (width - (WLON - 1 - a) * WLAT) % width
            turned = [pltpu.roll(v, shift, 1) if shift else v for v in (even, uneven)]
            rows.append(jnp.where(odd, turned[1], turned[0]))
        rows = jnp.concatenate(rows, axis=0)
        full = lax.dot_general(
            pick_ref[...], rows, (((0,), (0,)), ((), ())),
            precision=lax.Precision.HIGHEST, preferred_element_type=F32,
        ) * np.float32(np.log2(np.e))
        out_ref[b, 0] = full[:, :side]
        out_ref[b, 1] = full[:, side : 2 * side]


def bias_of(z, bias_table, p, weights):
    table = lax.dynamic_slice_in_dim(bias_table, p * z.nb, z.nb, axis=0)
    table = jnp.pad(table.transpose(1, 2, 0, 3, 4), ((0, 0),) * 3 + ((0, 2), (0, 0)))
    table = table.reshape(z.heads, WLAT, z.nb * 8, 2 * WLON - 1)
    wide = jax.ShapeDtypeStruct((z.d, 6 * LANES), BF16)
    tall = jax.ShapeDtypeStruct((2 * LANES, z.d), BF16)
    bias = jax.ShapeDtypeStruct((z.nb, 2, TOK, z.heads // 2 * TOK), F32)
    out = pl.pallas_call(
        functools.partial(bias_kernel, z),
        out_shape=[bias, wide, tall, wide, tall],
        scratch_shapes=[pltpu.VMEM((z.nb * 8, 4 * LANES), F32)] * 2,
        compiler_params=pltpu.CompilerParams(vmem_limit_bytes=40 * 2**20),
        cost_estimate=cost(4),
        name="bias",
    )(table, jnp.asarray(bias_rows(z)), *weights)
    return out[0], list(out[1:])


def lev_exchange(z, wire):
    return [wire[0]] + [lev_swap(z, wire[k], k) for k in range(1, z.lev)]


def lon_shift(z, array, distance):
    return lax.ppermute(array, "lon", [(w, (w + distance) % z.lon) for w in range(z.lon)])


def last_cells(z, wire):
    rows = [a[:, :, : z.nb * TOK].reshape(z.s, z.nblk, z.nb, TOK, LANES)[:, :, :, HALO0:] for a in wire]
    return jnp.stack(rows).reshape(z.lev, z.s, z.nblk, z.rh, LANES)


def on_device(
    inputs, cotangent, grid_sizes, offsets, gain_one, shift_one, qkv_window, out_window, bias_table,
    gain_two, shift_two, qkv_column, out_column, gain_three, shift_three, w_up, w_down,
):
    d = inputs.shape[-1]
    z = Sizes(lax.axis_size("lev"), lax.axis_size("lon"), inputs.shape, bias_table.shape[1], w_up.shape[1])
    p = lax.axis_index("lev")
    swap = lambda a: a.transpose(0, 1, 3, 2, 4)

    half = WLON // 2
    x, c = swap(inputs), swap(cotangent)
    halo_x = lon_shift(z, x[:, :, :half], -1)
    raw = (qkv_window, out_window, qkv_column, out_column)
    bias, weights = bias_of(z, bias_table, p, raw)
    weights = weights + [w_up, w_down.T]
    halo_x, bias = lax.optimization_barrier((halo_x, bias))
    halo_c = lon_shift(z, tie(c[:, :, :half], halo_x), -1)
    wire_x = pack(z, x, halo_x, offsets)
    halo_c = tie(halo_c, *wire_x)
    wire_x = lev_exchange(z, wire_x)
    wire_c = lev_exchange(z, pack(z, c, halo_c, offsets))
    of_key = np.arange(z.lt * GROUP) % GROUP
    of_query = np.tile(of_key, z.heads // 2)
    column_mask = jnp.asarray(
        np.where(of_key[:, None] == of_query[None, :], 0.0, NEGATIVE).astype(np.float32)
    )

    norms = [v[None] for v in (gain_one, shift_one, gain_two, shift_two, gain_three, shift_three)]
    wire_r, residuals = forward(z, wire_x, offsets, grid_sizes, bias, column_mask, norms, weights)
    wire_r = lev_exchange(z, wire_r)
    grads = backward(z, wire_c, residuals, norms, weights)
    (wire_g, late, mine, other), wire_r = lax.optimization_barrier((grads, wire_r))
    halo_r = lon_shift(z, last_cells(z, wire_r), 1)
    late = lon_shift(z, late, 1)
    sums = sum_cores(z, mine, other)
    sums = sum_levels(z, sums)
    wire_g = lev_exchange(z, merge_cells(z, wire_g, late, offsets))
    result = unpack(z, wire_r, halo_r, offsets)
    sums = sum_slabs(z, tie(sums, halo_r, late))
    sums = share_levels(z, tie(sums, result))
    input_grad = unpack(z, wire_g, None, offsets)
    own = jnp.stack(tie(sums, input_grad))
    other = lon_swap(z, own, 1)
    named, vec, table = finish(z, own, other)
    return (
        swap(result), swap(input_grad),
        vec[0], vec[1], named["qkv1"], named["o1"], table,
        vec[2], vec[3], named["qkv2"], named["o2"],
        vec[4], vec[5], named["up"], named["down_t"].T,
    )


def solution(mesh):
    tokens = P(None, "lev", None, "lon", None)
    return jax.shard_map(
        on_device,
        mesh=mesh,
        in_specs=(tokens, tokens) + (P(),) * 15,
        out_specs=(tokens, tokens) + (P(),) * 13,
        check_vma=False,
    )
```

```python
import functools

import jax
import jax.numpy as jnp
import numpy as np
from jax import lax
from jax.experimental import pallas as pl
from jax.experimental.pallas import tpu as pltpu
from jax.sharding import PartitionSpec as P

WLAT = 6
WLON = 12
TOK = WLAT * WLON
HALF = TOK // 2
HALO0 = 32
HALO = TOK - HALO0
GROUP = 8
CHUNK = 8
STOP = object()
LAG_F = 2
LAG_B = 0
EPSILON = 1e-05
NEGATIVE = -1000000000.0
F32 = jnp.float32
BF16 = jnp.bfloat16
LANES = 128
UNIT = 16


def up16(n):
    return (n + 15) // 16 * 16


def nn(a, b, **kw):
    return lax.dot_general(a, b, (((1,), (0,)), ((), ())), preferred_element_type=F32, **kw)


def nt(a, b):
    return lax.dot_general(a, b, (((1,), (1,)), ((), ())), preferred_element_type=F32)


def tn(a, b):
    return lax.dot_general(a, b, (((0,), (0,)), ((), ())), preferred_element_type=F32)


class Sizes:
    def __init__(self, lev, lon, shape, heads, hidden):
        self.lev, self.lon = lev, lon
        self.s, self.l, self.rows, self.cells, self.d = shape
        self.heads, self.ff = heads, hidden
        self.bands = self.rows // WLAT
        self.nb = self.bands // lev
        self.lt = self.l * lev
        self.n = self.lt * TOK
        self.ro = up16(self.nb * TOK)
        self.rh = self.nb * HALO
        self.nblk = self.l + (self.l + 1) // 2
        self.tokens = self.cells * self.rows
        self.np = 2 * lev
        self.blocks = 2 * (2 * hidden // 2 + 3 * self.d + self.d) // LANES * (self.d // 96)
        self.hb = self.blocks // self.np
        self.units = self.bands * 4 + 2
        self.upp = -(-self.units // self.np)
        self.pr = self.hb * 96 + self.upp * UNIT


def slot_rows(z):
    own = np.full((z.ro,), -(10**6), np.int32)
    halo = np.full((z.rh,), -(10**6), np.int32)
    for b in range(z.nb):
        for t in range(TOK):
            own[b * TOK + t] = (t // WLAT) * z.rows + b * WLAT + t % WLAT
            if t >= HALF:
                halo[b * HALO + t - HALO0] = own[b * TOK + t] - z.tokens
    return own, halo


def lane_parts(z, levels):
    parts = [v[:, :LANES] for v in levels]
    high = [v[:, LANES:] for v in levels]
    if z.l % 2:
        high.append(jnp.zeros_like(high[0]))
    for l in range(0, len(high), 2):
        parts.append(jnp.concatenate([high[l], high[l + 1]], axis=1))
    return parts


def pack_kernel(z, offsets, base, x_ref, halo_ref, *rest):
    outs, onehot = rest[: z.lev], rest[z.lev]
    p = lax.axis_index("lev")
    rows = z.tokens + halo_ref.shape[2] * z.rows
    column = lax.broadcasted_iota(jnp.int32, (z.ro, rows), 1)
    for s in range(z.s):
        for k in range(z.lev):
            hit = column == base[...] + (offsets[s] * z.rows + (p ^ k) * (z.nb * WLAT))
            onehot[s, k * z.ro : (k + 1) * z.ro] = jnp.where(hit, 1.0, 0.0).astype(BF16)
        levels = []
        for l in range(z.l):
            cells = [r[s, l].reshape(r.shape[2] * z.rows, z.d) for r in (x_ref, halo_ref)]
            levels.append(jnp.concatenate(cells, axis=0))
        moved = nn(onehot[s], jnp.concatenate(lane_parts(z, levels), axis=1)).astype(BF16)
        for k in range(z.lev):
            for j in range(z.nblk):
                outs[k][s, j] = moved[k * z.ro : (k + 1) * z.ro, j * LANES : (j + 1) * LANES]


def in_vmem(count):
    return [pl.BlockSpec(memory_space=pltpu.VMEM)] * count


def in_smem(count):
    return [pl.BlockSpec(memory_space=pltpu.SMEM)] * count


def pack(z, x, halo, offsets):
    own, _ = slot_rows(z)
    rows = z.tokens + halo.shape[2] * z.rows
    return pl.pallas_call(
        functools.partial(pack_kernel, z),
        in_specs=in_smem(1) + in_vmem(3),
        out_specs=in_vmem(z.lev),
        scratch_shapes=[pltpu.VMEM((z.s, z.lev * z.ro, rows), BF16)],
        out_shape=[jax.ShapeDtypeStruct((z.s, z.nblk, z.ro, LANES), BF16)] * z.lev,
        compiler_params=pltpu.CompilerParams(vmem_limit_bytes=40 * 2**20),
        cost_estimate=cost(4),
        name="pack",
    )(offsets, jnp.asarray(own)[:, None], x, halo)


def unpack_kernel(z, merged, offsets, *rest):
    count = 1 if merged else 2
    bases, pieces = rest[:count], rest[count : count + z.lev]
    halo_ref, out_ref, onehot = rest[-3], rest[-2], rest[-1]
    p = lax.axis_index("lev")
    for s in range(z.s):
        at = 0
        for base, size in zip(bases, (z.ro, z.rh)):
            row = lax.broadcasted_iota(jnp.int32, (z.tokens, size), 0)
            for k in range(z.lev):
                place = base[...] + (offsets[s] * z.rows + (p ^ k) * (z.nb * WLAT))
                if merged:
                    place = jnp.where(place >= z.tokens, place - z.tokens, place)
                onehot[s, :, at : at + size] = jnp.where(row == place, 1.0, 0.0).astype(BF16)
                at += size
        columns = []
        for j in range(z.nblk):
            rows = [r[s, j] for r in pieces]
            if not merged:
                rows += [halo_ref[k, s, j] for k in range(z.lev)]
            columns.append(jnp.concatenate(rows, axis=0))
        moved = nn(onehot[s], jnp.concatenate(columns, axis=1))
        half = z.d - LANES
        for l in range(z.l):
            low = moved[:, l * LANES : (l + 1) * LANES]
            at = (z.l + l // 2) * LANES + (l % 2) * half
            tokens = jnp.concatenate([low, moved[:, at : at + half]], axis=1)
            out_ref[s, l] = tokens.reshape(z.cells, z.rows, z.d).astype(BF16)


def unpack(z, own, halo, offsets):
    merged = halo is None
    bases = [jnp.asarray(v)[None] for v in slot_rows(z)][: 1 if merged else 2]
    slots = z.ro if merged else z.ro + z.rh
    arrays = bases + list(own) + ([] if merged else [halo])
    return pl.pallas_call(
        functools.partial(unpack_kernel, z, merged),
        in_specs=in_smem(1) + in_vmem(len(arrays)),
        out_specs=pl.BlockSpec(memory_space=pltpu.VMEM),
        scratch_shapes=[pltpu.VMEM((z.s, z.tokens, z.lev * slots), BF16)],
        out_shape=jax.ShapeDtypeStruct((z.s, z.l, z.cells, z.rows, z.d), BF16),
        compiler_params=pltpu.CompilerParams(vmem_limit_bytes=40 * 2**20),
        cost_estimate=cost(4),
        name="unpack",
    )(offsets, *arrays)


def cost(microseconds):
    return pl.CostEstimate(
        flops=int(microseconds * 5e8), transcendentals=0, bytes_accessed=int(microseconds * 3e6)
    )


def loop(n, body, unroll=None):
    unroll = n if unroll is None else unroll

    def some(i, c):
        for j in range(unroll):
            body(i * unroll + j)
        return c

    if n == unroll:
        some(0, 0)
    else:
        lax.fori_loop(0, n // unroll, some, 0)


def head_masks(z, weight=1.0):
    lane = lax.broadcasted_iota(jnp.int32, (1, LANES), 1)
    size = z.d // z.heads
    inside = [(lane >= h * size) & (lane < (h + 1) * size) for h in range(z.heads // 2)]
    return [jnp.where(m, weight, 0.0) for m in inside]


def spread(values, factors):
    return jnp.concatenate([values * f for f in factors], axis=0).astype(BF16)


def gather_heads(stacked, factors):
    n = stacked.shape[0] // len(factors)
    total = stacked[:n] * factors[0]
    for h in range(1, len(factors)):
        total = total + stacked[h * n : (h + 1) * n] * factors[h]
    return total


def pipelined(n, first, second, third):
    one, two = {}, {}
    for i in range(n + 2):
        if i < n:
            one[i] = first(i)
        if 0 <= i - 1 < n:
            two[i - 1] = second(i - 1, one.pop(i - 1))
        if i >= 2:
            third(i - 2, two.pop(i - 2))
        yield


def interleave(programs, lag):
    programs = [(i * lag, p) for i, p in enumerate(programs)]
    at = 0
    while programs:
        programs = [(start, p) for start, p in programs if at < start or next(p, STOP) is not STOP]
        at += 1


def score(q, k, ones):
    return nt(k.astype(BF16), spread(q, ones))


def soften(scores):
    exps = jnp.exp2(scores - jnp.max(scores, axis=0, keepdims=True))
    return (exps * (1.0 / jnp.sum(exps, axis=0, keepdims=True))).astype(BF16)


def mix(probs, v, ones):
    return gather_heads(tn(probs, v.astype(BF16)), ones)


def grad_scores_of(probs, grad_probs):
    wide = probs.astype(F32)
    inner = jnp.sum(grad_probs * wide, axis=0, keepdims=True)
    return (wide * (grad_probs - inner)).astype(BF16)


def centered(values):
    return values - jnp.mean(values, axis=-1, keepdims=True)


def rstd_of(center):
    return lax.rsqrt(jnp.mean(center * center, axis=-1, keepdims=True) + EPSILON)


def norm_levels(n, load, store):
    def first(i):
        values = load(i)
        return values, centered(values)

    def second(i, got):
        return got + (rstd_of(got[1]),)

    def third(i, got):
        values, center, rstd = got
        store(i, values, center * rstd, rstd)

    yield from pipelined(n, first, second, third)


def fold_rows(values):
    return jnp.sum(values.reshape(values.shape[0] // 8, 8, values.shape[1]), axis=0)


def load_wire(z, refs, wire_s):
    for k in range(z.lev):
        wire_s[k] = refs[k][0].astype(F32)


def wire_level(z, wire_s, k, l, b):
    half = z.d - LANES
    at = (l % 2) * half
    rows = slice(b * TOK, (b + 1) * TOK)
    low, high = wire_s[k, l, rows, :], wire_s[k, z.l + l // 2, rows, :]
    return jnp.concatenate([low, high[:, at : at + half]], axis=1)


def store_wire_levels(z, wire_s, b, level):
    for k in range(z.lev):
        parts = lane_parts(z, [level(k * z.l + l) for l in range(z.l)])
        for j, part in enumerate(parts):
            wire_s[k, j, b * TOK : (b + 1) * TOK, :] = part


def flush_wire(z, wire_s, refs):
    if z.ro > z.nb * TOK:
        wire_s[:, :, z.nb * TOK :, :] = jnp.zeros_like(wire_s[:, :, z.nb * TOK :, :])
    for k in range(z.lev):
        refs[k][0] = wire_s[k].astype(BF16)


def bf16_rows(z, ref):
    return ref[...].reshape(z.n, ref.shape[-1]).astype(BF16)


def put_rows(z, ref, values):
    ref[...] = values.reshape(z.lt, TOK, values.shape[-1])


def some_rows(z, ref, i):
    rows = ref[i * CHUNK : (i + 1) * CHUNK]
    return rows.reshape(CHUNK * TOK, ref.shape[-1]).astype(BF16)


def tile(j, t):
    return slice((2 * j + t) * LANES, (2 * j + t + 1) * LANES)


def put(ref, at, value):
    ref[at] = value


def group(g):
    return slice(g * GROUP, (g + 1) * GROUP)


def attention(n, qkv, bias, probs_at, store, ones, factor):
    def first(i):
        return [
            (score(qkv(i, 0, t), qkv(i, 1, t), ones) * factor + bias(t), qkv(i, 2, t)) for t in range(2)
        ]

    def second(i, got):
        return [(soften(scores), v) for scores, v in got]

    def third(i, got):
        outs = [mix(probs, v, ones) for probs, v in got]
        for t in range(2):
            probs_at(i, t)[...] = got[t][0]
            store(i, t, outs[t])

    yield from pipelined(n, first, second, third)


def attention_back(n, qkv, grad, probs_at, store, ones, scales, scale):
    def first(i):
        out = []
        for t in range(2):
            q, k, v = (qkv(i, j, t) for j in range(3))
            g_rows = spread(grad(i, t), ones)
            out.append(
                (probs_at(i, t)[...], nt(v.astype(BF16), g_rows), g_rows, spread(q, ones), k.astype(BF16))
            )
        return out

    def second(i, got):
        return [(item[0], grad_scores_of(item[0], item[1])) + item[2:] for item in got]

    def third(i, got):
        outs = []
        for probs, grad_scores, g_rows, q_rows, k in got:
            outs.append(
                (
                    gather_heads(tn(grad_scores, k), scales),
                    nn(grad_scores, q_rows) * scale,
                    nn(probs, g_rows),
                    grad_scores,
                )
            )
        for t in range(2):
            store(i, t, outs[t])

    yield from pipelined(n, first, second, third)


def score_factor(z):
    return np.float32((z.d // z.heads) ** (-0.5) * np.log2(np.e))


def of_band(b, refs):
    return [ref.at[:, b : b + 1] for ref in refs]


def forward_kernel(z, *refs):
    wire_in, wire_out = refs[: z.lev], refs[z.lev + 16 : 2 * z.lev + 16]
    wire_s = refs[2 * z.lev + 25]
    load_wire(z, wire_in, wire_s)
    interleave([forward_band(z, b, *refs) for b in range(z.nb)], LAG_F)
    flush_wire(z, wire_s, wire_out)


def forward_band(z, b, *refs):
    it = iter(refs)
    take = lambda n: [next(it) for _ in range(n)]
    wire_in = take(z.lev)
    offsets, sizes, bias_ref, column_mask = take(4)
    gain1, shift1, gain2, shift2, gain3, shift3 = take(6)
    w_qkv1, wo1, w_qkv2, wo2, w_up, w_down_t = take(6)
    wire_out = take(z.lev)
    kept = of_band(b, take(9))
    norm1_ref, norm2_ref, norm3_ref, att_ref, co_ref, act_ref, slope_ref, probs_ref, probs2_ref = kept
    (wire_s,) = take(1)
    x_s, n_s, o_s, a_s, qkv_s, bias_s = (ref.at[b] for ref in take(6))
    ones = head_masks(z)
    s = pl.program_id(0)
    token = lax.broadcasted_iota(jnp.int32, (TOK, 1), 0)
    cell = (token * 43) >> 8
    row = token - cell * WLAT + (lax.axis_index("lev") * z.nb + b) * WLAT
    cell = cell + (lax.axis_index("lon") * z.cells + offsets[s])
    cell = jnp.where(cell >= z.cells * z.lon, cell - z.cells * z.lon, cell)
    valid = (row < sizes[s, 0]) & (cell < sizes[s, 1])
    bias_s[...] = bias_ref[b] + jnp.where(valid, 0.0, NEGATIVE)

    def keep(ref, gain, shift):
        def store(lv, values, normed, rstd):
            x_s[lv] = values
            n_s[lv] = normed * gain[...] + shift[...]
            room = jnp.broadcast_to(rstd, (TOK, 2 * LANES - z.d))
            ref[0, 0, lv] = jnp.concatenate([normed, room], axis=1)

        return store

    yield from norm_levels(
        z.lt, lambda lv: wire_level(z, wire_s, lv // z.l, lv % z.l, b), keep(norm1_ref, gain1, shift1)
    )
    put_rows(z, qkv_s, nn(bf16_rows(z, n_s), w_qkv1[...]))

    yield from attention(
        z.lt,
        lambda lv, j, t: qkv_s[lv, :, tile(j, t)],
        lambda t: bias_s[t],
        lambda lv, t: probs_ref.at[0, 0, lv, t],
        lambda lv, t, out: put(a_s, (lv, slice(None), tile(0, t)), out),
        ones,
        score_factor(z),
    )
    att = bf16_rows(z, a_s)
    att_ref[0, 0] = att
    put_rows(z, o_s, nn(att, wo1[...]))

    yield from norm_levels(z.lt, lambda lv: x_s[lv] + o_s[lv], keep(norm2_ref, gain2, shift2))
    put_rows(z, qkv_s, nn(bf16_rows(z, n_s), w_qkv2[...]))

    yield from attention(
        TOK // GROUP,
        lambda g, j, t: qkv_s[:, group(g), tile(j, t)].reshape(z.lt * GROUP, LANES),
        lambda t: column_mask[...],
        lambda g, t: probs2_ref.at[0, 0, g, t],
        lambda g, t, out: put(a_s, (slice(None), group(g), tile(0, t)), out.reshape(z.lt, GROUP, LANES)),
        ones,
        score_factor(z),
    )
    co = bf16_rows(z, a_s)
    co_ref[0, 0] = co
    put_rows(z, o_s, nn(co, wo2[...]))

    yield from norm_levels(z.lt, lambda lv: x_s[lv] + o_s[lv], keep(norm3_ref, gain3, shift3))

    def up(i):
        return nn(some_rows(z, n_s, i), w_up[...])

    def gelu(i, hidden):
        share = 0.5 + 0.5 * lax.erf(hidden * (0.5**0.5))
        density = jnp.exp(hidden * hidden * -0.5) * ((2.0 * np.pi) ** -0.5)
        return (hidden * share).astype(BF16), (share + hidden * density).astype(BF16)

    def down(i, got):
        act, slope = got
        out = nt(act, w_down_t[...])
        rows = slice(i * CHUNK * TOK, (i + 1) * CHUNK * TOK)
        act_ref[0, 0, rows], slope_ref[0, 0, rows] = act, slope
        o_s[i * CHUNK : (i + 1) * CHUNK] = out.reshape(CHUNK, TOK, z.d)

    yield from pipelined(z.lt // CHUNK, up, gelu, down)

    store_wire_levels(z, wire_s, b, lambda lv: x_s[lv] + o_s[lv])


def wire_specs(z):
    return [pl.BlockSpec((1, z.nblk, z.ro, LANES), lambda s: (s, 0, 0, 0))] * z.lev


def wire_shapes(z):
    return [jax.ShapeDtypeStruct((z.s, z.nblk, z.ro, LANES), BF16)] * z.lev


def unit_spec(shape):
    return pl.BlockSpec((1,) + shape, lambda s: (s,) + (0,) * len(shape))


def whole_spec(array):
    return pl.BlockSpec(array.shape, lambda s: (0,) * array.ndim)


def residual_shapes(z):
    return [
        ((z.lt, TOK, 2 * LANES), F32),
        ((z.lt, TOK, 2 * LANES), F32),
        ((z.lt, TOK, 2 * LANES), F32),
        ((z.n, 2 * LANES), BF16),
        ((z.n, 2 * LANES), BF16),
        ((z.n, z.ff), BF16),
        ((z.n, z.ff), BF16),
        ((z.lt, 2, TOK, z.heads // 2 * TOK), BF16),
        ((TOK // GROUP, 2, z.lt * GROUP, z.heads // 2 * z.lt * GROUP), BF16),
    ]


def forward(z, wire, offsets, sizes, bias, column_mask, norms, weights):
    res = residual_shapes(z)
    rows3 = (z.nb, z.lt, TOK, z.d)
    out = pl.pallas_call(
        functools.partial(forward_kernel, z),
        grid=(z.s,),
        in_specs=wire_specs(z)
        + [
            *in_smem(2),
            whole_spec(bias),
            whole_spec(column_mask),
        ]
        + [whole_spec(a) for a in norms]
        + [whole_spec(a) for a in weights],
        out_specs=wire_specs(z) + [unit_spec((z.nb,) + shape) for shape, _ in res],
        out_shape=wire_shapes(z) + [jax.ShapeDtypeStruct((z.s, z.nb) + shape, t) for shape, t in res],
        scratch_shapes=[pltpu.VMEM((z.lev, z.nblk, z.ro, LANES), F32)]
        + [pltpu.VMEM(rows3, F32)] * 3
        + [
            pltpu.VMEM((z.nb, z.lt, TOK, 2 * LANES), F32),
            pltpu.VMEM((z.nb, z.lt, TOK, 6 * LANES), F32),
            pltpu.VMEM((z.nb, 2, TOK, z.heads // 2 * TOK), F32),
        ],
        compiler_params=pltpu.CompilerParams(vmem_limit_bytes=60 * 2**20),
        cost_estimate=cost(30),
        name="forward",
    )(*wire, offsets, sizes, bias, column_mask, *norms, *weights)
    return out[: z.lev], out[z.lev :]


def grad_list(z):
    return [
        ("up", z.ff), ("down_t", z.ff),
        ("qkv1", 3 * z.d), ("qkv2", 3 * z.d),
        ("o1", z.d), ("o2", z.d),
    ]


def half_blocks(z):
    full, rest = [], []
    for name, columns in grad_list(z):
        for row in range(0, z.d, 96):
            for col in range(0, columns, LANES):
                width = min(LANES, columns - col)
                (full if width == LANES else rest).append((name, row, col, width))
    out = [[piece + (0,)] for piece in full]
    for i in range(0, len(rest), 2):
        out.append([rest[i] + (0,), rest[i + 1] + (rest[i][3],)])
    return out


def grad_buffer(z, name, columns):
    if name[:3] == "qkv":
        return (z.d, 6 * LANES)
    if name[0] == "o":
        return (2 * LANES, columns)
    return (z.d, columns)


def grad_block(z, name, ref, row, col, width):
    half = z.d // 2
    if name[0] == "o":
        start = row // half * LANES
        return ref[start : start + 96, col : col + width]
    if name[:3] != "qkv":
        return ref[row : row + 96, col : col + width]
    pieces = []
    while width:
        t, lane = col // half, col % half
        count = min(width, half - lane)
        pieces.append(ref[row : row + 96, t * LANES + lane : t * LANES + lane + count])
        col, width = col + count, width - count
    return pieces[0] if len(pieces) == 1 else jnp.concatenate(pieces, axis=1)


def bias_rows(z):
    pick = np.zeros((WLON * 8, TOK), np.float32)
    for a in range(WLON):
        for i in range(WLAT):
            pick[a * 8 + i, a * WLAT + i] = 1.0
    return pick


def backward_band(z, b, kept, norms, weights, wire_s, own, db_s, vec_s, grads):
    norm1_ref, norm2_ref, norm3_ref, att_ref, co_ref, act_ref, slope_ref, probs_ref, probs2_ref = kept
    gain1, shift1, gain2, shift2, gain3, shift3 = norms
    w_qkv1, wo1, w_qkv2, wo2, w_up, w_down_t = weights
    g_s, o_s, a_s, qkv_s, grad_s, gh_s = own
    scale = np.float32((z.d // z.heads) ** (-0.5))
    ones, scales = head_masks(z), head_masks(z, scale)

    for k in range(z.lev):
        got = [wire_level(z, wire_s, k, l, b) for l in range(z.l)]
        for l in range(z.l):
            g_s[k * z.l + l] = got[l]

    def normed_tokens(ref, gain, shift):
        normed = ref[0, 0][:, :, : z.d] * gain[...] + shift[...]
        return normed.reshape(z.n, z.d).astype(BF16)

    def back_down(i):
        rows = slice(i * CHUNK * TOK, (i + 1) * CHUNK * TOK)
        return nn(some_rows(z, g_s, i), w_down_t[...]), slope_ref[0, 0, rows, :].astype(F32)

    def back_gelu(i, got):
        return (got[0] * got[1]).astype(BF16)

    def back_up(i, grad):
        out = nt(grad, w_up[...])
        gh_s[i * CHUNK * TOK : (i + 1) * CHUNK * TOK] = grad
        o_s[i * CHUNK : (i + 1) * CHUNK] = out.reshape(CHUNK, TOK, z.d)

    yield from pipelined(z.lt // CHUNK, back_down, back_gelu, back_up)
    grads["down_t"][...] += tn(bf16_rows(z, g_s), act_ref[0, 0])
    grads["up"][...] += tn(normed_tokens(norm3_ref, gain3, shift3), gh_s[...])

    def norm_step(ref, gain, at, target):
        sums = [vec_s[b, at], vec_s[b, at + 1]]

        def first(lv):
            grad, normed, rstd = o_s[lv], ref[0, 0, lv, :, : z.d], ref[0, 0, lv, :, z.d : z.d + 1]
            sums[0] += fold_rows(grad * normed)
            sums[1] += fold_rows(grad)
            return target[lv], normed, rstd, grad * gain[...]

        def second(lv, got):
            old, normed, rstd, gained = got
            one = jnp.mean(gained, axis=-1, keepdims=True)
            two = jnp.mean(gained * normed, axis=-1, keepdims=True)
            return old, normed, rstd, gained, one, two

        def third(lv, got):
            old, normed, rstd, gained, one, two = got
            target[lv] = old + rstd * (gained - one - normed * two)

        yield from pipelined(z.lt, first, second, third)
        vec_s[b, at], vec_s[b, at + 1] = sums

    yield from norm_step(norm3_ref, gain3, 4, g_s)

    branch = bf16_rows(z, g_s)
    grads["o2"][...] += tn(co_ref[0, 0], branch)
    put_rows(z, a_s, nt(branch, wo2[...]))
    tokens = normed_tokens(norm2_ref, gain2, shift2)
    put_rows(z, qkv_s, nn(tokens, w_qkv2[...]))

    def keep_column(g, t, got):
        for j in range(3):
            grad_s[:, group(g), tile(j, t)] = got[j].reshape(z.lt, GROUP, LANES)

    yield from attention_back(
        TOK // GROUP,
        lambda g, j, t: qkv_s[:, group(g), tile(j, t)].reshape(z.lt * GROUP, LANES),
        lambda g, t: a_s[:, group(g), tile(0, t)].reshape(z.lt * GROUP, LANES),
        lambda g, t: probs2_ref.at[0, 0, g, t],
        keep_column,
        ones,
        scales,
        scale,
    )

    def project_back(tokens, name, w):
        grad = bf16_rows(z, grad_s)
        grads[name][...] += tn(tokens, grad)
        put_rows(z, o_s, nt(grad, w[...]))

    project_back(tokens, "qkv2", w_qkv2)
    yield from norm_step(norm2_ref, gain2, 2, g_s)

    branch = bf16_rows(z, g_s)
    grads["o1"][...] += tn(att_ref[0, 0], branch)
    put_rows(z, a_s, nt(branch, wo1[...]))
    tokens = normed_tokens(norm1_ref, gain1, shift1)
    put_rows(z, qkv_s, nn(tokens, w_qkv1[...]))

    def keep_window(lv, t, got):
        for j in range(3):
            grad_s[lv, :, tile(j, t)] = got[j]
        db_s[b, t] += got[3].astype(F32)

    yield from attention_back(
        z.lt,
        lambda lv, j, t: qkv_s[lv, :, tile(j, t)],
        lambda lv, t: a_s[lv, :, tile(0, t)],
        lambda lv, t: probs_ref.at[0, 0, lv, t],
        keep_window,
        ones,
        scales,
        scale,
    )
    project_back(tokens, "qkv1", w_qkv1)
    yield from norm_step(norm1_ref, gain1, 0, g_s)

    store_wire_levels(z, wire_s, b, lambda lv: g_s[lv])


def backward_kernel(z, *refs):
    it = iter(refs)
    take = lambda n: [next(it) for _ in range(n)]
    wire_in = take(z.lev)
    kept = take(9)
    (pick_ref,) = take(1)
    gain1, shift1, gain2, shift2, gain3, shift3 = take(6)
    w_qkv1, wo1, w_qkv2, wo2, w_up, w_down_t = take(6)
    wire_out = take(z.lev)
    late_ref, mine_ref, other_ref = take(3)
    wire_s, late_s, g_s, o_s, a_s, qkv_s, grad_s, gh_s, db_s, vec_s, sums_s = take(11)
    grads = {name: ref for (name, _), ref in zip(grad_list(z), take(len(grad_list(z))))}
    s = pl.program_id(0)

    @pl.when(s == 0)
    def _():
        for ref in list(grads.values()) + [db_s, vec_s]:
            ref[...] = jnp.zeros_like(ref)

    load_wire(z, wire_in, wire_s)
    bands = []
    for b in range(z.nb):
        own = [ref.at[b] for ref in (g_s, o_s, a_s, qkv_s, grad_s, gh_s)]
        norms = (gain1, shift1, gain2, shift2, gain3, shift3)
        weights = (w_qkv1, wo1, w_qkv2, wo2, w_up, w_down_t)
        bands.append(
            backward_band(z, b, of_band(b, kept), norms, weights, wire_s, own, db_s, vec_s, grads)
        )
    interleave(bands, LAG_B)
    flush_wire(z, wire_s, wire_out)
    for band in range(z.nb):
        rows = wire_s[:, :, band * TOK + HALO0 : (band + 1) * TOK, :]
        late_s[:, :, band * HALO : (band + 1) * HALO, :] = rows
    late_ref[:, 0] = late_s[...].astype(BF16)

    @pl.when(s == z.s - 1)
    def _():
        p, core = lax.axis_index("lev"), lax.axis_index("lon") % 2

        def place(i):
            return ((i // z.lev) ^ core) * z.lev + ((i % z.lev) ^ p)

        for at, pieces in enumerate(half_blocks(z)):
            values = [grad_block(z, n, grads[n], r, c, width) for n, r, c, width, _ in pieces]
            block = values[0] if len(values) == 1 else jnp.concatenate(values, axis=1)
            start = (at % z.hb) * 96
            sums_s[place(at // z.hb), start : start + 96, :] = block.astype(BF16)
        extra = z.hb * 96
        sums_s[:, extra:, :] = jnp.zeros_like(sums_s[:, extra:, :])
        vectors = [jnp.sum(jnp.sum(vec_s[:, i], axis=0), axis=0, keepdims=True) for i in range(6)]
        vectors = jnp.concatenate(vectors + [jnp.zeros((UNIT - 6, z.d), F32)], axis=0)
        vectors = jnp.concatenate([vectors, jnp.zeros((UNIT, 2 * LANES - z.d), F32)], axis=1)

        def put_unit(u, value):
            start = extra + (u % z.upp) * UNIT
            if not isinstance(u, int):
                start = pl.multiple_of(start, UNIT)
            sums_s[place(u // z.upp), pl.ds(start, UNIT), :] = value.astype(BF16)

        for j in range(2):
            put_unit(z.bands * 4 + j, vectors[:, j * LANES : (j + 1) * LANES])
        lane = lax.broadcasted_iota(jnp.int32, (1, z.heads * TOK), 1)
        odd = jnp.zeros(lane.shape, jnp.bool_)
        for h in range(1, z.heads, 2):
            odd = odd | ((lane >= h * TOK) & (lane < (h + 1) * TOK))
        width = -(-(z.heads * TOK) // LANES) * LANES
        for band in range(z.nb):
            rows = [nn(pick_ref[...], db_s[band, t], precision=lax.Precision.HIGHEST) for t in range(2)]
            rows = jnp.concatenate(rows, axis=1)
            halves = []
            for parity in range(2):
                kept = jnp.where(odd if parity else ~odd, rows, 0.0)
                kept = jnp.concatenate(
                    [kept, jnp.zeros((rows.shape[0], width - z.heads * TOK), F32)], axis=1
                )
                total = None
                for a in range(WLON):
                    part = kept[a * 8 : (a + 1) * 8]
                    shift = (WLON - 1 - a) * WLAT
                    if shift:
                        part = pltpu.roll(part, shift, 1)
                    total = part if total is None else total + part
                halves.append(total)
            both = jnp.concatenate(halves, axis=0)
            for j in range(4):
                put_unit((p * z.nb + band) * 4 + j, both[:, j * LANES : (j + 1) * LANES])
        mine_ref[...] = sums_s[: z.lev]
        other_ref[...] = sums_s[z.lev :]


def backward(z, wire, residuals, norms, weights):
    res = residual_shapes(z)
    rows3 = (z.nb, z.lt, TOK, z.d)
    pick = jnp.asarray(bias_rows(z))
    half = (z.lev, z.pr, LANES)
    out = pl.pallas_call(
        functools.partial(backward_kernel, z),
        **dict(
            grid=(z.s,),
            in_specs=[
                spec
                for spec in wire_specs(z)
                + [unit_spec((z.nb,) + shape) for shape, _ in res]
                + [whole_spec(pick)]
                + [whole_spec(a) for a in norms]
                + [whole_spec(a) for a in weights]
            ],
            out_specs=[spec for spec in wire_specs(z)]
            + [pl.BlockSpec((z.lev, 1, z.nblk, z.rh, LANES), lambda s: (0, s, 0, 0, 0))]
            + [pl.BlockSpec(half, lambda s: (0, 0, 0))] * 2,
            scratch_shapes=[
                pltpu.VMEM((z.lev, z.nblk, z.ro, LANES), F32),
                pltpu.VMEM((z.lev, z.nblk, z.rh, LANES), F32),
            ]
            + [pltpu.VMEM(rows3, F32)] * 2
            + [
                pltpu.VMEM((z.nb, z.lt, TOK, 2 * LANES), F32),
                pltpu.VMEM((z.nb, z.lt, TOK, 6 * LANES), F32),
                pltpu.VMEM((z.nb, z.lt, TOK, 6 * LANES), F32),
                pltpu.VMEM((z.nb, z.n, z.ff), BF16),
                pltpu.VMEM((z.nb, 2, TOK, z.heads // 2 * TOK), F32),
                pltpu.VMEM((z.nb, 6, 8, z.d), F32),
                pltpu.VMEM((z.np, z.pr, LANES), BF16),
            ]
            + [pltpu.VMEM(grad_buffer(z, *item), F32) for item in grad_list(z)],
        ),
        out_shape=wire_shapes(z)
        + [jax.ShapeDtypeStruct((z.lev, z.s, z.nblk, z.rh, LANES), BF16)]
        + [jax.ShapeDtypeStruct(half, BF16)] * 2,
        compiler_params=pltpu.CompilerParams(vmem_limit_bytes=62 * 2**20),
        cost_estimate=cost(40),
        name="backward",
    )(*wire, *residuals, pick, *norms, *weights)
    return out[: z.lev], out[z.lev], out[z.lev + 1], out[z.lev + 2]


def tree(parts):
    while len(parts) > 1:
        parts = [parts[i] + parts[i + 1] for i in range(0, len(parts), 2)]
    return parts[0]


def lev_swap(z, array, k):
    return lax.ppermute(array, "lev", [(i, i ^ k) for i in range(z.lev)])


def lon_swap(z, array, k):
    return lax.ppermute(array, "lon", [(i, i ^ k) for i in range(z.lon)])


def merge_kernel(z, offsets, *refs):
    wire, late_ref, outs = refs[: z.lev], refs[z.lev], refs[z.lev + 1 :]
    row = lax.broadcasted_iota(jnp.int32, (HALO, LANES), 0) + HALO0
    for s in range(z.s):
        moved = row >= (z.cells - offsets[s]) * WLAT
        for k in range(z.lev):
            for j in range(z.nblk):
                rows, late = wire[k][s, j].astype(F32), late_ref[k, s, j].astype(F32)
                parts = []
                for b in range(z.nb):
                    own = rows[b * TOK : (b + 1) * TOK]
                    got = late[b * HALO : (b + 1) * HALO]
                    parts += [own[:HALO0], jnp.where(moved, got, own[HALO0:])]
                if z.ro > z.nb * TOK:
                    parts.append(rows[z.nb * TOK :])
                outs[k][s, j] = jnp.concatenate(parts, axis=0).astype(BF16)


def merge_cells(z, wire, late, offsets):
    return pl.pallas_call(
        functools.partial(merge_kernel, z),
        in_specs=in_smem(1) + in_vmem(z.lev + 1),
        out_specs=in_vmem(z.lev),
        out_shape=[jax.ShapeDtypeStruct((z.s, z.nblk, z.ro, LANES), BF16)] * z.lev,
        compiler_params=pltpu.CompilerParams(vmem_limit_bytes=40 * 2**20),
        cost_estimate=cost(3),
        name="merge",
    )(offsets, *wire, late)


def tie(values, *others):
    return lax.optimization_barrier((values,) + others)[0]


def sum_cores(z, mine, other):
    got = lon_swap(z, other, 1)
    return [(mine[k].astype(F32) + got[k].astype(F32)).astype(BF16) for k in range(z.lev)]


def sum_levels(z, half):
    parts = [half[0]] + [lev_swap(z, half[k], k) for k in range(1, z.lev)]
    return tree([v.astype(F32) for v in parts]).astype(BF16)


def sum_slabs(z, quarter):
    parts = [quarter] + [lon_swap(z, quarter, 2 * k) for k in range(1, z.lon // 2)]
    return tree([v.astype(F32) for v in parts]).astype(BF16)


def share_levels(z, done):
    return [done] + [lev_swap(z, done, k) for k in range(1, z.lev)]


def table_lanes(z, h):
    lanes = np.full((WLAT, 32), -1, np.int32)
    for i in range(WLAT):
        lanes[i, : 2 * WLON - 1] = h * TOK + np.arange(2 * WLON - 1) * WLAT + i
    return lanes.reshape(1, WLAT * 32)


def finish_kernel(z, lanes, order, own, other, *outs):
    p, core = lax.axis_index("lev"), lax.axis_index("lon") % 2
    named = {name: ref for (name, _), ref in zip(grad_list(z), outs)}
    vec_refs, bias_ref = outs[len(named) : len(named) + 6], outs[len(named) + 6]

    def read(piece, start, size):
        half, j = piece // z.lev, piece % z.lev
        rows = slice(start, start + size)
        return jnp.where(core == half, own[p ^ j, rows, :], other[p ^ j, rows, :])

    for at, pieces in enumerate(half_blocks(z)):
        block = read(at // z.hb, (at % z.hb) * 96, 96).astype(F32)
        for n, r, c, width, lane in pieces:
            named[n][r : r + 96, c : c + width] = block[:, lane : lane + width]
    extra = z.hb * 96
    units = [read(u // z.upp, extra + (u % z.upp) * UNIT, UNIT) for u in range(z.units)]
    vectors = jnp.concatenate(units[z.bands * 4 :], axis=1).astype(F32)
    for i in range(6):
        vec_refs[i][...] = vectors[i : i + 1, : z.d]
    table = [jnp.concatenate(units[4 * k : 4 * k + 4], axis=1) for k in range(z.bands)]
    table = nn(order[...], jnp.concatenate(table, axis=0)).astype(BF16)
    half = table.shape[0] // 2
    for h in range(z.heads):
        at = lax.broadcasted_iota(jnp.int32, (4 * LANES, WLAT * 32), 0)
        pick = jnp.where(at == lanes[h : h + 1, :], 1.0, 0.0).astype(BF16)
        rows = table[(h % 2) * half : (h % 2) * half + half]
        got = nn(rows, pick)
        for i in range(WLAT):
            values = got[: WLAT * z.bands, i * 32 : i * 32 + 2 * WLON - 1]
            bias_ref[h, i] = values.reshape(WLAT, z.bands, 2 * WLON - 1)


def finish(z, own, other):
    shapes = [jax.ShapeDtypeStruct((z.d, columns), F32) for _, columns in grad_list(z)]
    shapes += [jax.ShapeDtypeStruct((1, z.d), F32)] * 6
    shapes += [jax.ShapeDtypeStruct((z.heads, WLAT, WLAT, z.bands, 2 * WLON - 1), F32)]
    lanes = jnp.asarray(np.concatenate([table_lanes(z, h) for h in range(z.heads)]))
    order = np.zeros((2 * 8 * z.bands, z.bands * UNIT), np.float32)
    for parity in range(2):
        for i in range(8):
            for k in range(z.bands):
                order[parity * 8 * z.bands + i * z.bands + k, k * UNIT + parity * 8 + i] = 1.0
    order = jnp.asarray(order, BF16)
    out = pl.pallas_call(
        functools.partial(finish_kernel, z),
        in_specs=in_vmem(4),
        out_specs=in_vmem(len(shapes)),
        out_shape=shapes,
        compiler_params=pltpu.CompilerParams(vmem_limit_bytes=40 * 2**20),
        cost_estimate=cost(4),
        name="finish",
    )(lanes, order, own, other)
    named = {name: value for (name, _), value in zip(grad_list(z), out)}
    vectors = [v.reshape(z.d) for v in out[len(named) : len(named) + 6]]
    return named, vectors, out[-1].transpose(3, 0, 1, 2, 4)


def bias_kernel(z, table_ref, pick_ref, qkv1, out1, qkv2, out2, out_ref, *rest):
    even_s, odd_s = rest[4:]
    side = z.d // 2
    for source, target in ((qkv1, rest[0]), (qkv2, rest[2])):
        room = jnp.zeros((z.d, LANES - side), BF16)
        for t in range(6):
            part = source[:, t * side : (t + 1) * side]
            target[:, t * LANES : (t + 1) * LANES] = jnp.concatenate([part, room], axis=1)
    for source, target in ((out1, rest[1]), (out2, rest[3])):
        for t in range(2):
            target[t * LANES : t * LANES + side] = source[t * side : (t + 1) * side]
            target[t * LANES + side : (t + 1) * LANES] = jnp.zeros((LANES - side, z.d), BF16)
    width = 4 * LANES
    lane = lax.broadcasted_iota(jnp.int32, (2 * WLON - 1, width), 1)
    step = lax.broadcasted_iota(jnp.int32, (2 * WLON - 1, width), 0) * WLAT
    for parity, ref in ((0, even_s), (1, odd_s)):
        total = None
        for h in range(parity, z.heads, 2):
            for i in range(WLAT):
                place = jnp.where(lane == step + (h * TOK + i), 1.0, 0.0).astype(BF16)
                values = table_ref[h, i]
                high = values.astype(BF16)
                low = (values - high.astype(F32)).astype(BF16)
                part = nn(jnp.concatenate([high, low], axis=0), place)
                total = part if total is None else total + part
        rows = z.nb * 8
        ref[...] = total[:rows] + total[rows:]
    head = lax.broadcasted_iota(jnp.int32, (1, width), 1)
    odd = jnp.zeros(head.shape, jnp.bool_)
    for h in range(1, z.heads, 2):
        odd = odd | ((head >= h * TOK) & (head < (h + 1) * TOK))
    side = z.heads // 2 * TOK
    for b in range(z.nb):
        even, uneven = even_s[b * 8 : (b + 1) * 8], odd_s[b * 8 : (b + 1) * 8]
        rows = []
        for a in range(WLON):
            shift = (width - (WLON - 1 - a) * WLAT) % width
            turned = [pltpu.roll(v, shift, 1) if shift else v for v in (even, uneven)]
            rows.append(jnp.where(odd, turned[1], turned[0]))
        rows = jnp.concatenate(rows, axis=0)
        full = lax.dot_general(
            pick_ref[...], rows, (((0,), (0,)), ((), ())),
            precision=lax.Precision.HIGHEST, preferred_element_type=F32,
        ) * np.float32(np.log2(np.e))
        out_ref[b, 0] = full[:, :side]
        out_ref[b, 1] = full[:, side : 2 * side]


def bias_of(z, bias_table, p, weights):
    table = lax.dynamic_slice_in_dim(bias_table, p * z.nb, z.nb, axis=0)
    table = jnp.pad(table.transpose(1, 2, 0, 3, 4), ((0, 0),) * 3 + ((0, 2), (0, 0)))
    table = table.reshape(z.heads, WLAT, z.nb * 8, 2 * WLON - 1)
    wide = jax.ShapeDtypeStruct((z.d, 6 * LANES), BF16)
    tall = jax.ShapeDtypeStruct((2 * LANES, z.d), BF16)
    bias = jax.ShapeDtypeStruct((z.nb, 2, TOK, z.heads // 2 * TOK), F32)
    out = pl.pallas_call(
        functools.partial(bias_kernel, z),
        out_shape=[bias, wide, tall, wide, tall],
        scratch_shapes=[pltpu.VMEM((z.nb * 8, 4 * LANES), F32)] * 2,
        compiler_params=pltpu.CompilerParams(vmem_limit_bytes=40 * 2**20),
        cost_estimate=cost(4),
        name="bias",
    )(table, jnp.asarray(bias_rows(z)), *weights)
    return out[0], list(out[1:])


def lev_exchange(z, wire):
    return [wire[0]] + [lev_swap(z, wire[k], k) for k in range(1, z.lev)]


def lon_shift(z, array, distance):
    return lax.ppermute(array, "lon", [(w, (w + distance) % z.lon) for w in range(z.lon)])


def last_cells(z, wire):
    rows = [a[:, :, : z.nb * TOK].reshape(z.s, z.nblk, z.nb, TOK, LANES)[:, :, :, HALO0:] for a in wire]
    return jnp.stack(rows).reshape(z.lev, z.s, z.nblk, z.rh, LANES)


def on_device(
    inputs, cotangent, grid_sizes, offsets, gain_one, shift_one, qkv_window, out_window, bias_table,
    gain_two, shift_two, qkv_column, out_column, gain_three, shift_three, w_up, w_down,
):
    d = inputs.shape[-1]
    z = Sizes(lax.axis_size("lev"), lax.axis_size("lon"), inputs.shape, bias_table.shape[1], w_up.shape[1])
    p = lax.axis_index("lev")
    swap = lambda a: a.transpose(0, 1, 3, 2, 4)

    half = WLON // 2
    x, c = swap(inputs), swap(cotangent)
    halo_x = lon_shift(z, x[:, :, :half], -1)
    raw = (qkv_window, out_window, qkv_column, out_column)
    bias, weights = bias_of(z, bias_table, p, raw)
    weights = weights + [w_up, w_down.T]
    first_c = tie(c, bias)[:, :, :half]
    halo_x, bias, first_c = lax.optimization_barrier((halo_x, bias, first_c))
    halo_c = lon_shift(z, first_c, -1)
    wire_x = pack(z, x, halo_x, offsets)
    halo_c = tie(halo_c, *wire_x)
    wire_x = lev_exchange(z, wire_x)
    wire_c = lev_exchange(z, pack(z, c, halo_c, offsets))
    of_key = np.arange(z.lt * GROUP) % GROUP
    of_query = np.tile(of_key, z.heads // 2)
    column_mask = jnp.asarray(
        np.where(of_key[:, None] == of_query[None, :], 0.0, NEGATIVE).astype(np.float32)
    )

    norms = [v[None] for v in (gain_one, shift_one, gain_two, shift_two, gain_three, shift_three)]
    wire_r, residuals = forward(z, wire_x, offsets, grid_sizes, bias, column_mask, norms, weights)
    wire_r = lev_exchange(z, wire_r)
    grads = backward(z, wire_c, residuals, norms, weights)
    (wire_g, late, mine, other), wire_r = lax.optimization_barrier((grads, wire_r))
    halo_r = lon_shift(z, last_cells(z, wire_r), 1)
    late = lon_shift(z, late, 1)
    sums = sum_cores(z, mine, other)
    sums = sum_levels(z, sums)
    wire_g = lev_exchange(z, merge_cells(z, wire_g, late, offsets))
    result = unpack(z, wire_r, halo_r, offsets)
    sums = sum_slabs(z, sums)
    sums = share_levels(z, tie(sums, result))
    input_grad = unpack(z, wire_g, None, offsets)
    own = jnp.stack(tie(sums, input_grad))
    other = lon_swap(z, own, 1)
    named, vec, table = finish(z, own, other)
    return (
        swap(result), swap(input_grad),
        vec[0], vec[1], named["qkv1"], named["o1"], table,
        vec[2], vec[3], named["qkv2"], named["o2"],
        vec[4], vec[5], named["up"], named["down_t"].T,
    )


def solution(mesh):
    tokens = P(None, "lev", None, "lon", None)
    return jax.shard_map(
        on_device,
        mesh=mesh,
        in_specs=(tokens, tokens) + (P(),) * 15,
        out_specs=(tokens, tokens) + (P(),) * 13,
        check_vma=False,
    )
```
